128 devices in a mesh: queue: 8 (over y_lo, x), spatial: 16 (over y_hi, z, core).
Axes of the slice: x: 4, y: 4 (y_hi: 2, y_lo: 2; y = y_hi * 2 + y_lo), z: 4, core: 2. Of those that a mesh axis runs over, the one named last changes fastest.
Arguments:
- hidden: bfloat16 [16, 1024, 5120], P('queue', 'spatial'), may hold values from -6 to 6
- queries: bfloat16 [16, 1024, 4096], P('queue', 'spatial'), may hold values from -6 to 6, as said below
- keys: bfloat16 [16, 1024, 4096], P('queue', 'spatial'), may hold values from -6 to 6, as said below
- values: bfloat16 [16, 1024, 4096], P('queue', 'spatial'), may hold values from -6 to 6
- out_weight: bfloat16 [4096, 5120], P('spatial', 'queue'), may hold values from -5 to 5
- gate_table: float32 [50, 5120], P(None, 'queue'), may hold values from 0.5 to 2
- levels: int32 [16], replicated, may hold values from 0 to 49
- entering: bfloat16 [1024, 5120], P('spatial'), may hold values from -6 to 6
Outputs:
- next_queue: bfloat16 [16, 1024, 5120], P('queue', 'spatial')
The draws below stay inside these ranges and needn't reach their ends.
Inputs may be any that keep to these rules, and one draw needn't show every extreme that they name: `queries`: queries are of order one, with absolute values up to 6. `keys`: keys are of order one, with absolute values up to 6.
All inputs are finite; a program needn't handle non-finite values.
Results may differ from the reference program's by a relative error of at most 0.0057.
Values may be sent and summed in bfloat16 or wider, within the bound.
No kernel may reach another device: no remote copies, remote signals or barrier semaphores. Data moves between devices by JAX's collectives and lax.ppermute only.
A program may use at most 64 MiB of HBM per device.

```python
import jax
import jax.numpy as jnp
from jax import lax

D = 5120
HEADS = 32
HD = 128
LEVELS = 50
WMAX = 2
FRAMES = 16
TOK_FRAME = 1024


def draw_queries(key, part):
    key = jax.random.fold_in(key, 11)
    full_shape = (FRAMES, TOK_FRAME, HEADS * HD)
    values_drawn = jnp.clip(jax.random.normal(key, full_shape, jnp.float32), -6.0, 6.0)
    return values_drawn.astype(jnp.bfloat16)


def draw_keys(key, part):
    key = jax.random.fold_in(key, 23)
    full_shape = (FRAMES, TOK_FRAME, HEADS * HD)
    values_drawn = jnp.clip(jax.random.normal(key, full_shape, jnp.float32), -6.0, 6.0)
    return values_drawn.astype(jnp.bfloat16)


def with_ends(entries, key, smallest, largest):
    index_at = [jax.random.randint(jax.random.fold_in(key, axis), (), 0, length) for axis, length in enumerate(entries.shape)]
    longest = entries.shape.index(max(entries.shape))
    next_to = index_at[:longest] + [(index_at[longest] + 1) % entries.shape[longest]] + index_at[longest + 1:]
    return entries.at[tuple(index_at)].set(smallest).at[tuple(next_to)].set(largest)


def level_of(stream_key, extent, cuts, least, largest):
    level, own = 1.0, jax.random.fold_in(stream_key, 6)
    for dim, blocks in cuts:
        steps = jnp.exp(jax.random.uniform(jax.random.fold_in(own, dim), (blocks,), jnp.float32, least / len(cuts), largest / len(cuts)))
        level = level * jnp.repeat(steps, extent[dim] // blocks).reshape([-1 if axis == dim else 1 for axis in range(len(extent))])
    return level


def bell_draw(rng, shape, scale, bound, pieces=(), kind=jnp.bfloat16):
    values = scale * jax.random.normal(rng, shape, jnp.float32)
    if pieces:
        values = values * level_of(rng, shape, pieces, -0.22, 0.18)
    return jnp.clip(values, -bound, bound).astype(kind)


def setup_inputs(seed: int = 0) -> dict:
    streams_of = jax.random.split(jax.random.key(seed), 9)
    return {
        "hidden": bell_draw(streams_of[0], (FRAMES, TOK_FRAME, D), 1.0, 6.0, ((0, 8), (1, 16))),
        "queries": draw_queries(jax.random.fold_in(streams_of[8], 71), 0),
        "keys": draw_keys(jax.random.fold_in(streams_of[8], 71), 0),
        "values": bell_draw(streams_of[3], (FRAMES, TOK_FRAME, HEADS * HD), 1.0, 6.0, ((0, 8), (1, 16))),
        "out_weight": bell_draw(streams_of[4], (HEADS * HD, D), (20.0 / (HEADS * HD) ** 0.5), 5.0, ((0, 16), (1, 8))),
        "gate_table": jnp.clip(0.5 + 1.5 * jax.random.uniform(streams_of[5], (LEVELS, D), jnp.float32) ** level_of(streams_of[5], (LEVELS, D), ((1, 8),), -0.2, 0.2), 0.5, 2.0),
        "levels": with_ends(jax.random.randint(streams_of[6], (FRAMES,), 0, LEVELS), jax.random.fold_in(streams_of[6], 1), 0, LEVELS - 1).astype(jnp.int32),
        "entering": bell_draw(streams_of[7], (TOK_FRAME, D), 1.0, 6.0, ((0, 16),)),
    }


NEG_FILL = -1.0e30


def reference(hidden, queries, keys, values, out_weight, gate_table, levels, entering):
    scaling = 1.0 / (HD ** 0.5)
    key_span = 2 * WMAX + 1
    padding = jnp.zeros((WMAX, TOK_FRAME, HEADS * HD), keys.dtype)
    keys_padded = jnp.concatenate((padding, keys, padding), 0)
    values_padded = jnp.concatenate((padding, values, padding), 0)
    offsets = jnp.arange(key_span, dtype=jnp.int32) - WMAX

    def one_frame(frame_at):
        nearby = frame_at + offsets
        visible = (nearby >= 0) & (nearby < FRAMES)
        allowed = jnp.repeat(visible, TOK_FRAME)
        frame_query = lax.dynamic_index_in_dim(queries, frame_at, 0, keepdims=False).reshape(TOK_FRAME, HEADS, HD)
        frame_keys = lax.dynamic_slice_in_dim(keys_padded, frame_at, key_span, 0).reshape(key_span * TOK_FRAME, HEADS, HD)
        frame_values = lax.dynamic_slice_in_dim(values_padded, frame_at, key_span, 0).reshape(key_span * TOK_FRAME, HEADS, HD)

        def one_head(operands):
            query_head, key_head, value_head = operands
            scores = jnp.dot(query_head, key_head.T, preferred_element_type=jnp.float32) * scaling
            scores = jnp.where(allowed[None, :], scores, NEG_FILL)
            row_max = jnp.max(scores, axis=1, keepdims=True)
            lifted = jnp.exp(scores - row_max)
            weights = (lifted / jnp.sum(lifted, axis=1, keepdims=True)).astype(jnp.bfloat16)
            return jnp.dot(weights, value_head, preferred_element_type=jnp.float32).astype(jnp.bfloat16)

        outputs = lax.map(one_head, (jnp.moveaxis(frame_query, 1, 0), jnp.moveaxis(frame_keys, 1, 0), jnp.moveaxis(frame_values, 1, 0)))
        return jnp.moveaxis(outputs, 0, 1).reshape(TOK_FRAME, HEADS * HD)

    attended = lax.map(one_frame, jnp.arange(FRAMES, dtype=jnp.int32))
    projected = jnp.dot(attended.reshape(FRAMES * TOK_FRAME, HEADS * HD), out_weight, preferred_element_type=jnp.float32).reshape(FRAMES, TOK_FRAME, D)
    selector = (levels[:, None] == jnp.arange(LEVELS, dtype=jnp.int32)[None, :]).astype(jnp.float32)
    gates = jnp.dot(selector, gate_table, precision=lax.Precision.HIGHEST, preferred_element_type=jnp.float32)
    branch = (gates[:, None, :] * projected).astype(jnp.bfloat16)
    updated = (hidden.astype(jnp.float32) + branch.astype(jnp.float32)).astype(jnp.bfloat16)
    return jnp.concatenate((entering[None], updated[:FRAMES - 1]), 0)
```

```python
import functools

import jax
import jax.numpy as jnp
from jax import lax
from jax.experimental import pallas as pl
from jax.experimental.pallas import tpu as pltpu
from jax.sharding import PartitionSpec as P

HEADS = 32
HD = 128
WMAX = 2
NEG_FILL = -1e30
SCALE_LOG2 = (HD ** -0.5) * 1.4426950408889634
BLOCK_Q = 512
VMEM = 48 * 1024 * 1024
QUEUE = 8
RING = 4
SPATIAL = 16
CORES = 2
PACK = 4
SPAN = 2 * WMAX + 1
ANY = pl.BlockSpec(memory_space=pl.ANY)
TOKEN = (8, 128)


def corner(array):
    rows = 8 if array.dtype == jnp.float32 else 16
    block = (1,) * (array.ndim - 2) + (rows, 128)
    return pl.BlockSpec(block, lambda *at: (0,) * array.ndim)


def pack(queries, keys, values):
    frames, tok, width = keys.shape
    group = width // SPATIAL
    piece = width // PACK
    count = SPATIAL // PACK

    def kernel(q_ref, k_ref, v_ref, kv0_ref, kv1_ref, out_ref):
        for i in range(count):
            for head, kv_ref in enumerate((kv0_ref, kv1_ref)):
                cols = slice(i * group + head * HD, i * group + (head + 1) * HD)
                kv_ref[i, 0] = k_ref[:, :, cols]
                kv_ref[i, 1] = v_ref[:, :, cols]
            out_ref[i] = q_ref[:, :, i * group : (i + 1) * group]

    spec = pl.BlockSpec((frames, tok, piece), lambda s: (0, 0, s))
    kv_spec = pl.BlockSpec((count, 2, frames, tok, HD), lambda s: (s, 0, 0, 0, 0))
    kv_shape = jax.ShapeDtypeStruct((SPATIAL, 2, frames, tok, HD), keys.dtype)
    return pl.pallas_call(
        kernel,
        grid=(PACK,),
        in_specs=[spec] * 3,
        out_specs=[kv_spec, kv_spec, pl.BlockSpec((count, frames, tok, group), lambda s: (s, 0, 0, 0))],
        out_shape=[
            kv_shape,
            kv_shape,
            jax.ShapeDtypeStruct((SPATIAL, frames, tok, group), queries.dtype),
        ],
        name="pack",
    )(queries, keys, values)


def last_frame(hidden, *earlier):
    frames, tok, width = hidden.shape

    def kernel(hidden_ref, *rest):
        rest[-1][...] = hidden_ref[...]

    return pl.pallas_call(
        kernel,
        grid=(1,),
        in_specs=[pl.BlockSpec((1, tok, width), lambda i: (frames - 1, 0, 0))]
        + [corner(e) for e in earlier],
        out_specs=pl.BlockSpec((1, tok, width), lambda i: (0, 0, 0)),
        out_shape=jax.ShapeDtypeStruct((1, tok, width), hidden.dtype),
        name="last_frame",
    )(hidden, *earlier)


def hold(array, *earlier):
    def kernel(*refs):
        pass

    return pl.pallas_call(
        kernel,
        grid=(1,),
        in_specs=[ANY] + [corner(e) for e in earlier],
        out_specs=ANY,
        out_shape=jax.ShapeDtypeStruct(array.shape, array.dtype),
        input_output_aliases={0: 0},
        name="hold",
    )(array, *earlier)


def attend(frame, head, position, query, own, before, after, partial, *earlier):
    groups, frames, tok, both = query.shape
    width = own.shape[-1]
    row_count = groups * tok
    groups_block = BLOCK_Q // tok
    order = ((2, 1, 3, 0, 4) if frame == 0 else (1, 2, 0, 3, 4))
    before_from = frame
    before_count = frames - frame
    after_count = frame + 1

    def kernel(pos_ref, q_ref, own_ref, before_ref, after_ref, *rest):
        out_ref, token_ref, kt_ref, vx_ref = rest[-4:]

        sources = (
            [(before_ref, f) for f in range(before_count)]
            + [(own_ref, f) for f in range(frames)]
            + [(after_ref, f) for f in range(after_count)]
        )

        @pl.when(pl.program_id(0) == 0)
        def _():
            for at, (ref, f) in enumerate(sources):
                rows = slice(at * row_count, (at + 1) * row_count)
                turned = ref[:, 0, f].reshape(row_count, width).T
                kt_ref[:width, rows] = turned
                kt_ref[width:, rows] = turned
                vx_ref[rows, :width] = ref[:, 1, f].reshape(row_count, width)
                vx_ref[rows, width:] = jnp.ones((row_count, width), vx_ref.dtype)

        q = q_ref[:, 0].reshape(BLOCK_Q, width).astype(jnp.float32) * SCALE_LOG2
        high = q.astype(jnp.bfloat16)
        low = (q - high.astype(jnp.float32)).astype(jnp.bfloat16)
        q = jnp.concatenate((high, low), axis=1)
        position_now = pos_ref[0]

        def scores(at):
            cols = slice(at * row_count, (at + 1) * row_count)
            return jnp.dot(q, kt_ref[:, cols], preferred_element_type=jnp.float32)

        top = jnp.full((BLOCK_Q, 1), NEG_FILL, jnp.float32)
        total = jnp.zeros((BLOCK_Q, 2 * width), jnp.float32)
        ahead = scores(order[0])
        for turn, at in enumerate(order):
            s = ahead
            if turn + 1 < SPAN:
                ahead = scores(order[turn + 1])
            peak = jnp.max(s, axis=1, keepdims=True)
            absent = None
            if at < before_count:
                absent = position_now == 0
            elif at >= before_count + frames:
                absent = position_now == QUEUE - 1
            if absent is not None:
                peak = jnp.where(absent, NEG_FILL, peak)
            lifted_top = jnp.maximum(top, peak)
            less = lifted_top if absent is None else jnp.where(absent, -NEG_FILL, lifted_top)
            weights = jnp.exp2(s - less).astype(jnp.bfloat16)
            rows = slice(at * row_count, (at + 1) * row_count)
            part = jnp.dot(weights, vx_ref[rows], preferred_element_type=jnp.float32)
            total = total * jnp.exp2(top - lifted_top) + part
            top = lifted_top
        result = total[:, :width] / total[:, width:]
        out_ref[...] = result.astype(out_ref.dtype).reshape(groups_block, tok, width)
        token_ref[...] = jnp.zeros_like(token_ref)

    in_specs = [
        pl.BlockSpec((groups_block, 1, tok, width), lambda b, pos: (b, frame, 0, head)),
        pl.BlockSpec(own.shape, lambda b, pos: (0, 0, 0, 0, 0)),
        pl.BlockSpec(
            (groups, 2, before_count, tok, width),
            lambda b, pos: (0, 0, before_from // before_count, 0, 0),
        ),
        pl.BlockSpec((groups, 2, after_count, tok, width), lambda b, pos: (0, 0, 0, 0, 0)),
    ]
    operands = [query, own, before, after]
    aliases = {}
    if partial is not None:
        aliases = {1 + len(operands): 0}
        operands.append(partial)
        in_specs.append(ANY)
    operands += earlier
    in_specs += [corner(e) for e in earlier]
    return pl.pallas_call(
        kernel,
        grid_spec=pltpu.PrefetchScalarGridSpec(
            num_scalar_prefetch=1,
            grid=(row_count // BLOCK_Q,),
            in_specs=in_specs,
            out_specs=[
                pl.BlockSpec((groups_block, tok, width), lambda b, pos: (b, 0, head)),
                pl.BlockSpec(TOKEN, lambda b, pos: (0, 0)),
            ],
            scratch_shapes=[
                pltpu.VMEM((2 * width, SPAN * row_count), jnp.bfloat16),
                pltpu.VMEM((SPAN * row_count, 2 * width), jnp.bfloat16),
            ],
        ),
        out_shape=[
            jax.ShapeDtypeStruct((groups, tok, both), query.dtype),
            jax.ShapeDtypeStruct(TOKEN, jnp.float32),
        ],
        input_output_aliases=aliases,
        compiler_params=pltpu.CompilerParams(vmem_limit_bytes=VMEM),
        cost_estimate=pl.CostEstimate(
            flops=row_count * SPAN * row_count * width * 8,
            bytes_accessed=4 * 1024 * 1024,
            transcendentals=row_count * SPAN * row_count,
        ),
        name="attend",
    )(position, *operands)


def project(frame, slot_shift, place, sources, weight_own, weight_pair, gates, *earlier):
    mine, left, right, far_low, far_high = sources
    groups, tok, width = mine.shape
    steps, sides, halves, rows_dev, cols_dev = weight_own.shape
    half = steps * sides
    depth = sides * width

    def kernel(
        place_ref, mine_ref, left_ref, right_ref, low_ref, high_ref, wo_ref, wp_ref, gates_ref, *rest
    ):
        out_ref, a_ref, total_ref = rest[-3:]
        x, core = place_ref[0], place_ref[1]
        step = pl.program_id(1)

        @pl.when((pl.program_id(0) == 0) & (step == 0))
        def _():
            for i in range(half):
                z, side = i // sides, i % sides
                for part in range(CORES):
                    group = side * half + CORES * z + (core if part == 0 else 1 - core)
                    cols = slice((part * half + i) * width, (part * half + i + 1) * width)
                    a_ref[0:tok, cols] = mine_ref[group]
                    a_ref[tok : 2 * tok, cols] = right_ref[group]
                    far = high_ref[group - half] if side else low_ref[group]
                    a_ref[2 * tok : 3 * tok, cols] = far
                    a_ref[3 * tok :, cols] = left_ref[group]

        @pl.when(step == 0)
        def _():
            total_ref[...] = jnp.zeros_like(total_ref)

        total = total_ref[...]
        for part, ref in enumerate((wo_ref, wp_ref)):
            start = pl.multiple_of(part * half * width + step * depth, depth)
            total += jnp.dot(
                a_ref[:, pl.ds(start, depth)],
                ref[0, :, 0].reshape(depth, cols_dev),
                preferred_element_type=jnp.float32,
            )
        total_ref[...] = total

        @pl.when(step == steps - 1)
        def _():
            for source in range(RING):
                at = lax.rem(x + source, RING)
                gate = gates_ref[0, pl.ds(at * 2 + frame, 1), :]
                rows = slice(source * tok, (source + 1) * tok)
                out_ref[lax.rem(at + slot_shift, RING), 0] = (gate * total_ref[rows]).astype(
                    out_ref.dtype
                )

    whole = pl.BlockSpec(mine.shape, lambda n, k, place: (0, 0, 0))
    part = pl.BlockSpec(far_low.shape, lambda n, k, place: (0, 0, 0))
    weight = pl.BlockSpec(
        (1, sides, 1, rows_dev, cols_dev), lambda n, k, place: (k, 0, n, 0, 0)
    )
    return pl.pallas_call(
        kernel,
        grid_spec=pltpu.PrefetchScalarGridSpec(
            num_scalar_prefetch=1,
            grid=(halves, steps),
            in_specs=[
                whole, whole, whole, part, part, weight, weight,
                pl.BlockSpec((1,) + gates.shape[1:], lambda n, k, place: (n, 0, 0)),
                *[corner(e) for e in earlier],
            ],
            out_specs=pl.BlockSpec((RING, 1, tok, cols_dev), lambda n, k, place: (0, n, 0, 0)),
            scratch_shapes=[
                pltpu.VMEM((RING * tok, groups * width), jnp.bfloat16),
                pltpu.VMEM((RING * tok, cols_dev), jnp.float32),
            ],
        ),
        out_shape=jax.ShapeDtypeStruct((RING, halves, tok, cols_dev), jnp.bfloat16),
        compiler_params=pltpu.CompilerParams(vmem_limit_bytes=VMEM),
        cost_estimate=pl.CostEstimate(
            flops=2 * RING * tok * groups * width * halves * cols_dev,
            bytes_accessed=12 * 1024 * 1024,
            transcendentals=0,
        ),
        name="project",
    )(place, *sources, weight_own, weight_pair, gates, *earlier)


def add_branch(slot, position, branch, base, entering, partial):
    sources, halves, tok, cols = branch.shape
    frames = 2
    first = slot == 0

    def kernel(pos_ref, b_ref, base_ref, *rest):
        out_ref = rest[-1]
        for half in range(halves):
            for source in range(sources):
                at = slice((half * sources + source) * cols, (half * sources + source + 1) * cols)
                value = base_ref[0, :, at].astype(jnp.float32) + b_ref[source, half].astype(jnp.float32)
                if first:
                    value = jnp.where(pos_ref[0] == 0, rest[0][:, at].astype(jnp.float32), value)
                out_ref[0, :, at] = value.astype(out_ref.dtype)

    frame_spec = pl.BlockSpec((1, tok, base.shape[-1]), lambda i, pos: (0, 0, 0))
    in_specs = [pl.BlockSpec(branch.shape, lambda i, pos: (0, 0, 0, 0)), frame_spec]
    if first:
        in_specs.append(pl.BlockSpec(entering.shape, lambda i, pos: (0, 0)))
        operands, aliases = [branch, base, entering], {}
    else:
        in_specs.append(ANY)
        operands, aliases = [branch, base, partial], {3: 0}
    return pl.pallas_call(
        kernel,
        grid_spec=pltpu.PrefetchScalarGridSpec(
            num_scalar_prefetch=1,
            grid=(1,),
            in_specs=in_specs,
            out_specs=pl.BlockSpec((1, tok, base.shape[-1]), lambda i, pos: (slot, 0, 0)),
        ),
        out_shape=jax.ShapeDtypeStruct((frames, tok, base.shape[-1]), base.dtype),
        input_output_aliases=aliases,
        name="add_branch",
    )(position, *operands)


def body(hidden, queries, keys, values, out_weight, gate_table, levels, entering):
    frames = queries.shape[0]
    position = lax.axis_index("queue")
    spatial = lax.axis_index("spatial")
    y_low, x = position // RING, position % RING
    core = spatial % CORES
    position_now = position.astype(jnp.int32)[None]
    place = jnp.stack((x, core)).astype(jnp.int32)

    up = [(p, p + 1) for p in range(QUEUE - 1)]
    down = [(p + 1, p) for p in range(QUEUE - 1)]
    ring = [[r * RING + i for i in range(RING)] for r in range(QUEUE // RING)]
    ring_up = [(g[i], g[(i + 1) % RING]) for g in ring for i in range(RING)]
    ring_down = [(g[(i + 1) % RING], g[i]) for g in ring for i in range(RING)]
    swap_low = [(p, (p + RING) % QUEUE) for p in range(QUEUE)]
    swap_core = [(s, s ^ 1) for s in range(SPATIAL)]
    along_y = [
        [(low * RING + i) * SPATIAL + side * (SPATIAL // 2) + r for side in range(2) for low in range(2)]
        for i in range(RING)
        for r in range(SPATIAL // 2)
    ]
    along_z = [
        [side * (SPATIAL // 2) + z * CORES + c for z in range(SPATIAL // 2 // CORES)]
        for side in range(2)
        for c in range(CORES)
    ]

    to_heads = functools.partial(
        lax.all_to_all, axis_name="spatial", split_axis=0, concat_axis=0, tiled=True
    )

    kv0, kv1, query = pack(queries, keys, values)
    kv0 = to_heads(kv0)
    kv1 = to_heads(hold(kv1, kv0))
    kv0 = hold(kv0, kv1)
    kv0_before, kv0_after = lax.ppermute(kv0, "queue", up), lax.ppermute(kv0, "queue", down)
    query = to_heads(hold(query, kv1))
    kv1 = hold(kv1, query)
    kv1_before, kv1_after = lax.ppermute(kv1, "queue", up), lax.ppermute(kv1, "queue", down)

    weight = lax.all_gather(out_weight, ("queue", "spatial"), axis_index_groups=along_y, axis=0)
    weight = hold(weight, query)
    weight = lax.all_gather(weight, "spatial", axis_index_groups=along_z, axis=0)
    weight = weight.reshape(-1, 2, 2, *out_weight.shape)

    selector = (levels[:, None] == jnp.arange(gate_table.shape[0], dtype=jnp.int32)[None, :]).astype(
        jnp.float32
    )
    gates = jnp.dot(
        selector, gate_table, precision=lax.Precision.HIGHEST, preferred_element_type=jnp.float32
    )
    other_gates = lax.ppermute(gates, "queue", swap_low)
    gates = jnp.where(y_low == 0, jnp.stack((gates, other_gates)), jnp.stack((other_gates, gates)))
    gates = lax.dynamic_slice_in_dim(gates, y_low * RING * frames, RING * frames, axis=1)

    def spread(attended):
        mine = to_heads(attended)
        left = lax.ppermute(mine, "queue", ring_up)
        right = lax.ppermute(mine, "queue", ring_down)
        far_low = lax.ppermute(left[: SPATIAL // 2], "queue", ring_up)
        far_high = lax.ppermute(right[SPATIAL // 2 :], "queue", ring_down)
        return mine, left, right, far_low, far_high

    head0 = (position_now, query, kv0, kv0_before, kv0_after)
    head1 = (position_now, query, kv1, kv1_before, kv1_after)
    odd, token = attend(1, 0, *head0, None)
    even, token = attend(0, 0, *head0, None, token, gates)
    shifted = lax.ppermute(last_frame(hidden, token), "queue", up)
    odd, token = attend(1, 1, *head1, odd, token)
    odd_sources = spread(odd)
    even, token = attend(0, 1, *head1, even, token)
    even_sources = spread(even)
    weight_own = hold(weight, token)
    weight_pair = lax.ppermute(weight_own, "spatial", swap_core)

    branch = project(1, 1, place, odd_sources, weight_own, weight_pair, gates, shifted)
    crossing = lax.ppermute(branch[:1], "queue", [(p, p + RING) for p in range(QUEUE - RING)])
    branch = jnp.concatenate((crossing, branch[1:]))
    to_positions = functools.partial(
        lax.all_to_all, axis_name="queue", split_axis=0, concat_axis=0, axis_index_groups=ring, tiled=True
    )
    result = add_branch(0, position_now, to_positions(branch), shifted, entering, None)
    branch = project(0, 0, place, even_sources, weight_own, weight_pair, gates)
    return add_branch(1, position_now, to_positions(branch), hidden, None, result)


def solution(mesh):
    return jax.shard_map(
        body,
        mesh=mesh,
        in_specs=(
            P("queue", "spatial", None),
            P("queue", "spatial", None),
            P("queue", "spatial", None),
            P("queue", "spatial", None),
            P("spatial", "queue"),
            P(None, "queue"),
            P(),
            P("spatial", None),
        ),
        out_specs=P("queue", "spatial", None),
        check_vma=False,
    )
```

```python
import functools

import jax
import jax.numpy as jnp
from jax import lax
from jax.experimental import pallas as pl
from jax.experimental.pallas import tpu as pltpu
from jax.sharding import PartitionSpec as P

HEADS = 32
HD = 128
WMAX = 2
NEG_FILL = -1e30
SCALE_LOG2 = (HD ** -0.5) * 1.4426950408889634
BLOCK_Q = 512
VMEM = 48 * 1024 * 1024
QUEUE = 8
RING = 4
SPATIAL = 16
CORES = 2
PACK = 4
SPAN = 2 * WMAX + 1
ANY = pl.BlockSpec(memory_space=pl.ANY)
TOKEN = (8, 128)


def corner(array):
    rows = 8 if array.dtype == jnp.float32 else 16
    block = (1,) * (array.ndim - 2) + (rows, 128)
    return pl.BlockSpec(block, lambda *at: (0,) * array.ndim)


def pack(queries, keys, values):
    frames, tok, width = keys.shape
    group = width // SPATIAL
    piece = width // PACK
    count = SPATIAL // PACK

    def kernel(q_ref, k_ref, v_ref, kv0_ref, kv1_ref, out_ref):
        for i in range(count):
            for head, kv_ref in enumerate((kv0_ref, kv1_ref)):
                cols = slice(i * group + head * HD, i * group + (head + 1) * HD)
                kv_ref[i, 0] = k_ref[:, :, cols]
                kv_ref[i, 1] = v_ref[:, :, cols]
            out_ref[i] = q_ref[:, :, i * group : (i + 1) * group]

    spec = pl.BlockSpec((frames, tok, piece), lambda s: (0, 0, s))
    kv_spec = pl.BlockSpec((count, 2, frames, tok, HD), lambda s: (s, 0, 0, 0, 0))
    kv_shape = jax.ShapeDtypeStruct((SPATIAL, 2, frames, tok, HD), keys.dtype)
    return pl.pallas_call(
        kernel,
        grid=(PACK,),
        in_specs=[spec] * 3,
        out_specs=[kv_spec, kv_spec, pl.BlockSpec((count, frames, tok, group), lambda s: (s, 0, 0, 0))],
        out_shape=[
            kv_shape,
            kv_shape,
            jax.ShapeDtypeStruct((SPATIAL, frames, tok, group), queries.dtype),
        ],
        name="pack",
    )(queries, keys, values)


def last_frame(hidden, *earlier):
    frames, tok, width = hidden.shape

    def kernel(hidden_ref, *rest):
        rest[-1][...] = hidden_ref[...]

    return pl.pallas_call(
        kernel,
        grid=(1,),
        in_specs=[pl.BlockSpec((1, tok, width), lambda i: (frames - 1, 0, 0))]
        + [corner(e) for e in earlier],
        out_specs=pl.BlockSpec((1, tok, width), lambda i: (0, 0, 0)),
        out_shape=jax.ShapeDtypeStruct((1, tok, width), hidden.dtype),
        name="last_frame",
    )(hidden, *earlier)


def hold(array, *earlier):
    def kernel(*refs):
        pass

    return pl.pallas_call(
        kernel,
        grid=(1,),
        in_specs=[ANY] + [corner(e) for e in earlier],
        out_specs=ANY,
        out_shape=jax.ShapeDtypeStruct(array.shape, array.dtype),
        input_output_aliases={0: 0},
        name="hold",
    )(array, *earlier)


def attend(frame, position, query, head, own, before, after, *earlier):
    groups, frames, tok, both = query.shape
    width = own.shape[-1]
    row_count = groups * tok
    groups_block = BLOCK_Q // tok
    blocks = row_count // BLOCK_Q
    asked = range(frames) if frame is None else (frame,)
    before_from = min(asked)
    before_count = frames - before_from
    after_count = max(asked) + 1
    loaded = before_count + frames + after_count

    def kernel(pos_ref, q_ref, own_ref, before_ref, after_ref, *rest):
        out_ref, token_ref, kt_ref, vx_ref = rest[-4:]
        sources = (
            [(before_ref, f) for f in range(before_count)]
            + [(own_ref, f) for f in range(frames)]
            + [(after_ref, f) for f in range(after_count)]
        )
        turn_frame = pl.program_id(0)

        @pl.when((turn_frame == 0) & (pl.program_id(1) == 0))
        def _():
            for at, (ref, f) in enumerate(sources):
                rows = slice(at * row_count, (at + 1) * row_count)
                turned = ref[:, 0, f].reshape(row_count, width).T
                kt_ref[:width, rows] = turned
                kt_ref[width:, rows] = turned
                vx_ref[rows, :width] = ref[:, 1, f].reshape(row_count, width)
                vx_ref[rows, width:] = jnp.ones((row_count, width), vx_ref.dtype)

        q = q_ref[:, 0].reshape(BLOCK_Q, width).astype(jnp.float32) * SCALE_LOG2
        high = q.astype(jnp.bfloat16)
        low = (q - high.astype(jnp.float32)).astype(jnp.bfloat16)
        q = jnp.concatenate((high, low), axis=1)
        position_now = pos_ref[0]

        def rows_of(step):
            start = (turn_frame + step) * row_count
            return pl.ds(pl.multiple_of(start, row_count), row_count)

        def scores(step):
            return jnp.dot(q, kt_ref[:, rows_of(step)], preferred_element_type=jnp.float32)

        top = jnp.full((BLOCK_Q, 1), NEG_FILL, jnp.float32)
        total = jnp.zeros((BLOCK_Q, 2 * width), jnp.float32)
        order = (2, 1, 3, 0, 4)
        ahead = scores(order[0])
        for turn, step in enumerate(order):
            s = ahead
            if turn + 1 < SPAN:
                ahead = scores(order[turn + 1])
            at = turn_frame + step
            absent = ((position_now == 0) & (at < before_count)) | (
                (position_now == QUEUE - 1) & (at >= before_count + frames)
            )
            peak = jnp.max(s, axis=1, keepdims=True)
            peak = jnp.where(absent, NEG_FILL, peak)
            lifted_top = jnp.maximum(top, peak)
            less = jnp.where(absent, -NEG_FILL, lifted_top)
            weights = jnp.exp2(s - less).astype(jnp.bfloat16)
            part = jnp.dot(weights, vx_ref[rows_of(step)], preferred_element_type=jnp.float32)
            total = total * jnp.exp2(top - lifted_top) + part
            top = lifted_top
        result = total[:, :width] / total[:, width:]
        out_ref[:, 0] = result.astype(out_ref.dtype).reshape(groups_block, tok, width)
        token_ref[...] = jnp.zeros_like(token_ref)

    first = asked[0]
    in_specs = [
        pl.BlockSpec((groups_block, 1, tok, width), lambda f, b, pos: (b, first + f, 0, head)),
        pl.BlockSpec(own.shape, lambda f, b, pos: (0, 0, 0, 0, 0)),
        pl.BlockSpec(
            (groups, 2, before_count, tok, width),
            lambda f, b, pos: (0, 0, before_from // before_count, 0, 0),
        ),
        pl.BlockSpec((groups, 2, after_count, tok, width), lambda f, b, pos: (0, 0, 0, 0, 0)),
    ]
    return pl.pallas_call(
        kernel,
        grid_spec=pltpu.PrefetchScalarGridSpec(
            num_scalar_prefetch=1,
            grid=(len(asked), blocks),
            in_specs=in_specs + [corner(e) for e in earlier],
            out_specs=[
                pl.BlockSpec((groups_block, 1, tok, width), lambda f, b, pos: (b, f, 0, 0)),
                pl.BlockSpec(TOKEN, lambda f, b, pos: (0, 0)),
            ],
            scratch_shapes=[
                pltpu.VMEM((2 * width, loaded * row_count), jnp.bfloat16),
                pltpu.VMEM((loaded * row_count, 2 * width), jnp.bfloat16),
            ],
        ),
        out_shape=[
            jax.ShapeDtypeStruct((groups, len(asked), tok, width), query.dtype),
            jax.ShapeDtypeStruct(TOKEN, jnp.float32),
        ],
        compiler_params=pltpu.CompilerParams(vmem_limit_bytes=VMEM),
        cost_estimate=pl.CostEstimate(
            flops=len(asked) * row_count * SPAN * row_count * width * 8,
            bytes_accessed=4 * 1024 * 1024,
            transcendentals=len(asked) * row_count * SPAN * row_count,
        ),
        name="attend",
    )(position, query, own, before, after, *earlier)


def project(frame, slot_shift, place, whole_sources, frame_sources, weight_own, weight_pair, gates, *earlier):
    groups, _, tok, width = frame_sources[0].shape
    steps, sides, halves, rows_dev, cols_dev = weight_own.shape
    half = steps * sides
    depth = sides * rows_dev
    count = len(frame_sources)

    def kernel(place_ref, *refs):
        heads = refs[:count], refs[count : 2 * count]
        wo_ref, wp_ref, gates_ref = refs[2 * count : 2 * count + 3]
        out_ref, a_ref, total_ref = refs[-3:]
        x, core = place_ref[0], place_ref[1]
        step = pl.program_id(1)

        @pl.when((pl.program_id(0) == 0) & (step == 0))
        def _():
            for i in range(half):
                z, side = i // sides, i % sides
                for part in range(CORES):
                    group = side * half + CORES * z + (core if part == 0 else 1 - core)
                    for head, (mine_ref, left_ref, right_ref, low_ref, high_ref) in enumerate(heads):
                        start = (part * half + i) * rows_dev + head * width
                        cols = slice(start, start + width)
                        a_ref[0:tok, cols] = mine_ref[group, 0]
                        a_ref[tok : 2 * tok, cols] = right_ref[group, 0]
                        far = high_ref[group - half, 0] if side else low_ref[group, 0]
                        a_ref[2 * tok : 3 * tok, cols] = far
                        a_ref[3 * tok :, cols] = left_ref[group, 0]

        @pl.when(step == 0)
        def _():
            total_ref[...] = jnp.zeros_like(total_ref)

        total = total_ref[...]
        for part, ref in enumerate((wo_ref, wp_ref)):
            start = pl.multiple_of(part * half * rows_dev + step * depth, depth)
            total += jnp.dot(
                a_ref[:, pl.ds(start, depth)],
                ref[0, :, 0].reshape(depth, cols_dev),
                preferred_element_type=jnp.float32,
            )
        total_ref[...] = total

        @pl.when(step == steps - 1)
        def _():
            for source in range(RING):
                at = lax.rem(x + source, RING)
                gate = gates_ref[0, pl.ds(at * 2 + frame, 1), :]
                rows = slice(source * tok, (source + 1) * tok)
                out_ref[lax.rem(at + slot_shift, RING), 0] = (gate * total_ref[rows]).astype(
                    out_ref.dtype
                )

    def source_spec(array, at):
        return pl.BlockSpec((array.shape[0], 1, tok, width), lambda n, k, place: (0, at, 0, 0))

    weight = pl.BlockSpec((1, sides, 1, rows_dev, cols_dev), lambda n, k, place: (k, 0, n, 0, 0))
    return pl.pallas_call(
        kernel,
        grid_spec=pltpu.PrefetchScalarGridSpec(
            num_scalar_prefetch=1,
            grid=(halves, steps),
            in_specs=[
                *[source_spec(a, frame) for a in whole_sources],
                *[source_spec(a, 0) for a in frame_sources],
                weight,
                weight,
                pl.BlockSpec((1,) + gates.shape[1:], lambda n, k, place: (n, 0, 0)),
                *[corner(e) for e in earlier],
            ],
            out_specs=pl.BlockSpec((RING, 1, tok, cols_dev), lambda n, k, place: (0, n, 0, 0)),
            scratch_shapes=[
                pltpu.VMEM((RING * tok, groups * rows_dev), jnp.bfloat16),
                pltpu.VMEM((RING * tok, cols_dev), jnp.float32),
            ],
        ),
        out_shape=jax.ShapeDtypeStruct((RING, halves, tok, cols_dev), jnp.bfloat16),
        compiler_params=pltpu.CompilerParams(vmem_limit_bytes=VMEM),
        cost_estimate=pl.CostEstimate(
            flops=2 * RING * tok * groups * rows_dev * halves * cols_dev,
            bytes_accessed=12 * 1024 * 1024,
            transcendentals=0,
        ),
        name="project",
    )(place, *whole_sources, *frame_sources, weight_own, weight_pair, gates, *earlier)


def add_branch(slot, position, branch, base, entering, partial):
    sources, halves, tok, cols = branch.shape
    frames = 2
    first = slot == 0

    def kernel(pos_ref, b_ref, base_ref, *rest):
        out_ref = rest[-1]
        for half in range(halves):
            for source in range(sources):
                at = slice((half * sources + source) * cols, (half * sources + source + 1) * cols)
                value = base_ref[0, :, at].astype(jnp.float32) + b_ref[source, half].astype(jnp.float32)
                if first:
                    value = jnp.where(pos_ref[0] == 0, rest[0][:, at].astype(jnp.float32), value)
                out_ref[0, :, at] = value.astype(out_ref.dtype)

    frame_spec = pl.BlockSpec((1, tok, base.shape[-1]), lambda i, pos: (0, 0, 0))
    in_specs = [pl.BlockSpec(branch.shape, lambda i, pos: (0, 0, 0, 0)), frame_spec]
    if first:
        in_specs.append(pl.BlockSpec(entering.shape, lambda i, pos: (0, 0)))
        operands, aliases = [branch, base, entering], {}
    else:
        in_specs.append(ANY)
        operands, aliases = [branch, base, partial], {3: 0}
    return pl.pallas_call(
        kernel,
        grid_spec=pltpu.PrefetchScalarGridSpec(
            num_scalar_prefetch=1,
            grid=(1,),
            in_specs=in_specs,
            out_specs=pl.BlockSpec((1, tok, base.shape[-1]), lambda i, pos: (slot, 0, 0)),
        ),
        out_shape=jax.ShapeDtypeStruct((frames, tok, base.shape[-1]), base.dtype),
        input_output_aliases=aliases,
        name="add_branch",
    )(position, *operands)


def body(hidden, queries, keys, values, out_weight, gate_table, levels, entering):
    frames = queries.shape[0]
    position = lax.axis_index("queue")
    spatial = lax.axis_index("spatial")
    y_low, x = position // RING, position % RING
    core = spatial % CORES
    position_now = position.astype(jnp.int32)[None]
    place = jnp.stack((x, core)).astype(jnp.int32)

    up = [(p, p + 1) for p in range(QUEUE - 1)]
    down = [(p + 1, p) for p in range(QUEUE - 1)]
    ring = [[r * RING + i for i in range(RING)] for r in range(QUEUE // RING)]
    ring_up = [(g[i], g[(i + 1) % RING]) for g in ring for i in range(RING)]
    ring_down = [(g[(i + 1) % RING], g[i]) for g in ring for i in range(RING)]
    swap_low = [(p, (p + RING) % QUEUE) for p in range(QUEUE)]
    swap_core = [(s, s ^ 1) for s in range(SPATIAL)]
    along_y = [
        [(low * RING + i) * SPATIAL + side * (SPATIAL // 2) + r for side in range(2) for low in range(2)]
        for i in range(RING)
        for r in range(SPATIAL // 2)
    ]
    along_z = [
        [side * (SPATIAL // 2) + z * CORES + c for z in range(SPATIAL // 2 // CORES)]
        for side in range(2)
        for c in range(CORES)
    ]

    to_heads = functools.partial(
        lax.all_to_all, axis_name="spatial", split_axis=0, concat_axis=0, tiled=True
    )

    selector = (levels[:, None] == jnp.arange(gate_table.shape[0], dtype=jnp.int32)[None, :]).astype(
        jnp.float32
    )
    gates = jnp.dot(
        selector, gate_table, precision=lax.Precision.HIGHEST, preferred_element_type=jnp.float32
    )
    other_gates = lax.ppermute(gates, "queue", swap_low)
    gates = jnp.where(y_low == 0, jnp.stack((gates, other_gates)), jnp.stack((other_gates, gates)))
    gates = lax.dynamic_slice_in_dim(gates, y_low * RING * frames, RING * frames, axis=1)

    kv0, kv1, query = pack(queries, keys, values)
    kv0 = to_heads(kv0)
    kv0_before, kv0_after = lax.ppermute(kv0, "queue", up), lax.ppermute(kv0, "queue", down)
    kv1 = to_heads(hold(kv1, kv0, gates))
    query = to_heads(hold(query, kv1, kv0_before, kv0_after))
    shifted = lax.ppermute(last_frame(hidden, kv0_before), "queue", up)
    kv1 = hold(kv1, query, shifted)
    kv1_before, kv1_after = lax.ppermute(kv1, "queue", up), lax.ppermute(kv1, "queue", down)

    weight = lax.all_gather(out_weight, ("queue", "spatial"), axis_index_groups=along_y, axis=0)
    weight = hold(weight, query)
    weight = lax.all_gather(weight, "spatial", axis_index_groups=along_z, axis=0)
    weight = weight.reshape(-1, 2, 2, *out_weight.shape)

    def spread(attended):
        mine = to_heads(attended)
        left = lax.ppermute(mine, "queue", ring_up)
        right = lax.ppermute(mine, "queue", ring_down)
        far_low = lax.ppermute(left[: SPATIAL // 2], "queue", ring_up)
        far_high = lax.ppermute(right[SPATIAL // 2 :], "queue", ring_down)
        return mine, left, right, far_low, far_high

    first, token = attend(None, position_now, query, 0, kv0, kv0_before, kv0_after)
    whole_sources = spread(first)
    head1 = (position_now, query, 1, kv1, kv1_before, kv1_after)
    odd, token = attend(1, *head1, token, whole_sources[0])
    odd_sources = spread(odd)
    even, token = attend(0, *head1, token, *whole_sources[1:3])
    even_sources = spread(even)
    weight_own = hold(weight, token)
    weight_pair = lax.ppermute(weight_own, "spatial", swap_core)
    weights = (weight_own, weight_pair, gates)

    branch = project(1, 1, place, whole_sources, odd_sources, *weights)
    crossing = lax.ppermute(branch[:1], "queue", [(p, p + RING) for p in range(QUEUE - RING)])
    branch = jnp.concatenate((crossing, branch[1:]))
    to_positions = functools.partial(
        lax.all_to_all, axis_name="queue", split_axis=0, concat_axis=0, axis_index_groups=ring, tiled=True
    )
    result = add_branch(0, position_now, to_positions(branch), shifted, entering, None)
    branch = project(0, 0, place, whole_sources, even_sources, *weights)
    return add_branch(1, position_now, to_positions(branch), hidden, None, result)


def solution(mesh):
    return jax.shard_map(
        body,
        mesh=mesh,
        in_specs=(
            P("queue", "spatial", None),
            P("queue", "spatial", None),
            P("queue", "spatial", None),
            P("queue", "spatial", None),
            P("spatial", "queue"),
            P(None, "queue"),
            P(),
            P("spatial", None),
        ),
        out_specs=P("queue", "spatial", None),
        check_vma=False,
    )
```

```python
import functools

import jax
import jax.numpy as jnp
from jax import lax
from jax.experimental import pallas as pl
from jax.experimental.pallas import tpu as pltpu
from jax.sharding import PartitionSpec as P

HEADS = 32
HD = 128
WMAX = 2
NEG_FILL = -1e30
SCALE_LOG2 = (HD ** -0.5) * 1.4426950408889634
BLOCK_Q = 512
VMEM = 48 * 1024 * 1024
QUEUE = 8
RING = 4
SPATIAL = 16
CORES = 2
PACK = 4
SPAN = 2 * WMAX + 1
ANY = pl.BlockSpec(memory_space=pl.ANY)
TOKEN = (8, 128)


def corner(array):
    rows = 8 if array.dtype == jnp.float32 else 16
    block = (1,) * (array.ndim - 2) + (rows, 128)
    return pl.BlockSpec(block, lambda *at: (0,) * array.ndim)


def pack(queries, keys, values):
    frames, tok, width = keys.shape
    group = width // SPATIAL
    piece = width // PACK
    count = SPATIAL // PACK

    def kernel(q_ref, k_ref, v_ref, kv0_ref, kv1_ref, out_ref):
        for i in range(count):
            for head, kv_ref in enumerate((kv0_ref, kv1_ref)):
                cols = slice(i * group + head * HD, i * group + (head + 1) * HD)
                kv_ref[i, 0] = k_ref[:, :, cols]
                kv_ref[i, 1] = v_ref[:, :, cols]
            out_ref[i] = q_ref[:, :, i * group : (i + 1) * group]

    spec = pl.BlockSpec((frames, tok, piece), lambda s: (0, 0, s))
    kv_spec = pl.BlockSpec((count, 2, frames, tok, HD), lambda s: (s, 0, 0, 0, 0))
    kv_shape = jax.ShapeDtypeStruct((SPATIAL, 2, frames, tok, HD), keys.dtype)
    return pl.pallas_call(
        kernel,
        grid=(PACK,),
        in_specs=[spec] * 3,
        out_specs=[kv_spec, kv_spec, pl.BlockSpec((count, frames, tok, group), lambda s: (s, 0, 0, 0))],
        out_shape=[
            kv_shape,
            kv_shape,
            jax.ShapeDtypeStruct((SPATIAL, frames, tok, group), queries.dtype),
        ],
        name="pack",
    )(queries, keys, values)


def last_frame(hidden, *earlier):
    frames, tok, width = hidden.shape

    def kernel(hidden_ref, *rest):
        rest[-1][...] = hidden_ref[...]

    return pl.pallas_call(
        kernel,
        grid=(1,),
        in_specs=[pl.BlockSpec((1, tok, width), lambda i: (frames - 1, 0, 0))]
        + [corner(e) for e in earlier],
        out_specs=pl.BlockSpec((1, tok, width), lambda i: (0, 0, 0)),
        out_shape=jax.ShapeDtypeStruct((1, tok, width), hidden.dtype),
        name="last_frame",
    )(hidden, *earlier)


def hold(array, *earlier):
    def kernel(*refs):
        pass

    return pl.pallas_call(
        kernel,
        grid=(1,),
        in_specs=[ANY] + [corner(e) for e in earlier],
        out_specs=ANY,
        out_shape=jax.ShapeDtypeStruct(array.shape, array.dtype),
        input_output_aliases={0: 0},
        name="hold",
    )(array, *earlier)


def attend(frame, head, position, query, own, before, after, partial, *earlier):
    groups, frames, tok, both = query.shape
    width = own.shape[-1]
    row_count = groups * tok
    groups_block = BLOCK_Q // tok
    order = ((2, 1, 3, 0, 4) if frame == 0 else (1, 2, 0, 3, 4))
    before_from = frame
    before_count = frames - frame
    after_count = frame + 1

    def kernel(pos_ref, q_ref, own_ref, before_ref, after_ref, *rest):
        out_ref, token_ref, kt_ref, vx_ref = rest[-4:]

        sources = (
            [(before_ref, f) for f in range(before_count)]
            + [(own_ref, f) for f in range(frames)]
            + [(after_ref, f) for f in range(after_count)]
        )

        @pl.when(pl.program_id(0) == 0)
        def _():
            for at, (ref, f) in enumerate(sources):
                rows = slice(at * row_count, (at + 1) * row_count)
                turned = ref[:, 0, f].reshape(row_count, width).T
                kt_ref[:width, rows] = turned
                kt_ref[width:, rows] = turned
                vx_ref[rows, :width] = ref[:, 1, f].reshape(row_count, width)
                vx_ref[rows, width:] = jnp.ones((row_count, width), vx_ref.dtype)

        q = q_ref[:, 0].reshape(BLOCK_Q, width).astype(jnp.float32) * SCALE_LOG2
        high = q.astype(jnp.bfloat16)
        low = (q - high.astype(jnp.float32)).astype(jnp.bfloat16)
        q = jnp.concatenate((high, low), axis=1)
        position_now = pos_ref[0]

        def scores(at):
            cols = slice(at * row_count, (at + 1) * row_count)
            return jnp.dot(q, kt_ref[:, cols], preferred_element_type=jnp.float32)

        top = jnp.full((BLOCK_Q, 1), NEG_FILL, jnp.float32)
        total = jnp.zeros((BLOCK_Q, 2 * width), jnp.float32)
        ahead = scores(order[0])
        for turn, at in enumerate(order):
            s = ahead
            if turn + 1 < SPAN:
                ahead = scores(order[turn + 1])
            peak = jnp.max(s, axis=1, keepdims=True)
            absent = None
            if at < before_count:
                absent = position_now == 0
            elif at >= before_count + frames:
                absent = position_now == QUEUE - 1
            if absent is not None:
                peak = jnp.where(absent, NEG_FILL, peak)
            lifted_top = jnp.maximum(top, peak)
            less = lifted_top if absent is None else jnp.where(absent, -NEG_FILL, lifted_top)
            weights = jnp.exp2(s - less).astype(jnp.bfloat16)
            rows = slice(at * row_count, (at + 1) * row_count)
            part = jnp.dot(weights, vx_ref[rows], preferred_element_type=jnp.float32)
            total = total * jnp.exp2(top - lifted_top) + part
            top = lifted_top
        result = total[:, :width] / total[:, width:]
        out_ref[...] = result.astype(out_ref.dtype).reshape(groups_block, tok, width)
        token_ref[...] = jnp.zeros_like(token_ref)

    in_specs = [
        pl.BlockSpec((groups_block, 1, tok, width), lambda b, pos: (b, frame, 0, head)),
        pl.BlockSpec(own.shape, lambda b, pos: (0, 0, 0, 0, 0)),
        pl.BlockSpec(
            (groups, 2, before_count, tok, width),
            lambda b, pos: (0, 0, before_from // before_count, 0, 0),
        ),
        pl.BlockSpec((groups, 2, after_count, tok, width), lambda b, pos: (0, 0, 0, 0, 0)),
    ]
    operands = [query, own, before, after]
    aliases = {}
    if partial is not None:
        aliases = {1 + len(operands): 0}
        operands.append(partial)
        in_specs.append(ANY)
    operands += earlier
    in_specs += [corner(e) for e in earlier]
    return pl.pallas_call(
        kernel,
        grid_spec=pltpu.PrefetchScalarGridSpec(
            num_scalar_prefetch=1,
            grid=(row_count // BLOCK_Q,),
            in_specs=in_specs,
            out_specs=[
                pl.BlockSpec((groups_block, tok, width), lambda b, pos: (b, 0, head)),
                pl.BlockSpec(TOKEN, lambda b, pos: (0, 0)),
            ],
            scratch_shapes=[
                pltpu.VMEM((2 * width, SPAN * row_count), jnp.bfloat16),
                pltpu.VMEM((SPAN * row_count, 2 * width), jnp.bfloat16),
            ],
        ),
        out_shape=[
            jax.ShapeDtypeStruct((groups, tok, both), query.dtype),
            jax.ShapeDtypeStruct(TOKEN, jnp.float32),
        ],
        input_output_aliases=aliases,
        compiler_params=pltpu.CompilerParams(vmem_limit_bytes=VMEM),
        cost_estimate=pl.CostEstimate(
            flops=row_count * SPAN * row_count * width * 8,
            bytes_accessed=4 * 1024 * 1024,
            transcendentals=row_count * SPAN * row_count,
        ),
        name="attend",
    )(position, *operands)


def project(frame, slot_shift, place, sources, weight_own, weight_pair, gates, *earlier):
    mine, left, right, far_low, far_high = sources
    groups, tok, width = mine.shape
    steps, sides, halves, rows_dev, cols_dev = weight_own.shape
    half = steps * sides
    depth = sides * width

    def kernel(
        place_ref, mine_ref, left_ref, right_ref, low_ref, high_ref, wo_ref, wp_ref, gates_ref, *rest
    ):
        out_ref, a_ref, total_ref = rest[-3:]
        x, core = place_ref[0], place_ref[1]
        step = pl.program_id(1)

        @pl.when((pl.program_id(0) == 0) & (step == 0))
        def _():
            for i in range(half):
                z, side = i // sides, i % sides
                for part in range(CORES):
                    group = side * half + CORES * z + (core if part == 0 else 1 - core)
                    cols = slice((part * half + i) * width, (part * half + i + 1) * width)
                    a_ref[0:tok, cols] = mine_ref[group]
                    a_ref[tok : 2 * tok, cols] = right_ref[group]
                    far = high_ref[group - half] if side else low_ref[group]
                    a_ref[2 * tok : 3 * tok, cols] = far
                    a_ref[3 * tok :, cols] = left_ref[group]

        @pl.when(step == 0)
        def _():
            total_ref[...] = jnp.zeros_like(total_ref)

        total = total_ref[...]
        for part, ref in enumerate((wo_ref, wp_ref)):
            start = pl.multiple_of(part * half * width + step * depth, depth)
            total += jnp.dot(
                a_ref[:, pl.ds(start, depth)],
                ref[0, :, 0].reshape(depth, cols_dev),
                preferred_element_type=jnp.float32,
            )
        total_ref[...] = total

        @pl.when(step == steps - 1)
        def _():
            for source in range(RING):
                at = lax.rem(x + source, RING)
                gate = gates_ref[0, pl.ds(at * 2 + frame, 1), :]
                rows = slice(source * tok, (source + 1) * tok)
                out_ref[lax.rem(at + slot_shift, RING), 0] = (gate * total_ref[rows]).astype(
                    out_ref.dtype
                )

    whole = pl.BlockSpec(mine.shape, lambda n, k, place: (0, 0, 0))
    part = pl.BlockSpec(far_low.shape, lambda n, k, place: (0, 0, 0))
    weight = pl.BlockSpec(
        (1, sides, 1, rows_dev, cols_dev), lambda n, k, place: (k, 0, n, 0, 0)
    )
    return pl.pallas_call(
        kernel,
        grid_spec=pltpu.PrefetchScalarGridSpec(
            num_scalar_prefetch=1,
            grid=(halves, steps),
            in_specs=[
                whole, whole, whole, part, part, weight, weight,
                pl.BlockSpec((1,) + gates.shape[1:], lambda n, k, place: (n, 0, 0)),
                *[corner(e) for e in earlier],
            ],
            out_specs=pl.BlockSpec((RING, 1, tok, cols_dev), lambda n, k, place: (0, n, 0, 0)),
            scratch_shapes=[
                pltpu.VMEM((RING * tok, groups * width), jnp.bfloat16),
                pltpu.VMEM((RING * tok, cols_dev), jnp.float32),
            ],
        ),
        out_shape=jax.ShapeDtypeStruct((RING, halves, tok, cols_dev), jnp.bfloat16),
        compiler_params=pltpu.CompilerParams(vmem_limit_bytes=VMEM),
        cost_estimate=pl.CostEstimate(
            flops=2 * RING * tok * groups * width * halves * cols_dev,
            bytes_accessed=12 * 1024 * 1024,
            transcendentals=0,
        ),
        name="project",
    )(place, *sources, weight_own, weight_pair, gates, *earlier)


def add_branch(slot, position, branch, base, entering, partial):
    sources, halves, tok, cols = branch.shape
    frames = 2
    first = slot == 0

    def kernel(pos_ref, b_ref, base_ref, *rest):
        out_ref = rest[-1]
        for half in range(halves):
            for source in range(sources):
                at = slice((half * sources + source) * cols, (half * sources + source + 1) * cols)
                value = base_ref[0, :, at].astype(jnp.float32) + b_ref[source, half].astype(jnp.float32)
                if first:
                    value = jnp.where(pos_ref[0] == 0, rest[0][:, at].astype(jnp.float32), value)
                out_ref[0, :, at] = value.astype(out_ref.dtype)

    frame_spec = pl.BlockSpec((1, tok, base.shape[-1]), lambda i, pos: (0, 0, 0))
    in_specs = [pl.BlockSpec(branch.shape, lambda i, pos: (0, 0, 0, 0)), frame_spec]
    if first:
        in_specs.append(pl.BlockSpec(entering.shape, lambda i, pos: (0, 0)))
        operands, aliases = [branch, base, entering], {}
    else:
        in_specs.append(ANY)
        operands, aliases = [branch, base, partial], {3: 0}
    return pl.pallas_call(
        kernel,
        grid_spec=pltpu.PrefetchScalarGridSpec(
            num_scalar_prefetch=1,
            grid=(1,),
            in_specs=in_specs,
            out_specs=pl.BlockSpec((1, tok, base.shape[-1]), lambda i, pos: (slot, 0, 0)),
        ),
        out_shape=jax.ShapeDtypeStruct((frames, tok, base.shape[-1]), base.dtype),
        input_output_aliases=aliases,
        name="add_branch",
    )(position, *operands)


def body(hidden, queries, keys, values, out_weight, gate_table, levels, entering):
    frames = queries.shape[0]
    position = lax.axis_index("queue")
    spatial = lax.axis_index("spatial")
    y_low, x = position // RING, position % RING
    core = spatial % CORES
    position_now = position.astype(jnp.int32)[None]
    place = jnp.stack((x, core)).astype(jnp.int32)

    up = [(p, p + 1) for p in range(QUEUE - 1)]
    down = [(p + 1, p) for p in range(QUEUE - 1)]
    ring = [[r * RING + i for i in range(RING)] for r in range(QUEUE // RING)]
    ring_up = [(g[i], g[(i + 1) % RING]) for g in ring for i in range(RING)]
    ring_down = [(g[(i + 1) % RING], g[i]) for g in ring for i in range(RING)]
    swap_low = [(p, (p + RING) % QUEUE) for p in range(QUEUE)]
    swap_core = [(s, s ^ 1) for s in range(SPATIAL)]
    along_y = [
        [(low * RING + i) * SPATIAL + side * (SPATIAL // 2) + r for side in range(2) for low in range(2)]
        for i in range(RING)
        for r in range(SPATIAL // 2)
    ]
    along_z = [
        [side * (SPATIAL // 2) + z * CORES + c for z in range(SPATIAL // 2 // CORES)]
        for side in range(2)
        for c in range(CORES)
    ]

    to_heads = functools.partial(
        lax.all_to_all, axis_name="spatial", split_axis=0, concat_axis=0, tiled=True
    )

    selector = (levels[:, None] == jnp.arange(gate_table.shape[0], dtype=jnp.int32)[None, :]).astype(
        jnp.float32
    )
    gates = jnp.dot(
        selector, gate_table, precision=lax.Precision.HIGHEST, preferred_element_type=jnp.float32
    )
    other_gates = lax.ppermute(gates, "queue", swap_low)
    gates = jnp.where(y_low == 0, jnp.stack((gates, other_gates)), jnp.stack((other_gates, gates)))
    gates = lax.dynamic_slice_in_dim(gates, y_low * RING * frames, RING * frames, axis=1)

    kv0, kv1, query = pack(queries, keys, values)
    kv0 = to_heads(kv0)
    kv1 = to_heads(hold(kv1, kv0, gates))
    kv0 = hold(kv0, kv1)
    kv0_before, kv0_after = lax.ppermute(kv0, "queue", up), lax.ppermute(kv0, "queue", down)
    query = to_heads(hold(query, kv1))
    kv1 = hold(kv1, query)
    kv1_before, kv1_after = lax.ppermute(kv1, "queue", up), lax.ppermute(kv1, "queue", down)

    weight = lax.all_gather(out_weight, ("queue", "spatial"), axis_index_groups=along_y, axis=0)
    weight = hold(weight, query)
    weight = lax.all_gather(weight, "spatial", axis_index_groups=along_z, axis=0)
    weight = weight.reshape(-1, 2, 2, *out_weight.shape)

    def spread(attended):
        mine = to_heads(attended)
        left = lax.ppermute(mine, "queue", ring_up)
        right = lax.ppermute(mine, "queue", ring_down)
        far_low = lax.ppermute(left[: SPATIAL // 2], "queue", ring_up)
        far_high = lax.ppermute(right[SPATIAL // 2 :], "queue", ring_down)
        return mine, left, right, far_low, far_high

    head0 = (position_now, query, kv0, kv0_before, kv0_after)
    head1 = (position_now, query, kv1, kv1_before, kv1_after)
    odd, token = attend(1, 0, *head0, None)
    shifted = lax.ppermute(last_frame(hidden, token), "queue", up)
    even, token = attend(0, 0, *head0, None, token)
    odd, token = attend(1, 1, *head1, odd, token)
    odd_sources = spread(odd)
    weight_own = hold(weight, token)
    weight_pair = lax.ppermute(weight_own, "spatial", swap_core)
    even, token = attend(0, 1, *head1, even, token, shifted)
    even_sources = spread(even)

    branch = project(1, 1, place, odd_sources, weight_own, weight_pair, gates)
    crossing = lax.ppermute(branch[:1], "queue", [(p, p + RING) for p in range(QUEUE - RING)])
    branch = jnp.concatenate((crossing, branch[1:]))
    to_positions = functools.partial(
        lax.all_to_all, axis_name="queue", split_axis=0, concat_axis=0, axis_index_groups=ring, tiled=True
    )
    result = add_branch(0, position_now, to_positions(branch), shifted, entering, None)
    branch = project(0, 0, place, even_sources, weight_own, weight_pair, gates)
    return add_branch(1, position_now, to_positions(branch), hidden, None, result)


def solution(mesh):
    return jax.shard_map(
        body,
        mesh=mesh,
        in_specs=(
            P("queue", "spatial", None),
            P("queue", "spatial", None),
            P("queue", "spatial", None),
            P("queue", "spatial", None),
            P("spatial", "queue"),
            P(None, "queue"),
            P(),
            P("spatial", None),
        ),
        out_specs=P("queue", "spatial", None),
        check_vma=False,
    )
```

```python
import functools

import jax
import jax.numpy as jnp
from jax import lax
from jax.experimental import pallas as pl
from jax.experimental.pallas import tpu as pltpu
from jax.sharding import PartitionSpec as P

HEADS = 32
HD = 128
WMAX = 2
NEG_FILL = -1e30
SCALE_LOG2 = (HD ** -0.5) * 1.4426950408889634
BLOCK_Q = 512
VMEM = 48 * 1024 * 1024
QUEUE = 8
RING = 4
SPATIAL = 16
CORES = 2
PACK = 4
SPAN = 2 * WMAX + 1
ANY = pl.BlockSpec(memory_space=pl.ANY)
TOKEN = (8, 128)


def corner(array):
    rows = 8 if array.dtype == jnp.float32 else 16
    block = (1,) * (array.ndim - 2) + (rows, 128)
    return pl.BlockSpec(block, lambda *at: (0,) * array.ndim)


def pack(queries, keys, values):
    frames, tok, width = keys.shape
    group = width // SPATIAL
    piece = width // PACK
    count = SPATIAL // PACK

    def kernel(q_ref, k_ref, v_ref, *out_refs):
        for i in range(count):
            for head, out_ref in enumerate(out_refs):
                cols = slice(i * group + head * HD, i * group + (head + 1) * HD)
                for at, ref in enumerate((q_ref, k_ref, v_ref)):
                    out_ref[i, at] = ref[:, :, cols]

    heads = group // HD
    return pl.pallas_call(
        kernel,
        grid=(PACK,),
        in_specs=[pl.BlockSpec((frames, tok, piece), lambda s: (0, 0, s))] * 3,
        out_specs=[pl.BlockSpec((count, 3, frames, tok, HD), lambda s: (s, 0, 0, 0, 0))] * heads,
        out_shape=[jax.ShapeDtypeStruct((SPATIAL, 3, frames, tok, HD), keys.dtype)] * heads,
        name="pack",
    )(queries, keys, values)


def last_frame(hidden, *earlier):
    frames, tok, width = hidden.shape

    def kernel(hidden_ref, *rest):
        rest[-1][...] = hidden_ref[...]

    return pl.pallas_call(
        kernel,
        grid=(1,),
        in_specs=[pl.BlockSpec((1, tok, width), lambda i: (frames - 1, 0, 0))]
        + [corner(e) for e in earlier],
        out_specs=pl.BlockSpec((1, tok, width), lambda i: (0, 0, 0)),
        out_shape=jax.ShapeDtypeStruct((1, tok, width), hidden.dtype),
        name="last_frame",
    )(hidden, *earlier)


def hold(array, *earlier):
    def kernel(*refs):
        pass

    return pl.pallas_call(
        kernel,
        grid=(1,),
        in_specs=[ANY] + [corner(e) for e in earlier],
        out_specs=ANY,
        out_shape=jax.ShapeDtypeStruct(array.shape, array.dtype),
        input_output_aliases={0: 0},
        name="hold",
    )(array, *earlier)


def attend(frame, position, own, before, after, *earlier):
    groups, _, frames, tok, width = own.shape
    row_count = groups * tok
    groups_block = BLOCK_Q // tok
    blocks = row_count // BLOCK_Q
    asked = range(frames) if frame is None else (frame,)
    before_from = min(asked)
    before_count = frames - before_from
    after_count = max(asked) + 1
    loaded = before_count + frames + after_count

    def kernel(pos_ref, q_ref, own_ref, before_ref, after_ref, *rest):
        out_ref, token_ref, kt_ref, vx_ref = rest[-4:]
        sources = (
            [(before_ref, 0, f) for f in range(before_count)]
            + [(own_ref, 1, f) for f in range(frames)]
            + [(after_ref, 0, f) for f in range(after_count)]
        )
        turn_frame = pl.program_id(0)

        @pl.when((turn_frame == 0) & (pl.program_id(1) == 0))
        def _():
            for at, (ref, key, f) in enumerate(sources):
                rows = slice(at * row_count, (at + 1) * row_count)
                turned = ref[:, key, f].reshape(row_count, width).T
                kt_ref[:width, rows] = turned
                kt_ref[width:, rows] = turned
                vx_ref[rows, :width] = ref[:, key + 1, f].reshape(row_count, width)
                vx_ref[rows, width:] = jnp.ones((row_count, width), vx_ref.dtype)

        q = q_ref[:, 0, 0].reshape(BLOCK_Q, width).astype(jnp.float32) * SCALE_LOG2
        high = q.astype(jnp.bfloat16)
        low = (q - high.astype(jnp.float32)).astype(jnp.bfloat16)
        q = jnp.concatenate((high, low), axis=1)
        position_now = pos_ref[0]

        def rows_of(step):
            start = (turn_frame + step) * row_count
            return pl.ds(pl.multiple_of(start, row_count), row_count)

        def scores(step):
            return jnp.dot(q, kt_ref[:, rows_of(step)], preferred_element_type=jnp.float32)

        top = jnp.full((BLOCK_Q, 1), NEG_FILL, jnp.float32)
        total = jnp.zeros((BLOCK_Q, 2 * width), jnp.float32)
        order = (2, 1, 3, 0, 4)
        ahead = scores(order[0])
        for turn, step in enumerate(order):
            s = ahead
            if turn + 1 < SPAN:
                ahead = scores(order[turn + 1])
            at = turn_frame + step
            absent = ((position_now == 0) & (at < before_count)) | (
                (position_now == QUEUE - 1) & (at >= before_count + frames)
            )
            peak = jnp.max(s, axis=1, keepdims=True)
            peak = jnp.where(absent, NEG_FILL, peak)
            lifted_top = jnp.maximum(top, peak)
            less = jnp.where(absent, -NEG_FILL, lifted_top)
            weights = jnp.exp2(s - less).astype(jnp.bfloat16)
            part = jnp.dot(weights, vx_ref[rows_of(step)], preferred_element_type=jnp.float32)
            total = total * jnp.exp2(top - lifted_top) + part
            top = lifted_top
        result = total[:, :width] / total[:, width:]
        out_ref[:, 0] = result.astype(out_ref.dtype).reshape(groups_block, tok, width)
        token_ref[...] = jnp.zeros_like(token_ref)

    first = asked[0]
    in_specs = [
        pl.BlockSpec((groups_block, 1, 1, tok, width), lambda f, b, pos: (b, 0, first + f, 0, 0)),
        pl.BlockSpec(own.shape, lambda f, b, pos: (0, 0, 0, 0, 0)),
        pl.BlockSpec(
            (groups, 2, before_count, tok, width),
            lambda f, b, pos: (0, 0, before_from // before_count, 0, 0),
        ),
        pl.BlockSpec((groups, 2, after_count, tok, width), lambda f, b, pos: (0, 0, 0, 0, 0)),
    ]
    return pl.pallas_call(
        kernel,
        grid_spec=pltpu.PrefetchScalarGridSpec(
            num_scalar_prefetch=1,
            grid=(len(asked), blocks),
            in_specs=in_specs + [corner(e) for e in earlier],
            out_specs=[
                pl.BlockSpec((groups_block, 1, tok, width), lambda f, b, pos: (b, f, 0, 0)),
                pl.BlockSpec(TOKEN, lambda f, b, pos: (0, 0)),
            ],
            scratch_shapes=[
                pltpu.VMEM((2 * width, loaded * row_count), jnp.bfloat16),
                pltpu.VMEM((loaded * row_count, 2 * width), jnp.bfloat16),
            ],
        ),
        out_shape=[
            jax.ShapeDtypeStruct((groups, len(asked), tok, width), own.dtype),
            jax.ShapeDtypeStruct(TOKEN, jnp.float32),
        ],
        compiler_params=pltpu.CompilerParams(vmem_limit_bytes=VMEM),
        cost_estimate=pl.CostEstimate(
            flops=len(asked) * row_count * SPAN * row_count * width * 8,
            bytes_accessed=4 * 1024 * 1024,
            transcendentals=len(asked) * row_count * SPAN * row_count,
        ),
        name="attend",
    )(position, own, own, before, after, *earlier)


def project(head, place, sources, weight_own, weight_pair, partial, gates, *earlier):
    mine = sources[0]
    groups, frames, tok, width = mine.shape
    steps, sides, halves, rows_dev, cols_dev = weight_own.shape
    half = steps * sides
    rows = frames * tok
    last = partial is not None

    def kernel(place_ref, mine_ref, left_ref, right_ref, low_ref, high_ref, wo_ref, wp_ref, *rest):
        out_ref, a_ref = rest[-2:]
        x, core = place_ref[0], place_ref[1]

        @pl.when(pl.program_id(0) == 0)
        def _():
            for i in range(half):
                z, side = i // sides, i % sides
                for part in range(CORES):
                    group = side * half + CORES * z + (core if part == 0 else 1 - core)
                    cols = slice((part * half + i) * width, (part * half + i + 1) * width)
                    far = high_ref[group - half] if side else low_ref[group]
                    a_ref[0:rows, cols] = mine_ref[group].reshape(rows, width)
                    a_ref[rows : 2 * rows, cols] = right_ref[group].reshape(rows, width)
                    a_ref[2 * rows : 3 * rows, cols] = far.reshape(rows, width)
                    a_ref[3 * rows :, cols] = left_ref[group].reshape(rows, width)

        total = jnp.dot(
            a_ref[:, : half * width],
            wo_ref[:, :, 0].reshape(half * width, cols_dev),
            preferred_element_type=jnp.float32,
        )
        total += jnp.dot(
            a_ref[:, half * width :],
            wp_ref[:, :, 0].reshape(half * width, cols_dev),
            preferred_element_type=jnp.float32,
        )
        if not last:
            out_ref[0] = total
            return
        total += rest[0][0]
        gates_ref = rest[1]
        for source in range(RING):
            at = lax.rem(x + source, RING)
            for f in range(frames):
                gate = gates_ref[0, pl.ds(at * frames + f, 1), :]
                start = source * rows + f * tok
                slot = at * frames + 1 if f == 0 else lax.rem(at + 1, RING) * frames
                out_ref[slot, 0] = (gate * total[start : start + tok]).astype(out_ref.dtype)

    def whole(array):
        return pl.BlockSpec(array.shape, lambda n, place: (0,) * array.ndim)

    weight = pl.BlockSpec(
        (steps, sides, 1, width, cols_dev), lambda n, place: (0, 0, n, head, 0)
    )
    partial_spec = pl.BlockSpec((1, RING * rows, cols_dev), lambda n, place: (n, 0, 0))
    in_specs = [*map(whole, sources), weight, weight]
    operands = [*sources, weight_own, weight_pair]
    if last:
        in_specs += [partial_spec, pl.BlockSpec((1,) + gates.shape[1:], lambda n, place: (n, 0, 0))]
        operands += [partial, gates]
        out_spec = pl.BlockSpec((RING * frames, 1, tok, cols_dev), lambda n, place: (0, n, 0, 0))
        out_shape = jax.ShapeDtypeStruct((RING * frames, halves, tok, cols_dev), jnp.bfloat16)
    else:
        out_spec = partial_spec
        out_shape = jax.ShapeDtypeStruct((halves, RING * rows, cols_dev), jnp.float32)
    return pl.pallas_call(
        kernel,
        grid_spec=pltpu.PrefetchScalarGridSpec(
            num_scalar_prefetch=1,
            grid=(halves,),
            in_specs=in_specs + [corner(e) for e in earlier],
            out_specs=out_spec,
            scratch_shapes=[pltpu.VMEM((RING * rows, groups * width), jnp.bfloat16)],
        ),
        out_shape=out_shape,
        compiler_params=pltpu.CompilerParams(vmem_limit_bytes=VMEM),
        cost_estimate=pl.CostEstimate(
            flops=2 * RING * rows * groups * width * halves * cols_dev,
            bytes_accessed=8 * 1024 * 1024,
            transcendentals=0,
        ),
        name="project_last" if last else "project_first",
    )(place, *operands, *earlier)


def add_branch(position, branch, hidden, shifted, entering):
    sources, frames, halves, tok, cols = branch.shape
    width = hidden.shape[-1]

    def kernel(pos_ref, b_ref, hidden_ref, shifted_ref, entering_ref, out_ref):
        def add(base_ref, replaced):
            for half in range(halves):
                for source in range(sources):
                    start = (half * sources + source) * cols
                    at = slice(start, start + cols)
                    value = base_ref[0, :, at].astype(jnp.float32)
                    value += b_ref[source, 0, half].astype(jnp.float32)
                    if replaced:
                        value = jnp.where(
                            pos_ref[0] == 0, entering_ref[:, at].astype(jnp.float32), value
                        )
                    out_ref[0, :, at] = value.astype(out_ref.dtype)

        @pl.when(pl.program_id(0) == 0)
        def _():
            add(shifted_ref, True)

        @pl.when(pl.program_id(0) == 1)
        def _():
            add(hidden_ref, False)

    frame_spec = pl.BlockSpec((1, tok, width), lambda i, pos: (0, 0, 0))
    return pl.pallas_call(
        kernel,
        grid_spec=pltpu.PrefetchScalarGridSpec(
            num_scalar_prefetch=1,
            grid=(frames,),
            in_specs=[
                pl.BlockSpec((sources, 1, halves, tok, cols), lambda i, pos: (0, i, 0, 0, 0)),
                frame_spec,
                frame_spec,
                pl.BlockSpec((tok, width), lambda i, pos: (0, 0)),
            ],
            out_specs=pl.BlockSpec((1, tok, width), lambda i, pos: (i, 0, 0)),
        ),
        out_shape=jax.ShapeDtypeStruct((frames, tok, width), hidden.dtype),
        name="add_branch",
    )(position, branch, hidden, shifted, entering)


def body(hidden, queries, keys, values, out_weight, gate_table, levels, entering):
    frames = queries.shape[0]
    position = lax.axis_index("queue")
    spatial = lax.axis_index("spatial")
    y_low, x = position // RING, position % RING
    core = spatial % CORES
    position_now = position.astype(jnp.int32)[None]
    place = jnp.stack((x, core)).astype(jnp.int32)

    up = [(p, p + 1) for p in range(QUEUE - 1)]
    down = [(p + 1, p) for p in range(QUEUE - 1)]
    ring = [[r * RING + i for i in range(RING)] for r in range(QUEUE // RING)]
    ring_up = [(g[i], g[(i + 1) % RING]) for g in ring for i in range(RING)]
    ring_down = [(g[(i + 1) % RING], g[i]) for g in ring for i in range(RING)]
    swap_low = [(p, (p + RING) % QUEUE) for p in range(QUEUE)]
    swap_core = [(s, s ^ 1) for s in range(SPATIAL)]
    along_y = [
        [(low * RING + i) * SPATIAL + side * (SPATIAL // 2) + r for side in range(2) for low in range(2)]
        for i in range(RING)
        for r in range(SPATIAL // 2)
    ]
    along_z = [
        [side * (SPATIAL // 2) + z * CORES + c for z in range(SPATIAL // 2 // CORES)]
        for side in range(2)
        for c in range(CORES)
    ]

    to_heads = functools.partial(
        lax.all_to_all, axis_name="spatial", split_axis=0, concat_axis=0, tiled=True
    )

    selector = (levels[:, None] == jnp.arange(gate_table.shape[0], dtype=jnp.int32)[None, :]).astype(
        jnp.float32
    )
    gates = jnp.dot(
        selector, gate_table, precision=lax.Precision.HIGHEST, preferred_element_type=jnp.float32
    )
    other_gates = lax.ppermute(gates, "queue", swap_low)
    gates = jnp.where(y_low == 0, jnp.stack((gates, other_gates)), jnp.stack((other_gates, gates)))
    count = RING * frames
    is_last = (jnp.arange(count, dtype=jnp.int32) == count - 1)[None, :, None] & (y_low == 1)
    gates = jnp.where(
        is_last,
        gates[:, count - 1 : count],
        lax.dynamic_slice_in_dim(gates, y_low * count, count, axis=1),
    )

    first, second = pack(queries, keys, values)
    first = to_heads(first)
    first_kv = first[:, 1:]
    first_sides = lax.ppermute(first_kv, "queue", up), lax.ppermute(first_kv, "queue", down)
    second = to_heads(hold(second, *first_sides, gates))
    second_kv = second[:, 1:]
    second_sides = lax.ppermute(second_kv, "queue", up), lax.ppermute(second_kv, "queue", down)

    weight = lax.all_gather(out_weight, ("queue", "spatial"), axis_index_groups=along_y, axis=0)
    weight = hold(weight, first)
    weight = lax.all_gather(weight, "spatial", axis_index_groups=along_z, axis=0)
    weight = weight.reshape(-1, 2, 2, *out_weight.shape)

    def spread(even, odd):
        crossing = lax.ppermute(odd, "queue", [(RING - 1, QUEUE - 1)])
        odd = jnp.where(position == QUEUE - 1, crossing, odd)
        mine = to_heads(jnp.concatenate((even, odd), axis=1))
        left = lax.ppermute(mine, "queue", ring_up)
        right = lax.ppermute(mine, "queue", ring_down)
        far_low = lax.ppermute(left[: SPATIAL // 2], "queue", ring_up)
        far_high = lax.ppermute(right[SPATIAL // 2 :], "queue", ring_down)
        return mine, left, right, far_low, far_high

    both, token = attend(None, position_now, first, *first_sides)
    shifted = lax.ppermute(last_frame(hidden, *second_sides), "queue", up)
    first_sources = spread(both[:, :1], both[:, 1:])
    odd, token = attend(1, position_now, second, *second_sides, token)
    weight_own = hold(weight, token)
    weight_pair = lax.ppermute(weight_own, "spatial", swap_core)
    even, token = attend(0, position_now, second, *second_sides, token, first_sources[0])
    second_sources = spread(even, odd)

    partial = project(0, place, first_sources, weight_own, weight_pair, None, None, shifted)
    branch = project(1, place, second_sources, weight_own, weight_pair, partial, gates)
    branch = lax.all_to_all(
        branch, "queue", split_axis=0, concat_axis=0, axis_index_groups=ring, tiled=True
    )
    branch = branch.reshape(RING, frames, *branch.shape[1:])
    return add_branch(position_now, branch, hidden, shifted, entering)


def solution(mesh):
    return jax.shard_map(
        body,
        mesh=mesh,
        in_specs=(
            P("queue", "spatial", None),
            P("queue", "spatial", None),
            P("queue", "spatial", None),
            P("queue", "spatial", None),
            P("spatial", "queue"),
            P(None, "queue"),
            P(),
            P("spatial", None),
        ),
        out_specs=P("queue", "spatial", None),
        check_vma=False,
    )
```

```python
import functools

import jax
import jax.numpy as jnp
from jax import lax
from jax.experimental import pallas as pl
from jax.experimental.pallas import tpu as pltpu
from jax.sharding import PartitionSpec as P

HEADS = 32
HD = 128
WMAX = 2
NEG_FILL = -1e30
SCALE_LOG2 = (HD ** -0.5) * 1.4426950408889634
BLOCK_Q = 512
VMEM = 48 * 1024 * 1024
QUEUE = 8
RING = 4
SPATIAL = 16
CORES = 2
PACK = 4
SPAN = 2 * WMAX + 1
ANY = pl.BlockSpec(memory_space=pl.ANY)
TOKEN = (8, 128)


def corner(array):
    rows = 8 if array.dtype == jnp.float32 else 16
    block = (1,) * (array.ndim - 2) + (rows, 128)
    return pl.BlockSpec(block, lambda *at: (0,) * array.ndim)


def pack(queries, keys, values):
    frames, tok, width = keys.shape
    group = width // SPATIAL
    piece = width // PACK
    count = SPATIAL // PACK

    def kernel(q_ref, k_ref, v_ref, kv0_ref, kv1_ref, out_ref):
        for i in range(count):
            for head, kv_ref in enumerate((kv0_ref, kv1_ref)):
                cols = slice(i * group + head * HD, i * group + (head + 1) * HD)
                kv_ref[i, 0] = k_ref[:, :, cols]
                kv_ref[i, 1] = v_ref[:, :, cols]
            out_ref[i] = q_ref[:, :, i * group : (i + 1) * group]

    spec = pl.BlockSpec((frames, tok, piece), lambda s: (0, 0, s))
    kv_spec = pl.BlockSpec((count, 2, frames, tok, HD), lambda s: (s, 0, 0, 0, 0))
    kv_shape = jax.ShapeDtypeStruct((SPATIAL, 2, frames, tok, HD), keys.dtype)
    return pl.pallas_call(
        kernel,
        grid=(PACK,),
        in_specs=[spec] * 3,
        out_specs=[kv_spec, kv_spec, pl.BlockSpec((count, frames, tok, group), lambda s: (s, 0, 0, 0))],
        out_shape=[
            kv_shape,
            kv_shape,
            jax.ShapeDtypeStruct((SPATIAL, frames, tok, group), queries.dtype),
        ],
        name="pack",
    )(queries, keys, values)


def assemble(position, first, first_crossing, even, odd, odd_crossing, *earlier):
    groups, frames, tok, width = first.shape
    count = groups // PACK

    def kernel(pos_ref, first_ref, crossing0_ref, even_ref, odd_ref, crossing1_ref, *rest):
        out_ref = rest[-1]
        out_ref[:, 0, :, :width] = first_ref[:, 0]
        out_ref[:, 0, :, width:] = even_ref[:, 0]

        @pl.when(pos_ref[0] != QUEUE - 1)
        def _():
            out_ref[:, 1, :, :width] = first_ref[:, 1]
            out_ref[:, 1, :, width:] = odd_ref[:, 0]

        @pl.when(pos_ref[0] == QUEUE - 1)
        def _():
            out_ref[:, 1, :, :width] = crossing0_ref[:, 0]
            out_ref[:, 1, :, width:] = crossing1_ref[:, 0]

    one = pl.BlockSpec((count, 1, tok, width), lambda s, pos: (s, 0, 0, 0))
    return pl.pallas_call(
        kernel,
        grid_spec=pltpu.PrefetchScalarGridSpec(
            num_scalar_prefetch=1,
            grid=(PACK,),
            in_specs=[
                pl.BlockSpec((count, frames, tok, width), lambda s, pos: (s, 0, 0, 0)),
                one, one, one, one,
                *[corner(e) for e in earlier],
            ],
            out_specs=pl.BlockSpec((count, frames, tok, 2 * width), lambda s, pos: (s, 0, 0, 0)),
        ),
        out_shape=jax.ShapeDtypeStruct((groups, frames, tok, 2 * width), first.dtype),
        name="assemble",
    )(position, first, first_crossing, even, odd, odd_crossing, *earlier)


def last_frame(hidden, *earlier):
    frames, tok, width = hidden.shape

    def kernel(hidden_ref, *rest):
        rest[-1][...] = hidden_ref[...]

    return pl.pallas_call(
        kernel,
        grid=(1,),
        in_specs=[pl.BlockSpec((1, tok, width), lambda i: (frames - 1, 0, 0))]
        + [corner(e) for e in earlier],
        out_specs=pl.BlockSpec((1, tok, width), lambda i: (0, 0, 0)),
        out_shape=jax.ShapeDtypeStruct((1, tok, width), hidden.dtype),
        name="last_frame",
    )(hidden, *earlier)


def hold(array, *earlier):
    def kernel(*refs):
        pass

    return pl.pallas_call(
        kernel,
        grid=(1,),
        in_specs=[ANY] + [corner(e) for e in earlier],
        out_specs=ANY,
        out_shape=jax.ShapeDtypeStruct(array.shape, array.dtype),
        input_output_aliases={0: 0},
        name="hold",
    )(array, *earlier)


def attend(frame, position, query, head, own, before, after, *earlier):
    groups, frames, tok, both = query.shape
    width = own.shape[-1]
    row_count = groups * tok
    groups_block = BLOCK_Q // tok
    blocks = row_count // BLOCK_Q
    asked = range(frames) if frame is None else (frame,)
    before_from = min(asked)
    before_count = frames - before_from
    after_count = max(asked) + 1
    loaded = before_count + frames + after_count

    def kernel(pos_ref, q_ref, own_ref, before_ref, after_ref, *rest):
        out_ref, token_ref, kt_ref, vx_ref = rest[-4:]
        sources = (
            [(before_ref, f) for f in range(before_count)]
            + [(own_ref, f) for f in range(frames)]
            + [(after_ref, f) for f in range(after_count)]
        )
        turn_frame = pl.program_id(0)

        @pl.when((turn_frame == 0) & (pl.program_id(1) == 0))
        def _():
            for at, (ref, f) in enumerate(sources):
                rows = slice(at * row_count, (at + 1) * row_count)
                turned = ref[:, 0, f].reshape(row_count, width).T
                kt_ref[:width, rows] = turned
                kt_ref[width:, rows] = turned
                vx_ref[rows, :width] = ref[:, 1, f].reshape(row_count, width)
                vx_ref[rows, width:] = jnp.ones((row_count, width), vx_ref.dtype)

        q = q_ref[:, 0].reshape(BLOCK_Q, width).astype(jnp.float32) * SCALE_LOG2
        high = q.astype(jnp.bfloat16)
        low = (q - high.astype(jnp.float32)).astype(jnp.bfloat16)
        q = jnp.concatenate((high, low), axis=1)
        position_now = pos_ref[0]

        def rows_of(step):
            start = (turn_frame + step) * row_count
            return pl.ds(pl.multiple_of(start, row_count), row_count)

        def scores(step):
            return jnp.dot(q, kt_ref[:, rows_of(step)], preferred_element_type=jnp.float32)

        top = jnp.full((BLOCK_Q, 1), NEG_FILL, jnp.float32)
        total = jnp.zeros((BLOCK_Q, 2 * width), jnp.float32)
        order = (2, 1, 3, 0, 4)
        ahead = scores(order[0])
        for turn, step in enumerate(order):
            s = ahead
            if turn + 1 < SPAN:
                ahead = scores(order[turn + 1])
            at = turn_frame + step
            absent = ((position_now == 0) & (at < before_count)) | (
                (position_now == QUEUE - 1) & (at >= before_count + frames)
            )
            peak = jnp.max(s, axis=1, keepdims=True)
            peak = jnp.where(absent, NEG_FILL, peak)
            lifted_top = jnp.maximum(top, peak)
            less = jnp.where(absent, -NEG_FILL, lifted_top)
            weights = jnp.exp2(s - less).astype(jnp.bfloat16)
            part = jnp.dot(weights, vx_ref[rows_of(step)], preferred_element_type=jnp.float32)
            total = total * jnp.exp2(top - lifted_top) + part
            top = lifted_top
        result = total[:, :width] / total[:, width:]
        out_ref[:, 0] = result.astype(out_ref.dtype).reshape(groups_block, tok, width)
        token_ref[...] = jnp.zeros_like(token_ref)

    first = asked[0]
    in_specs = [
        pl.BlockSpec((groups_block, 1, tok, width), lambda f, b, pos: (b, first + f, 0, head)),
        pl.BlockSpec(own.shape, lambda f, b, pos: (0, 0, 0, 0, 0)),
        pl.BlockSpec(
            (groups, 2, before_count, tok, width),
            lambda f, b, pos: (0, 0, before_from // before_count, 0, 0),
        ),
        pl.BlockSpec((groups, 2, after_count, tok, width), lambda f, b, pos: (0, 0, 0, 0, 0)),
    ]
    return pl.pallas_call(
        kernel,
        grid_spec=pltpu.PrefetchScalarGridSpec(
            num_scalar_prefetch=1,
            grid=(len(asked), blocks),
            in_specs=in_specs + [corner(e) for e in earlier],
            out_specs=[
                pl.BlockSpec((groups_block, 1, tok, width), lambda f, b, pos: (b, f, 0, 0)),
                pl.BlockSpec(TOKEN, lambda f, b, pos: (0, 0)),
            ],
            scratch_shapes=[
                pltpu.VMEM((2 * width, loaded * row_count), jnp.bfloat16),
                pltpu.VMEM((loaded * row_count, 2 * width), jnp.bfloat16),
            ],
        ),
        out_shape=[
            jax.ShapeDtypeStruct((groups, len(asked), tok, width), query.dtype),
            jax.ShapeDtypeStruct(TOKEN, jnp.float32),
        ],
        compiler_params=pltpu.CompilerParams(vmem_limit_bytes=VMEM),
        cost_estimate=pl.CostEstimate(
            flops=len(asked) * row_count * SPAN * row_count * width * 8,
            bytes_accessed=4 * 1024 * 1024,
            transcendentals=len(asked) * row_count * SPAN * row_count,
        ),
        name="attend",
    )(position, query, own, before, after, *earlier)


def project(side, place, sources, weight_own, weight_pair, partial, gates, *earlier):
    groups, frames, tok, width = sources[1].shape
    steps, _, halves, _, cols_dev = weight_own.shape
    half = groups // CORES
    quarter = groups // 2
    rows = frames * tok
    last = partial is not None

    def kernel(place_ref, mine_ref, left_ref, right_ref, low_ref, high_ref, wo_ref, wp_ref, *rest):
        out_ref, a_ref = rest[-2:]
        x, core = place_ref[0], place_ref[1]

        @pl.when(pl.program_id(0) == 0)
        def _():
            for z in range(steps):
                for part in range(CORES):
                    group = CORES * z + (core if part == 0 else 1 - core)
                    cols = slice((part * half + z) * width, (part * half + z + 1) * width)
                    far = low_ref[group] if CORES * z < quarter else high_ref[group - quarter]
                    a_ref[0:rows, cols] = mine_ref[group].reshape(rows, width)
                    a_ref[rows : 2 * rows, cols] = right_ref[group].reshape(rows, width)
                    a_ref[2 * rows : 3 * rows, cols] = far.reshape(rows, width)
                    a_ref[3 * rows :, cols] = left_ref[group].reshape(rows, width)

        total = jnp.dot(
            a_ref[:, : half * width],
            wo_ref[:, 0, 0].reshape(half * width, cols_dev),
            preferred_element_type=jnp.float32,
        )
        total += jnp.dot(
            a_ref[:, half * width :],
            wp_ref[:, 0, 0].reshape(half * width, cols_dev),
            preferred_element_type=jnp.float32,
        )
        if not last:
            out_ref[0] = total
            return
        total += rest[0][0]
        gates_ref = rest[1]
        for source in range(RING):
            at = lax.rem(x + source, RING)
            for f in range(frames):
                gate = gates_ref[0, pl.ds(at * frames + f, 1), :]
                start = source * rows + f * tok
                slot = at * frames + 1 if f == 0 else lax.rem(at + 1, RING) * frames
                out_ref[slot, 0] = (gate * total[start : start + tok]).astype(out_ref.dtype)

    def whole(array):
        return pl.BlockSpec(array.shape, lambda n, place: (0,) * array.ndim)

    weight = pl.BlockSpec(
        (steps, 1, 1, width, cols_dev), lambda n, place: (0, side, n, 0, 0)
    )
    partial_spec = pl.BlockSpec((1, RING * rows, cols_dev), lambda n, place: (n, 0, 0))
    mine_spec = pl.BlockSpec(sources[1].shape, lambda n, place: (side, 0, 0, 0))
    in_specs = [mine_spec, *map(whole, sources[1:]), weight, weight]
    operands = [*sources, weight_own, weight_pair]
    if last:
        in_specs += [partial_spec, pl.BlockSpec((1,) + gates.shape[1:], lambda n, place: (n, 0, 0))]
        operands += [partial, gates]
        out_spec = pl.BlockSpec((RING * frames, 1, tok, cols_dev), lambda n, place: (0, n, 0, 0))
        out_shape = jax.ShapeDtypeStruct((RING * frames, halves, tok, cols_dev), jnp.bfloat16)
    else:
        out_spec = partial_spec
        out_shape = jax.ShapeDtypeStruct((halves, RING * rows, cols_dev), jnp.float32)
    return pl.pallas_call(
        kernel,
        grid_spec=pltpu.PrefetchScalarGridSpec(
            num_scalar_prefetch=1,
            grid=(halves,),
            in_specs=in_specs + [corner(e) for e in earlier],
            out_specs=out_spec,
            scratch_shapes=[pltpu.VMEM((RING * rows, groups * width), jnp.bfloat16)],
        ),
        out_shape=out_shape,
        compiler_params=pltpu.CompilerParams(vmem_limit_bytes=VMEM),
        cost_estimate=pl.CostEstimate(
            flops=2 * RING * rows * groups * width * halves * cols_dev,
            bytes_accessed=8 * 1024 * 1024,
            transcendentals=0,
        ),
        name="project_last" if last else "project_first",
    )(place, *operands, *earlier)


def add_branch(position, branch, hidden, shifted, entering):
    sources, frames, halves, tok, cols = branch.shape
    width = hidden.shape[-1]

    def kernel(pos_ref, b_ref, hidden_ref, shifted_ref, entering_ref, out_ref):
        def add(base_ref, replaced):
            for half in range(halves):
                for source in range(sources):
                    start = (half * sources + source) * cols
                    at = slice(start, start + cols)
                    value = base_ref[0, :, at].astype(jnp.float32)
                    value += b_ref[source, 0, half].astype(jnp.float32)
                    if replaced:
                        value = jnp.where(
                            pos_ref[0] == 0, entering_ref[:, at].astype(jnp.float32), value
                        )
                    out_ref[0, :, at] = value.astype(out_ref.dtype)

        @pl.when(pl.program_id(0) == 0)
        def _():
            add(shifted_ref, True)

        @pl.when(pl.program_id(0) == 1)
        def _():
            add(hidden_ref, False)

    frame_spec = pl.BlockSpec((1, tok, width), lambda i, pos: (0, 0, 0))
    return pl.pallas_call(
        kernel,
        grid_spec=pltpu.PrefetchScalarGridSpec(
            num_scalar_prefetch=1,
            grid=(frames,),
            in_specs=[
                pl.BlockSpec((sources, 1, halves, tok, cols), lambda i, pos: (0, i, 0, 0, 0)),
                frame_spec,
                frame_spec,
                pl.BlockSpec((tok, width), lambda i, pos: (0, 0)),
            ],
            out_specs=pl.BlockSpec((1, tok, width), lambda i, pos: (i, 0, 0)),
        ),
        out_shape=jax.ShapeDtypeStruct((frames, tok, width), hidden.dtype),
        name="add_branch",
    )(position, branch, hidden, shifted, entering)


def body(hidden, queries, keys, values, out_weight, gate_table, levels, entering):
    frames = queries.shape[0]
    position = lax.axis_index("queue")
    spatial = lax.axis_index("spatial")
    y_low, x = position // RING, position % RING
    core = spatial % CORES
    position_now = position.astype(jnp.int32)[None]
    place = jnp.stack((x, core)).astype(jnp.int32)

    up = [(p, p + 1) for p in range(QUEUE - 1)]
    down = [(p + 1, p) for p in range(QUEUE - 1)]
    ring = [[r * RING + i for i in range(RING)] for r in range(QUEUE // RING)]
    ring_up = [(g[i], g[(i + 1) % RING]) for g in ring for i in range(RING)]
    ring_down = [(g[(i + 1) % RING], g[i]) for g in ring for i in range(RING)]
    swap_low = [(p, (p + RING) % QUEUE) for p in range(QUEUE)]
    swap_core = [(s, s ^ 1) for s in range(SPATIAL)]
    along_y = [
        [(low * RING + i) * SPATIAL + side * (SPATIAL // 2) + r for side in range(2) for low in range(2)]
        for i in range(RING)
        for r in range(SPATIAL // 2)
    ]
    along_z = [
        [side * (SPATIAL // 2) + z * CORES + c for z in range(SPATIAL // 2 // CORES)]
        for side in range(2)
        for c in range(CORES)
    ]

    to_heads = functools.partial(
        lax.all_to_all, axis_name="spatial", split_axis=0, concat_axis=0, tiled=True
    )

    selector = (levels[:, None] == jnp.arange(gate_table.shape[0], dtype=jnp.int32)[None, :]).astype(
        jnp.float32
    )
    gates = jnp.dot(
        selector, gate_table, precision=lax.Precision.HIGHEST, preferred_element_type=jnp.float32
    )
    other_gates = lax.ppermute(gates, "queue", swap_low)
    gates = jnp.where(y_low == 0, jnp.stack((gates, other_gates)), jnp.stack((other_gates, gates)))
    count = RING * frames
    is_last = (jnp.arange(count, dtype=jnp.int32) == count - 1)[None, :, None] & (y_low == 1)
    gates = jnp.where(
        is_last,
        gates[:, count - 1 : count],
        lax.dynamic_slice_in_dim(gates, y_low * count, count, axis=1),
    )

    kv0, kv1, query = pack(queries, keys, values)
    kv0 = to_heads(kv0)
    kv0_before, kv0_after = lax.ppermute(kv0, "queue", up), lax.ppermute(kv0, "queue", down)
    kv1 = to_heads(hold(kv1, kv0, gates))
    query = to_heads(hold(query, kv1, kv0_before, kv0_after))
    kv1 = hold(kv1, query)
    kv1_before, kv1_after = lax.ppermute(kv1, "queue", up), lax.ppermute(kv1, "queue", down)

    weight = lax.all_gather(out_weight, ("queue", "spatial"), axis_index_groups=along_y, axis=0)
    weight = hold(weight, kv0)
    weight = lax.all_gather(weight, "spatial", axis_index_groups=along_z, axis=0)
    weight = weight.reshape(-1, 2, 2, *out_weight.shape)

    cross = [(RING - 1, QUEUE - 1)]
    both, token = attend(None, position_now, query, 0, kv0, kv0_before, kv0_after)
    first_crossing = lax.ppermute(both[:, 1:], "queue", cross)
    shifted = lax.ppermute(last_frame(hidden, token), "queue", up)
    head1 = (position_now, query, 1, kv1, kv1_before, kv1_after)
    odd, token = attend(1, *head1, token)
    odd_crossing = lax.ppermute(odd, "queue", cross)
    weight_own = hold(weight, token)
    weight_pair = lax.ppermute(weight_own, "spatial", swap_core)
    even, _ = attend(0, *head1, token, first_crossing)
    mine = to_heads(
        assemble(position_now, both, first_crossing, even, odd, odd_crossing, shifted)
    )

    def spread(side):
        half = SPATIAL // 2
        part = mine[side * half : (side + 1) * half]
        left = lax.ppermute(part, "queue", ring_up)
        right = lax.ppermute(part, "queue", ring_down)
        far_low = lax.ppermute(left[: half // 2], "queue", ring_up)
        far_high = lax.ppermute(right[half // 2 :], "queue", ring_down)
        return mine, left, right, far_low, far_high

    first_sources = spread(0)
    second_sources = spread(1)
    partial = project(0, place, first_sources, weight_own, weight_pair, None, None)
    branch = project(1, place, second_sources, weight_own, weight_pair, partial, gates)
    branch = lax.all_to_all(
        branch, "queue", split_axis=0, concat_axis=0, axis_index_groups=ring, tiled=True
    )
    branch = branch.reshape(RING, frames, *branch.shape[1:])
    return add_branch(position_now, branch, hidden, shifted, entering)


def solution(mesh):
    return jax.shard_map(
        body,
        mesh=mesh,
        in_specs=(
            P("queue", "spatial", None),
            P("queue", "spatial", None),
            P("queue", "spatial", None),
            P("queue", "spatial", None),
            P("spatial", "queue"),
            P(None, "queue"),
            P(),
            P("spatial", None),
        ),
        out_specs=P("queue", "spatial", None),
        check_vma=False,
    )
```

```python
import functools

import jax
import jax.numpy as jnp
from jax import lax
from jax.experimental import pallas as pl
from jax.experimental.pallas import tpu as pltpu
from jax.sharding import PartitionSpec as P

HEADS = 32
HD = 128
WMAX = 2
NEG_FILL = -1e30
SCALE_LOG2 = (HD ** -0.5) * 1.4426950408889634
BLOCK_Q = 512
VMEM = 48 * 1024 * 1024
QUEUE = 8
RING = 4
SPATIAL = 16
CORES = 2
PACK = 4
SPAN = 2 * WMAX + 1
ANY = pl.BlockSpec(memory_space=pl.ANY)
TOKEN = (8, 128)


def corner(array):
    rows = 8 if array.dtype == jnp.float32 else 16
    block = (1,) * (array.ndim - 2) + (rows, 128)
    return pl.BlockSpec(block, lambda *at: (0,) * array.ndim)


def pack(queries, keys, values):
    frames, tok, width = keys.shape
    group = width // SPATIAL
    piece = width // PACK
    count = SPATIAL // PACK

    def kernel(q_ref, k_ref, v_ref, kv0_ref, kv1_ref, out_ref):
        for i in range(count):
            for head, kv_ref in enumerate((kv0_ref, kv1_ref)):
                cols = slice(i * group + head * HD, i * group + (head + 1) * HD)
                kv_ref[i, 0] = k_ref[:, :, cols]
                kv_ref[i, 1] = v_ref[:, :, cols]
            out_ref[i] = q_ref[:, :, i * group : (i + 1) * group]

    spec = pl.BlockSpec((frames, tok, piece), lambda s: (0, 0, s))
    kv_spec = pl.BlockSpec((count, 2, frames, tok, HD), lambda s: (s, 0, 0, 0, 0))
    kv_shape = jax.ShapeDtypeStruct((SPATIAL, 2, frames, tok, HD), keys.dtype)
    return pl.pallas_call(
        kernel,
        grid=(PACK,),
        in_specs=[spec] * 3,
        out_specs=[kv_spec, kv_spec, pl.BlockSpec((count, frames, tok, group), lambda s: (s, 0, 0, 0))],
        out_shape=[
            kv_shape,
            kv_shape,
            jax.ShapeDtypeStruct((SPATIAL, frames, tok, group), queries.dtype),
        ],
        name="pack",
    )(queries, keys, values)


def last_frame(hidden, *earlier):
    frames, tok, width = hidden.shape

    def kernel(hidden_ref, *rest):
        rest[-1][...] = hidden_ref[...]

    return pl.pallas_call(
        kernel,
        grid=(1,),
        in_specs=[pl.BlockSpec((1, tok, width), lambda i: (frames - 1, 0, 0))]
        + [corner(e) for e in earlier],
        out_specs=pl.BlockSpec((1, tok, width), lambda i: (0, 0, 0)),
        out_shape=jax.ShapeDtypeStruct((1, tok, width), hidden.dtype),
        name="last_frame",
    )(hidden, *earlier)


def hold(array, *earlier):
    def kernel(*refs):
        pass

    return pl.pallas_call(
        kernel,
        grid=(1,),
        in_specs=[ANY] + [corner(e) for e in earlier],
        out_specs=ANY,
        out_shape=jax.ShapeDtypeStruct(array.shape, array.dtype),
        input_output_aliases={0: 0},
        name="hold",
    )(array, *earlier)


def attend(frame, position, query, head, own, before, after, *earlier):
    groups, frames, tok, both = query.shape
    width = own.shape[-1]
    row_count = groups * tok
    groups_block = BLOCK_Q // tok
    blocks = row_count // BLOCK_Q
    asked = range(frames) if frame is None else (frame,)
    before_from = min(asked)
    before_count = frames - before_from
    after_count = max(asked) + 1
    loaded = before_count + frames + after_count

    def kernel(pos_ref, q_ref, own_ref, before_ref, after_ref, *rest):
        out_ref, token_ref, kt_ref, vx_ref = rest[-4:]
        sources = (
            [(before_ref, f) for f in range(before_count)]
            + [(own_ref, f) for f in range(frames)]
            + [(after_ref, f) for f in range(after_count)]
        )
        turn_frame = pl.program_id(0)

        @pl.when((turn_frame == 0) & (pl.program_id(1) == 0))
        def _():
            for at, (ref, f) in enumerate(sources):
                rows = slice(at * row_count, (at + 1) * row_count)
                turned = ref[:, 0, f].reshape(row_count, width).T
                kt_ref[:width, rows] = turned
                kt_ref[width:, rows] = turned
                vx_ref[rows, :width] = ref[:, 1, f].reshape(row_count, width)
                vx_ref[rows, width:] = jnp.ones((row_count, width), vx_ref.dtype)

        q = q_ref[:, 0].reshape(BLOCK_Q, width).astype(jnp.float32) * SCALE_LOG2
        high = q.astype(jnp.bfloat16)
        low = (q - high.astype(jnp.float32)).astype(jnp.bfloat16)
        q = jnp.concatenate((high, low), axis=1)
        position_now = pos_ref[0]

        def rows_of(step):
            start = (turn_frame + step) * row_count
            return pl.ds(pl.multiple_of(start, row_count), row_count)

        def scores(step):
            return jnp.dot(q, kt_ref[:, rows_of(step)], preferred_element_type=jnp.float32)

        top = jnp.full((BLOCK_Q, 1), NEG_FILL, jnp.float32)
        total = jnp.zeros((BLOCK_Q, 2 * width), jnp.float32)
        order = (2, 1, 3, 0, 4)
        ahead = scores(order[0])
        for turn, step in enumerate(order):
            s = ahead
            if turn + 1 < SPAN:
                ahead = scores(order[turn + 1])
            at = turn_frame + step
            absent = ((position_now == 0) & (at < before_count)) | (
                (position_now == QUEUE - 1) & (at >= before_count + frames)
            )
            peak = jnp.max(s, axis=1, keepdims=True)
            peak = jnp.where(absent, NEG_FILL, peak)
            lifted_top = jnp.maximum(top, peak)
            less = jnp.where(absent, -NEG_FILL, lifted_top)
            weights = jnp.exp2(s - less).astype(jnp.bfloat16)
            part = jnp.dot(weights, vx_ref[rows_of(step)], preferred_element_type=jnp.float32)
            total = total * jnp.exp2(top - lifted_top) + part
            top = lifted_top
        result = total[:, :width] / total[:, width:]
        out_ref[:, 0] = result.astype(out_ref.dtype).reshape(groups_block, tok, width)
        token_ref[...] = jnp.zeros_like(token_ref)

    first = asked[0]
    in_specs = [
        pl.BlockSpec((groups_block, 1, tok, width), lambda f, b, pos: (b, first + f, 0, head)),
        pl.BlockSpec(own.shape, lambda f, b, pos: (0, 0, 0, 0, 0)),
        pl.BlockSpec(
            (groups, 2, before_count, tok, width),
            lambda f, b, pos: (0, 0, before_from // before_count, 0, 0),
        ),
        pl.BlockSpec((groups, 2, after_count, tok, width), lambda f, b, pos: (0, 0, 0, 0, 0)),
    ]
    return pl.pallas_call(
        kernel,
        grid_spec=pltpu.PrefetchScalarGridSpec(
            num_scalar_prefetch=1,
            grid=(len(asked), blocks),
            in_specs=in_specs + [corner(e) for e in earlier],
            out_specs=[
                pl.BlockSpec((groups_block, 1, tok, width), lambda f, b, pos: (b, f, 0, 0)),
                pl.BlockSpec(TOKEN, lambda f, b, pos: (0, 0)),
            ],
            scratch_shapes=[
                pltpu.VMEM((2 * width, loaded * row_count), jnp.bfloat16),
                pltpu.VMEM((loaded * row_count, 2 * width), jnp.bfloat16),
            ],
        ),
        out_shape=[
            jax.ShapeDtypeStruct((groups, len(asked), tok, width), query.dtype),
            jax.ShapeDtypeStruct(TOKEN, jnp.float32),
        ],
        compiler_params=pltpu.CompilerParams(vmem_limit_bytes=VMEM),
        cost_estimate=pl.CostEstimate(
            flops=len(asked) * row_count * SPAN * row_count * width * 8,
            bytes_accessed=4 * 1024 * 1024,
            transcendentals=len(asked) * row_count * SPAN * row_count,
        ),
        name="attend",
    )(position, query, own, before, after, *earlier)


def project(head, place, sources, weight_own, weight_pair, partial, gates, *earlier):
    mine = sources[0]
    groups, frames, tok, width = mine.shape
    steps, sides, halves, rows_dev, cols_dev = weight_own.shape
    half = steps * sides
    rows = frames * tok
    last = partial is not None

    def kernel(place_ref, mine_ref, left_ref, right_ref, low_ref, high_ref, wo_ref, wp_ref, *rest):
        out_ref, a_ref = rest[-2:]
        x, core = place_ref[0], place_ref[1]

        @pl.when(pl.program_id(0) == 0)
        def _():
            for i in range(half):
                z, side = i // sides, i % sides
                for part in range(CORES):
                    group = side * half + CORES * z + (core if part == 0 else 1 - core)
                    cols = slice((part * half + i) * width, (part * half + i + 1) * width)
                    far = high_ref[group - half] if side else low_ref[group]
                    a_ref[0:rows, cols] = mine_ref[group].reshape(rows, width)
                    a_ref[rows : 2 * rows, cols] = right_ref[group].reshape(rows, width)
                    a_ref[2 * rows : 3 * rows, cols] = far.reshape(rows, width)
                    a_ref[3 * rows :, cols] = left_ref[group].reshape(rows, width)

        total = jnp.dot(
            a_ref[:, : half * width],
            wo_ref[:, :, 0].reshape(half * width, cols_dev),
            preferred_element_type=jnp.float32,
        )
        total += jnp.dot(
            a_ref[:, half * width :],
            wp_ref[:, :, 0].reshape(half * width, cols_dev),
            preferred_element_type=jnp.float32,
        )
        if not last:
            out_ref[0] = total
            return
        total += rest[0][0]
        gates_ref = rest[1]
        for source in range(RING):
            at = lax.rem(x + source, RING)
            for f in range(frames):
                gate = gates_ref[0, pl.ds(at * frames + f, 1), :]
                start = source * rows + f * tok
                slot = at * frames + 1 if f == 0 else lax.rem(at + 1, RING) * frames
                out_ref[slot, 0] = (gate * total[start : start + tok]).astype(out_ref.dtype)

    def whole(array):
        return pl.BlockSpec(array.shape, lambda n, place: (0,) * array.ndim)

    weight = pl.BlockSpec(
        (steps, sides, 1, width, cols_dev), lambda n, place: (0, 0, n, head, 0)
    )
    partial_spec = pl.BlockSpec((1, RING * rows, cols_dev), lambda n, place: (n, 0, 0))
    in_specs = [*map(whole, sources), weight, weight]
    operands = [*sources, weight_own, weight_pair]
    if last:
        in_specs += [partial_spec, pl.BlockSpec((1,) + gates.shape[1:], lambda n, place: (n, 0, 0))]
        operands += [partial, gates]
        out_spec = pl.BlockSpec((RING * frames, 1, tok, cols_dev), lambda n, place: (0, n, 0, 0))
        out_shape = jax.ShapeDtypeStruct((RING * frames, halves, tok, cols_dev), jnp.bfloat16)
    else:
        out_spec = partial_spec
        out_shape = jax.ShapeDtypeStruct((halves, RING * rows, cols_dev), jnp.float32)
    return pl.pallas_call(
        kernel,
        grid_spec=pltpu.PrefetchScalarGridSpec(
            num_scalar_prefetch=1,
            grid=(halves,),
            in_specs=in_specs + [corner(e) for e in earlier],
            out_specs=out_spec,
            scratch_shapes=[pltpu.VMEM((RING * rows, groups * width), jnp.bfloat16)],
        ),
        out_shape=out_shape,
        compiler_params=pltpu.CompilerParams(vmem_limit_bytes=VMEM),
        cost_estimate=pl.CostEstimate(
            flops=2 * RING * rows * groups * width * halves * cols_dev,
            bytes_accessed=8 * 1024 * 1024,
            transcendentals=0,
        ),
        name="project_last" if last else "project_first",
    )(place, *operands, *earlier)


def add_branch(position, branch, hidden, shifted, entering):
    sources, frames, halves, tok, cols = branch.shape
    width = hidden.shape[-1]

    def kernel(pos_ref, b_ref, hidden_ref, shifted_ref, entering_ref, out_ref):
        def add(base_ref, replaced):
            for half in range(halves):
                for source in range(sources):
                    start = (half * sources + source) * cols
                    at = slice(start, start + cols)
                    value = base_ref[0, :, at].astype(jnp.float32)
                    value += b_ref[source, 0, half].astype(jnp.float32)
                    if replaced:
                        value = jnp.where(
                            pos_ref[0] == 0, entering_ref[:, at].astype(jnp.float32), value
                        )
                    out_ref[0, :, at] = value.astype(out_ref.dtype)

        @pl.when(pl.program_id(0) == 0)
        def _():
            add(shifted_ref, True)

        @pl.when(pl.program_id(0) == 1)
        def _():
            add(hidden_ref, False)

    frame_spec = pl.BlockSpec((1, tok, width), lambda i, pos: (0, 0, 0))
    return pl.pallas_call(
        kernel,
        grid_spec=pltpu.PrefetchScalarGridSpec(
            num_scalar_prefetch=1,
            grid=(frames,),
            in_specs=[
                pl.BlockSpec((sources, 1, halves, tok, cols), lambda i, pos: (0, i, 0, 0, 0)),
                frame_spec,
                frame_spec,
                pl.BlockSpec((tok, width), lambda i, pos: (0, 0)),
            ],
            out_specs=pl.BlockSpec((1, tok, width), lambda i, pos: (i, 0, 0)),
        ),
        out_shape=jax.ShapeDtypeStruct((frames, tok, width), hidden.dtype),
        name="add_branch",
    )(position, branch, hidden, shifted, entering)


def body(hidden, queries, keys, values, out_weight, gate_table, levels, entering):
    frames = queries.shape[0]
    position = lax.axis_index("queue")
    spatial = lax.axis_index("spatial")
    y_low, x = position // RING, position % RING
    core = spatial % CORES
    position_now = position.astype(jnp.int32)[None]
    place = jnp.stack((x, core)).astype(jnp.int32)

    up = [(p, p + 1) for p in range(QUEUE - 1)]
    down = [(p + 1, p) for p in range(QUEUE - 1)]
    ring = [[r * RING + i for i in range(RING)] for r in range(QUEUE // RING)]
    ring_up = [(g[i], g[(i + 1) % RING]) for g in ring for i in range(RING)]
    ring_down = [(g[(i + 1) % RING], g[i]) for g in ring for i in range(RING)]
    swap_low = [(p, (p + RING) % QUEUE) for p in range(QUEUE)]
    swap_core = [(s, s ^ 1) for s in range(SPATIAL)]
    along_y = [
        [(low * RING + i) * SPATIAL + side * (SPATIAL // 2) + r for side in range(2) for low in range(2)]
        for i in range(RING)
        for r in range(SPATIAL // 2)
    ]
    along_z = [
        [side * (SPATIAL // 2) + z * CORES + c for z in range(SPATIAL // 2 // CORES)]
        for side in range(2)
        for c in range(CORES)
    ]

    to_heads = functools.partial(
        lax.all_to_all, axis_name="spatial", split_axis=0, concat_axis=0, tiled=True
    )

    selector = (levels[:, None] == jnp.arange(gate_table.shape[0], dtype=jnp.int32)[None, :]).astype(
        jnp.float32
    )
    gates = jnp.dot(
        selector, gate_table, precision=lax.Precision.HIGHEST, preferred_element_type=jnp.float32
    )
    other_gates = lax.ppermute(gates, "queue", swap_low)
    gates = jnp.where(y_low == 0, jnp.stack((gates, other_gates)), jnp.stack((other_gates, gates)))
    count = RING * frames
    is_last = (jnp.arange(count, dtype=jnp.int32) == count - 1)[None, :, None] & (y_low == 1)
    gates = jnp.where(
        is_last,
        gates[:, count - 1 : count],
        lax.dynamic_slice_in_dim(gates, y_low * count, count, axis=1),
    )

    kv0, kv1, query = pack(queries, keys, values)
    kv0 = to_heads(kv0)
    kv1 = to_heads(hold(kv1, kv0, gates))
    kv0 = hold(kv0, kv1)
    kv0_before, kv0_after = lax.ppermute(kv0, "queue", up), lax.ppermute(kv0, "queue", down)
    query = to_heads(hold(query, kv1))
    kv1 = hold(kv1, query)
    kv1_before, kv1_after = lax.ppermute(kv1, "queue", up), lax.ppermute(kv1, "queue", down)

    weight = lax.all_gather(out_weight, ("queue", "spatial"), axis_index_groups=along_y, axis=0)
    weight = hold(weight, query)
    weight = lax.all_gather(weight, "spatial", axis_index_groups=along_z, axis=0)
    weight = weight.reshape(-1, 2, 2, *out_weight.shape)

    cross = [(RING - 1, QUEUE - 1)]

    def returned(even, odd, crossing):
        odd = jnp.where(position == QUEUE - 1, crossing, odd)
        return to_heads(jnp.concatenate((even, odd), axis=1))

    def spread(mine):
        left = lax.ppermute(mine, "queue", ring_up)
        right = lax.ppermute(mine, "queue", ring_down)
        far_low = lax.ppermute(left[: SPATIAL // 2], "queue", ring_up)
        far_high = lax.ppermute(right[SPATIAL // 2 :], "queue", ring_down)
        return mine, left, right, far_low, far_high

    head0 = (position_now, query, 0, kv0, kv0_before, kv0_after)
    head1 = (position_now, query, 1, kv1, kv1_before, kv1_after)
    odd0, token = attend(1, *head0)
    odd0_crossing = lax.ppermute(odd0, "queue", cross)
    even0, token = attend(0, *head0, token)
    first = returned(even0, odd0, odd0_crossing)
    odd1, token = attend(1, *head1, token, odd0_crossing)
    odd1_crossing = lax.ppermute(odd1, "queue", cross)
    shifted = lax.ppermute(last_frame(hidden, kv1_before, kv1_after), "queue", up)
    weight_own = hold(weight, token)
    weight_pair = lax.ppermute(weight_own, "spatial", swap_core)
    even1, token = attend(0, *head1, token)
    first_sources = spread(hold(first, token, shifted))
    second_sources = spread(returned(even1, odd1, odd1_crossing))

    partial = project(0, place, first_sources, weight_own, weight_pair, None, None)
    branch = project(1, place, second_sources, weight_own, weight_pair, partial, gates)
    branch = lax.all_to_all(
        branch, "queue", split_axis=0, concat_axis=0, axis_index_groups=ring, tiled=True
    )
    branch = branch.reshape(RING, frames, *branch.shape[1:])
    return add_branch(position_now, branch, hidden, shifted, entering)


def solution(mesh):
    return jax.shard_map(
        body,
        mesh=mesh,
        in_specs=(
            P("queue", "spatial", None),
            P("queue", "spatial", None),
            P("queue", "spatial", None),
            P("queue", "spatial", None),
            P("spatial", "queue"),
            P(None, "queue"),
            P(),
            P("spatial", None),
        ),
        out_specs=P("queue", "spatial", None),
        check_vma=False,
    )
```

```python
import functools

import jax
import jax.numpy as jnp
from jax import lax
from jax.experimental import pallas as pl
from jax.experimental.pallas import tpu as pltpu
from jax.sharding import PartitionSpec as P

HEADS = 32
HD = 128
WMAX = 2
NEG_FILL = -1e30
SCALE_LOG2 = (HD ** -0.5) * 1.4426950408889634
BLOCK_Q = 512
VMEM = 28 * 1024 * 1024
SMALL = pltpu.CompilerParams(vmem_limit_bytes=1024 * 1024)
MEDIUM = pltpu.CompilerParams(vmem_limit_bytes=12 * 1024 * 1024)
QUEUE = 8
RING = 4
SPATIAL = 16
CORES = 2
PACK = 4
SPAN = 2 * WMAX + 1
ANY = pl.BlockSpec(memory_space=pl.ANY)
TOKEN = (8, 128)


def corner(array):
    rows = 8 if array.dtype == jnp.float32 else 16
    block = (1,) * (array.ndim - 2) + (rows, 128)
    return pl.BlockSpec(block, lambda *at: (0,) * array.ndim)


def pack(queries, keys, values):
    frames, tok, width = keys.shape
    group = width // SPATIAL
    piece = width // PACK
    count = SPATIAL // PACK

    def kernel(q_ref, k_ref, v_ref, kv0_ref, kv1_ref, out_ref):
        for i in range(count):
            for head, kv_ref in enumerate((kv0_ref, kv1_ref)):
                cols = slice(i * group + head * HD, i * group + (head + 1) * HD)
                kv_ref[i, 0] = k_ref[:, :, cols]
                kv_ref[i, 1] = v_ref[:, :, cols]
            out_ref[i] = q_ref[:, :, i * group : (i + 1) * group]

    spec = pl.BlockSpec((frames, tok, piece), lambda s: (0, 0, s))
    kv_spec = pl.BlockSpec((count, 2, frames, tok, HD), lambda s: (s, 0, 0, 0, 0))
    kv_shape = jax.ShapeDtypeStruct((SPATIAL, 2, frames, tok, HD), keys.dtype)
    return pl.pallas_call(
        kernel,
        grid=(PACK,),
        in_specs=[spec] * 3,
        out_specs=[kv_spec, kv_spec, pl.BlockSpec((count, frames, tok, group), lambda s: (s, 0, 0, 0))],
        out_shape=[
            kv_shape,
            kv_shape,
            jax.ShapeDtypeStruct((SPATIAL, frames, tok, group), queries.dtype),
        ],
        compiler_params=MEDIUM,
        name="pack",
    )(queries, keys, values)


def hold(array, *earlier):
    def kernel(*refs):
        pass

    return pl.pallas_call(
        kernel,
        grid=(1,),
        in_specs=[ANY] + [corner(e) for e in earlier],
        out_specs=ANY,
        out_shape=jax.ShapeDtypeStruct(array.shape, array.dtype),
        input_output_aliases={0: 0},
        compiler_params=SMALL,
        name="hold",
    )(array, *earlier)


def attend(frame, position, query, head, own, before, after, *earlier):
    groups, frames, tok, both = query.shape
    width = own.shape[-1]
    row_count = groups * tok
    groups_block = BLOCK_Q // tok
    blocks = row_count // BLOCK_Q
    asked = range(frames) if frame is None else (frame,)
    before_from = min(asked)
    before_count = frames - before_from
    after_count = max(asked) + 1
    loaded = before_count + frames + after_count

    def kernel(pos_ref, q_ref, own_ref, before_ref, after_ref, *rest):
        out_ref, token_ref, kt_ref, vx_ref = rest[-4:]
        sources = (
            [(before_ref, f) for f in range(before_count)]
            + [(own_ref, f) for f in range(frames)]
            + [(after_ref, f) for f in range(after_count)]
        )
        turn_frame = pl.program_id(0)

        @pl.when((turn_frame == 0) & (pl.program_id(1) == 0))
        def _():
            for at, (ref, f) in enumerate(sources):
                rows = slice(at * row_count, (at + 1) * row_count)
                turned = ref[:, 0, f].reshape(row_count, width).T
                kt_ref[:width, rows] = turned
                kt_ref[width:, rows] = turned
                vx_ref[rows, :width] = ref[:, 1, f].reshape(row_count, width)
                vx_ref[rows, width:] = jnp.ones((row_count, width), vx_ref.dtype)

        q = q_ref[:, 0].reshape(BLOCK_Q, width).astype(jnp.float32) * SCALE_LOG2
        high = q.astype(jnp.bfloat16)
        low = (q - high.astype(jnp.float32)).astype(jnp.bfloat16)
        q = jnp.concatenate((high, low), axis=1)
        position_now = pos_ref[0]

        def rows_of(step):
            start = (turn_frame + step) * row_count
            return pl.ds(pl.multiple_of(start, row_count), row_count)

        def scores(step):
            return jnp.dot(q, kt_ref[:, rows_of(step)], preferred_element_type=jnp.float32)

        top = jnp.full((BLOCK_Q, 1), NEG_FILL, jnp.float32)
        total = jnp.zeros((BLOCK_Q, 2 * width), jnp.float32)
        order = (2, 1, 3, 0, 4)
        ahead = scores(order[0])
        for turn, step in enumerate(order):
            s = ahead
            if turn + 1 < SPAN:
                ahead = scores(order[turn + 1])
            at = turn_frame + step
            absent = ((position_now == 0) & (at < before_count)) | (
                (position_now == QUEUE - 1) & (at >= before_count + frames)
            )
            peak = jnp.max(s, axis=1, keepdims=True)
            peak = jnp.where(absent, NEG_FILL, peak)
            lifted_top = jnp.maximum(top, peak)
            less = jnp.where(absent, -NEG_FILL, lifted_top)
            weights = jnp.exp2(s - less).astype(jnp.bfloat16)
            part = jnp.dot(weights, vx_ref[rows_of(step)], preferred_element_type=jnp.float32)
            total = total * jnp.exp2(top - lifted_top) + part
            top = lifted_top
        result = total[:, :width] / total[:, width:]
        out_ref[:, 0] = result.astype(out_ref.dtype).reshape(groups_block, tok, width)
        token_ref[...] = jnp.zeros_like(token_ref)

    first = asked[0]
    in_specs = [
        pl.BlockSpec((groups_block, 1, tok, width), lambda f, b, pos: (b, first + f, 0, head)),
        pl.BlockSpec(own.shape, lambda f, b, pos: (0, 0, 0, 0, 0)),
        pl.BlockSpec(
            (groups, 2, before_count, tok, width),
            lambda f, b, pos: (0, 0, before_from // before_count, 0, 0),
        ),
        pl.BlockSpec((groups, 2, after_count, tok, width), lambda f, b, pos: (0, 0, 0, 0, 0)),
    ]
    return pl.pallas_call(
        kernel,
        grid_spec=pltpu.PrefetchScalarGridSpec(
            num_scalar_prefetch=1,
            grid=(len(asked), blocks),
            in_specs=in_specs + [corner(e) for e in earlier],
            out_specs=[
                pl.BlockSpec((groups_block, 1, tok, width), lambda f, b, pos: (b, f, 0, 0)),
                pl.BlockSpec(TOKEN, lambda f, b, pos: (0, 0)),
            ],
            scratch_shapes=[
                pltpu.VMEM((2 * width, loaded * row_count), jnp.bfloat16),
                pltpu.VMEM((loaded * row_count, 2 * width), jnp.bfloat16),
            ],
        ),
        out_shape=[
            jax.ShapeDtypeStruct((groups, len(asked), tok, width), query.dtype),
            jax.ShapeDtypeStruct(TOKEN, jnp.float32),
        ],
        compiler_params=pltpu.CompilerParams(vmem_limit_bytes=VMEM),
        cost_estimate=pl.CostEstimate(
            flops=len(asked) * row_count * SPAN * row_count * width * 8,
            bytes_accessed=4 * 1024 * 1024,
            transcendentals=len(asked) * row_count * SPAN * row_count,
        ),
        name="attend",
    )(position, query, own, before, after, *earlier)


def project(head, place, sources, weight_own, weight_pair, partial, gates, *earlier):
    mine = sources[0]
    groups, frames, tok, width = mine.shape
    steps, sides, halves, rows_dev, cols_dev = weight_own.shape
    half = steps * sides
    rows = frames * tok
    last = partial is not None

    def kernel(place_ref, mine_ref, left_ref, right_ref, low_ref, high_ref, wo_ref, wp_ref, *rest):
        out_ref, a_ref = rest[-2:]
        x, core = place_ref[0], place_ref[1]

        @pl.when(pl.program_id(0) == 0)
        def _():
            for i in range(half):
                z, side = i // sides, i % sides
                for part in range(CORES):
                    group = side * half + CORES * z + (core if part == 0 else 1 - core)
                    cols = slice((part * half + i) * width, (part * half + i + 1) * width)
                    far = high_ref[group - half] if side else low_ref[group]
                    a_ref[0:rows, cols] = mine_ref[group].reshape(rows, width)
                    a_ref[rows : 2 * rows, cols] = right_ref[group].reshape(rows, width)
                    a_ref[2 * rows : 3 * rows, cols] = far.reshape(rows, width)
                    a_ref[3 * rows :, cols] = left_ref[group].reshape(rows, width)

        total = jnp.dot(
            a_ref[:, : half * width],
            wo_ref[:, :, 0].reshape(half * width, cols_dev),
            preferred_element_type=jnp.float32,
        )
        total += jnp.dot(
            a_ref[:, half * width :],
            wp_ref[:, :, 0].reshape(half * width, cols_dev),
            preferred_element_type=jnp.float32,
        )
        if not last:
            out_ref[0] = total
            return
        total += rest[0][0]
        gates_ref = rest[1]
        for source in range(RING):
            at = lax.rem(x + source, RING)
            for f in range(frames):
                gate = gates_ref[0, pl.ds(at * frames + f, 1), :]
                start = source * rows + f * tok
                slot = at * frames + 1 if f == 0 else lax.rem(at + 1, RING) * frames
                out_ref[slot, 0] = (gate * total[start : start + tok]).astype(out_ref.dtype)

    def whole(array):
        return pl.BlockSpec(array.shape, lambda n, place: (0,) * array.ndim)

    weight = pl.BlockSpec(
        (steps, sides, 1, width, cols_dev), lambda n, place: (0, 0, n, head, 0)
    )
    partial_spec = pl.BlockSpec((1, RING * rows, cols_dev), lambda n, place: (n, 0, 0))
    in_specs = [*map(whole, sources), weight, weight]
    operands = [*sources, weight_own, weight_pair]
    if last:
        in_specs += [partial_spec, pl.BlockSpec((1,) + gates.shape[1:], lambda n, place: (n, 0, 0))]
        operands += [partial, gates]
        out_spec = pl.BlockSpec((RING * frames, 1, tok, cols_dev), lambda n, place: (0, n, 0, 0))
        out_shape = jax.ShapeDtypeStruct((RING * frames, halves, tok, cols_dev), jnp.bfloat16)
    else:
        out_spec = partial_spec
        out_shape = jax.ShapeDtypeStruct((halves, RING * rows, cols_dev), jnp.float32)
    return pl.pallas_call(
        kernel,
        grid_spec=pltpu.PrefetchScalarGridSpec(
            num_scalar_prefetch=1,
            grid=(halves,),
            in_specs=in_specs + [corner(e) for e in earlier],
            out_specs=out_spec,
            scratch_shapes=[pltpu.VMEM((RING * rows, groups * width), jnp.bfloat16)],
        ),
        out_shape=out_shape,
        compiler_params=pltpu.CompilerParams(vmem_limit_bytes=VMEM),
        cost_estimate=pl.CostEstimate(
            flops=2 * RING * rows * groups * width * halves * cols_dev,
            bytes_accessed=8 * 1024 * 1024,
            transcendentals=0,
        ),
        name="project_last" if last else "project_first",
    )(place, *operands, *earlier)


def add_branch(position, branch, hidden, shifted, entering):
    sources, frames, halves, tok, cols = branch.shape
    width = hidden.shape[-1]

    def kernel(pos_ref, b_ref, hidden_ref, shifted_ref, entering_ref, out_ref):
        def add(base_ref, replaced):
            for half in range(halves):
                for source in range(sources):
                    start = (half * sources + source) * cols
                    at = slice(start, start + cols)
                    value = base_ref[0, :, at].astype(jnp.float32)
                    value += b_ref[source, 0, half].astype(jnp.float32)
                    if replaced:
                        value = jnp.where(
                            pos_ref[0] == 0, entering_ref[:, at].astype(jnp.float32), value
                        )
                    out_ref[0, :, at] = value.astype(out_ref.dtype)

        @pl.when(pl.program_id(0) == 0)
        def _():
            add(shifted_ref, True)

        @pl.when(pl.program_id(0) == 1)
        def _():
            add(hidden_ref, False)

    frame_spec = pl.BlockSpec((1, tok, width), lambda i, pos: (0, 0, 0))
    return pl.pallas_call(
        kernel,
        grid_spec=pltpu.PrefetchScalarGridSpec(
            num_scalar_prefetch=1,
            grid=(frames,),
            in_specs=[
                pl.BlockSpec((sources, 1, halves, tok, cols), lambda i, pos: (0, i, 0, 0, 0)),
                frame_spec,
                frame_spec,
                pl.BlockSpec((tok, width), lambda i, pos: (0, 0)),
            ],
            out_specs=pl.BlockSpec((1, tok, width), lambda i, pos: (i, 0, 0)),
        ),
        out_shape=jax.ShapeDtypeStruct((frames, tok, width), hidden.dtype),
        compiler_params=MEDIUM,
        name="add_branch",
    )(position, branch, hidden, shifted, entering)


def body(hidden, queries, keys, values, out_weight, gate_table, levels, entering):
    frames = queries.shape[0]
    position = lax.axis_index("queue")
    spatial = lax.axis_index("spatial")
    y_low, x = position // RING, position % RING
    core = spatial % CORES
    position_now = position.astype(jnp.int32)[None]
    place = jnp.stack((x, core)).astype(jnp.int32)

    up = [(p, p + 1) for p in range(QUEUE - 1)]
    down = [(p + 1, p) for p in range(QUEUE - 1)]
    ring = [[r * RING + i for i in range(RING)] for r in range(QUEUE // RING)]
    ring_up = [(g[i], g[(i + 1) % RING]) for g in ring for i in range(RING)]
    ring_down = [(g[(i + 1) % RING], g[i]) for g in ring for i in range(RING)]
    swap_low = [(p, (p + RING) % QUEUE) for p in range(QUEUE)]
    swap_core = [(s, s ^ 1) for s in range(SPATIAL)]
    along_y = [
        [(low * RING + i) * SPATIAL + side * (SPATIAL // 2) + r for side in range(2) for low in range(2)]
        for i in range(RING)
        for r in range(SPATIAL // 2)
    ]
    along_z = [
        [side * (SPATIAL // 2) + z * CORES + c for z in range(SPATIAL // 2 // CORES)]
        for side in range(2)
        for c in range(CORES)
    ]

    to_heads = functools.partial(
        lax.all_to_all, axis_name="spatial", split_axis=0, concat_axis=0, tiled=True
    )

    selector = (levels[:, None] == jnp.arange(gate_table.shape[0], dtype=jnp.int32)[None, :]).astype(
        jnp.float32
    )
    gates = jnp.dot(
        selector, gate_table, precision=lax.Precision.HIGHEST, preferred_element_type=jnp.float32
    )
    other_gates = lax.ppermute(gates, "queue", swap_low)
    gates = jnp.where(y_low == 0, jnp.stack((gates, other_gates)), jnp.stack((other_gates, gates)))
    count = RING * frames
    is_last = (jnp.arange(count, dtype=jnp.int32) == count - 1)[None, :, None] & (y_low == 1)
    gates = jnp.where(
        is_last,
        gates[:, count - 1 : count],
        lax.dynamic_slice_in_dim(gates, y_low * count, count, axis=1),
    )

    kv0, kv1, query = pack(queries, keys, values)
    kv0 = to_heads(kv0)
    kv1 = to_heads(hold(kv1, kv0, gates))
    kv0 = hold(kv0, kv1)
    kv0_before, kv0_after = lax.ppermute(kv0, "queue", up), lax.ppermute(kv0, "queue", down)
    query = to_heads(hold(query, kv1))
    kv1 = hold(kv1, query)
    kv1_before, kv1_after = lax.ppermute(kv1, "queue", up), lax.ppermute(kv1, "queue", down)

    weight = lax.all_gather(out_weight, ("queue", "spatial"), axis_index_groups=along_y, axis=0)
    weight = hold(weight, query)
    weight = lax.all_gather(weight, "spatial", axis_index_groups=along_z, axis=0)
    weight = weight.reshape(-1, 2, 2, *out_weight.shape)

    cross = [(RING - 1, QUEUE - 1)]

    def returned(even, odd, crossing):
        odd = jnp.where(position == QUEUE - 1, crossing, odd)
        return to_heads(jnp.concatenate((even, odd), axis=1))

    def spread(mine):
        left = lax.ppermute(mine, "queue", ring_up)
        right = lax.ppermute(mine, "queue", ring_down)
        far_low = lax.ppermute(left[: SPATIAL // 2], "queue", ring_up)
        far_high = lax.ppermute(right[SPATIAL // 2 :], "queue", ring_down)
        return mine, left, right, far_low, far_high

    head0 = (position_now, query, 0, kv0, kv0_before, kv0_after)
    head1 = (position_now, query, 1, kv1, kv1_before, kv1_after)
    odd0, token = attend(1, *head0)
    odd0_crossing = lax.ppermute(odd0, "queue", cross)
    even0, token = attend(0, *head0, token)
    first = returned(even0, odd0, odd0_crossing)
    odd1, token = attend(1, *head1, token, odd0_crossing)
    odd1_crossing = lax.ppermute(odd1, "queue", cross)
    shifted = lax.ppermute(hold(hidden[frames - 1 :], kv1_before), "queue", up)
    weight_own = hold(weight, token)
    weight_pair = lax.ppermute(weight_own, "spatial", swap_core)
    even1, token = attend(0, *head1, token)
    first_sources = spread(hold(first, token, shifted))
    second_sources = spread(returned(even1, odd1, odd1_crossing))

    partial = project(0, place, first_sources, weight_own, weight_pair, None, None)
    branch = project(1, place, second_sources, weight_own, weight_pair, partial, gates)
    branch = lax.all_to_all(
        branch, "queue", split_axis=0, concat_axis=0, axis_index_groups=ring, tiled=True
    )
    branch = branch.reshape(RING, frames, *branch.shape[1:])
    return add_branch(position_now, branch, hidden, shifted, entering)


def solution(mesh):
    return jax.shard_map(
        body,
        mesh=mesh,
        in_specs=(
            P("queue", "spatial", None),
            P("queue", "spatial", None),
            P("queue", "spatial", None),
            P("queue", "spatial", None),
            P("spatial", "queue"),
            P(None, "queue"),
            P(),
            P("spatial", None),
        ),
        out_specs=P("queue", "spatial", None),
        check_vma=False,
    )
```

```python
import functools

import jax
import jax.numpy as jnp
from jax import lax
from jax.experimental import pallas as pl
from jax.experimental.pallas import tpu as pltpu
from jax.sharding import PartitionSpec as P

HEADS = 32
HD = 128
WMAX = 2
NEG_FILL = -1e30
SCALE_LOG2 = (HD ** -0.5) * 1.4426950408889634
BLOCK_Q = 512
VMEM = 28 * 1024 * 1024
LARGE = pltpu.CompilerParams(vmem_limit_bytes=58 * 1024 * 1024)
SMALL = pltpu.CompilerParams(vmem_limit_bytes=1024 * 1024)
MEDIUM = pltpu.CompilerParams(vmem_limit_bytes=12 * 1024 * 1024)
QUEUE = 8
RING = 4
SPATIAL = 16
CORES = 2
PACK = 4
SPAN = 2 * WMAX + 1
ANY = pl.BlockSpec(memory_space=pl.ANY)
TOKEN = (8, 128)


def corner(array):
    rows = 8 if array.dtype == jnp.float32 else 16
    block = (1,) * (array.ndim - 2) + (rows, 128)
    return pl.BlockSpec(block, lambda *at: (0,) * array.ndim)


def pack(queries, keys, values):
    frames, tok, width = keys.shape
    group = width // SPATIAL
    piece = width // PACK
    count = SPATIAL // PACK
    heads = group // HD

    def kernel(q_ref, k_ref, v_ref, *out_refs):
        for i in range(count):
            for head in range(heads):
                kv_ref, out_ref = out_refs[head], out_refs[heads + head]
                cols = slice(i * group + head * HD, i * group + (head + 1) * HD)
                kv_ref[i, 0] = k_ref[:, :, cols]
                kv_ref[i, 1] = v_ref[:, :, cols]
                out_ref[i] = q_ref[:, :, cols]

    spec = pl.BlockSpec((frames, tok, piece), lambda s: (0, 0, s))
    kv_spec = pl.BlockSpec((count, 2, frames, tok, HD), lambda s: (s, 0, 0, 0, 0))
    q_spec = pl.BlockSpec((count, frames, tok, HD), lambda s: (s, 0, 0, 0))
    kv_shape = jax.ShapeDtypeStruct((SPATIAL, 2, frames, tok, HD), keys.dtype)
    q_shape = jax.ShapeDtypeStruct((SPATIAL, frames, tok, HD), queries.dtype)
    return pl.pallas_call(
        kernel,
        grid=(PACK,),
        in_specs=[spec] * 3,
        out_specs=[kv_spec] * heads + [q_spec] * heads,
        out_shape=[kv_shape] * heads + [q_shape] * heads,
        compiler_params=LARGE,
        name="pack",
    )(queries, keys, values)


def hold(array, *earlier):
    def kernel(*refs):
        pass

    return pl.pallas_call(
        kernel,
        grid=(1,),
        in_specs=[ANY] + [corner(e) for e in earlier],
        out_specs=ANY,
        out_shape=jax.ShapeDtypeStruct(array.shape, array.dtype),
        input_output_aliases={0: 0},
        compiler_params=SMALL,
        name="hold",
    )(array, *earlier)


def attend(frame, position, query, own, before, after, *earlier):
    groups, frames, tok, _ = query.shape
    width = own.shape[-1]
    row_count = groups * tok
    groups_block = BLOCK_Q // tok
    blocks = row_count // BLOCK_Q
    asked = range(frames) if frame is None else (frame,)
    before_from = min(asked)
    before_count = frames - before_from
    after_count = max(asked) + 1
    loaded = before_count + frames + after_count

    def kernel(pos_ref, q_ref, own_ref, before_ref, after_ref, *rest):
        out_ref, token_ref, kt_ref, vx_ref = rest[-4:]
        sources = (
            [(before_ref, f) for f in range(before_count)]
            + [(own_ref, f) for f in range(frames)]
            + [(after_ref, f) for f in range(after_count)]
        )
        turn_frame = pl.program_id(0)

        @pl.when((turn_frame == 0) & (pl.program_id(1) == 0))
        def _():
            for at, (ref, f) in enumerate(sources):
                rows = slice(at * row_count, (at + 1) * row_count)
                turned = ref[:, 0, f].reshape(row_count, width).T
                kt_ref[:width, rows] = turned
                kt_ref[width:, rows] = turned
                vx_ref[rows, :width] = ref[:, 1, f].reshape(row_count, width)
                vx_ref[rows, width:] = jnp.ones((row_count, width), vx_ref.dtype)

        q = q_ref[:, 0].reshape(BLOCK_Q, width).astype(jnp.float32) * SCALE_LOG2
        high = q.astype(jnp.bfloat16)
        low = (q - high.astype(jnp.float32)).astype(jnp.bfloat16)
        q = jnp.concatenate((high, low), axis=1)
        position_now = pos_ref[0]

        def rows_of(step):
            start = (turn_frame + step) * row_count
            return pl.ds(pl.multiple_of(start, row_count), row_count)

        def scores(step):
            return jnp.dot(q, kt_ref[:, rows_of(step)], preferred_element_type=jnp.float32)

        top = jnp.full((BLOCK_Q, 1), NEG_FILL, jnp.float32)
        total = jnp.zeros((BLOCK_Q, 2 * width), jnp.float32)
        order = (2, 1, 3, 0, 4)
        ahead = scores(order[0])
        for turn, step in enumerate(order):
            s = ahead
            if turn + 1 < SPAN:
                ahead = scores(order[turn + 1])
            at = turn_frame + step
            absent = ((position_now == 0) & (at < before_count)) | (
                (position_now == QUEUE - 1) & (at >= before_count + frames)
            )
            peak = jnp.max(s, axis=1, keepdims=True)
            peak = jnp.where(absent, NEG_FILL, peak)
            lifted_top = jnp.maximum(top, peak)
            less = jnp.where(absent, -NEG_FILL, lifted_top)
            weights = jnp.exp2(s - less).astype(jnp.bfloat16)
            part = jnp.dot(weights, vx_ref[rows_of(step)], preferred_element_type=jnp.float32)
            total = total * jnp.exp2(top - lifted_top) + part
            top = lifted_top
        result = total[:, :width] / total[:, width:]
        out_ref[:, 0] = result.astype(out_ref.dtype).reshape(groups_block, tok, width)
        token_ref[...] = jnp.zeros_like(token_ref)

    first = asked[0]
    in_specs = [
        pl.BlockSpec((groups_block, 1, tok, width), lambda f, b, pos: (b, first + f, 0, 0)),
        pl.BlockSpec(own.shape, lambda f, b, pos: (0, 0, 0, 0, 0)),
        pl.BlockSpec(
            (groups, 2, before_count, tok, width),
            lambda f, b, pos: (0, 0, before_from // before_count, 0, 0),
        ),
        pl.BlockSpec((groups, 2, after_count, tok, width), lambda f, b, pos: (0, 0, 0, 0, 0)),
    ]
    return pl.pallas_call(
        kernel,
        grid_spec=pltpu.PrefetchScalarGridSpec(
            num_scalar_prefetch=1,
            grid=(len(asked), blocks),
            in_specs=in_specs + [corner(e) for e in earlier],
            out_specs=[
                pl.BlockSpec((groups_block, 1, tok, width), lambda f, b, pos: (b, f, 0, 0)),
                pl.BlockSpec(TOKEN, lambda f, b, pos: (0, 0)),
            ],
            scratch_shapes=[
                pltpu.VMEM((2 * width, loaded * row_count), jnp.bfloat16),
                pltpu.VMEM((loaded * row_count, 2 * width), jnp.bfloat16),
            ],
        ),
        out_shape=[
            jax.ShapeDtypeStruct((groups, len(asked), tok, width), query.dtype),
            jax.ShapeDtypeStruct(TOKEN, jnp.float32),
        ],
        compiler_params=pltpu.CompilerParams(vmem_limit_bytes=VMEM),
        cost_estimate=pl.CostEstimate(
            flops=len(asked) * row_count * SPAN * row_count * width * 8,
            bytes_accessed=4 * 1024 * 1024,
            transcendentals=len(asked) * row_count * SPAN * row_count,
        ),
        name="attend",
    )(position, query, own, before, after, *earlier)


def project(head, place, sources, weight_own, weight_pair, partial, gates, *earlier):
    mine = sources[0]
    groups, frames, tok, width = mine.shape
    steps, sides, halves, rows_dev, cols_dev = weight_own.shape
    half = steps * sides
    rows = frames * tok
    last = partial is not None

    def kernel(place_ref, mine_ref, left_ref, right_ref, low_ref, high_ref, wo_ref, wp_ref, *rest):
        out_ref, a_ref = rest[-2:]
        x, core = place_ref[0], place_ref[1]

        @pl.when(pl.program_id(0) == 0)
        def _():
            for i in range(half):
                z, side = i // sides, i % sides
                for part in range(CORES):
                    group = side * half + CORES * z + (core if part == 0 else 1 - core)
                    cols = slice((part * half + i) * width, (part * half + i + 1) * width)
                    far = high_ref[group - half] if side else low_ref[group]
                    a_ref[0:rows, cols] = mine_ref[group].reshape(rows, width)
                    a_ref[rows : 2 * rows, cols] = right_ref[group].reshape(rows, width)
                    a_ref[2 * rows : 3 * rows, cols] = far.reshape(rows, width)
                    a_ref[3 * rows :, cols] = left_ref[group].reshape(rows, width)

        total = jnp.dot(
            a_ref[:, : half * width],
            wo_ref[:, :, 0].reshape(half * width, cols_dev),
            preferred_element_type=jnp.float32,
        )
        total += jnp.dot(
            a_ref[:, half * width :],
            wp_ref[:, :, 0].reshape(half * width, cols_dev),
            preferred_element_type=jnp.float32,
        )
        if not last:
            out_ref[0] = total
            return
        total += rest[0][0]
        gates_ref = rest[1]
        for source in range(RING):
            at = lax.rem(x + source, RING)
            for f in range(frames):
                gate = gates_ref[0, pl.ds(at * frames + f, 1), :]
                start = source * rows + f * tok
                slot = at * frames + 1 if f == 0 else lax.rem(at + 1, RING) * frames
                out_ref[slot, 0] = (gate * total[start : start + tok]).astype(out_ref.dtype)

    def whole(array):
        return pl.BlockSpec(array.shape, lambda n, place: (0,) * array.ndim)

    weight = pl.BlockSpec(
        (steps, sides, 1, width, cols_dev), lambda n, place: (0, 0, n, head, 0)
    )
    partial_spec = pl.BlockSpec((1, RING * rows, cols_dev), lambda n, place: (n, 0, 0))
    in_specs = [*map(whole, sources), weight, weight]
    operands = [*sources, weight_own, weight_pair]
    if last:
        in_specs += [partial_spec, pl.BlockSpec((1,) + gates.shape[1:], lambda n, place: (n, 0, 0))]
        operands += [partial, gates]
        out_spec = pl.BlockSpec((RING * frames, 1, tok, cols_dev), lambda n, place: (0, n, 0, 0))
        out_shape = jax.ShapeDtypeStruct((RING * frames, halves, tok, cols_dev), jnp.bfloat16)
    else:
        out_spec = partial_spec
        out_shape = jax.ShapeDtypeStruct((halves, RING * rows, cols_dev), jnp.float32)
    return pl.pallas_call(
        kernel,
        grid_spec=pltpu.PrefetchScalarGridSpec(
            num_scalar_prefetch=1,
            grid=(halves,),
            in_specs=in_specs + [corner(e) for e in earlier],
            out_specs=out_spec,
            scratch_shapes=[pltpu.VMEM((RING * rows, groups * width), jnp.bfloat16)],
        ),
        out_shape=out_shape,
        compiler_params=LARGE,
        cost_estimate=pl.CostEstimate(
            flops=2 * RING * rows * groups * width * halves * cols_dev,
            bytes_accessed=8 * 1024 * 1024,
            transcendentals=0,
        ),
        name="project_last" if last else "project_first",
    )(place, *operands, *earlier)


def add_branch(position, branch, hidden, shifted, entering):
    sources, frames, halves, tok, cols = branch.shape
    width = hidden.shape[-1]

    def kernel(pos_ref, b_ref, hidden_ref, shifted_ref, entering_ref, out_ref):
        def add(base_ref, replaced):
            for half in range(halves):
                for source in range(sources):
                    start = (half * sources + source) * cols
                    at = slice(start, start + cols)
                    value = base_ref[0, :, at].astype(jnp.float32)
                    value += b_ref[source, 0, half].astype(jnp.float32)
                    if replaced:
                        value = jnp.where(
                            pos_ref[0] == 0, entering_ref[:, at].astype(jnp.float32), value
                        )
                    out_ref[0, :, at] = value.astype(out_ref.dtype)

        @pl.when(pl.program_id(0) == 0)
        def _():
            add(shifted_ref, True)

        @pl.when(pl.program_id(0) == 1)
        def _():
            add(hidden_ref, False)

    frame_spec = pl.BlockSpec((1, tok, width), lambda i, pos: (0, 0, 0))
    return pl.pallas_call(
        kernel,
        grid_spec=pltpu.PrefetchScalarGridSpec(
            num_scalar_prefetch=1,
            grid=(frames,),
            in_specs=[
                pl.BlockSpec((sources, 1, halves, tok, cols), lambda i, pos: (0, i, 0, 0, 0)),
                frame_spec,
                frame_spec,
                pl.BlockSpec((tok, width), lambda i, pos: (0, 0)),
            ],
            out_specs=pl.BlockSpec((1, tok, width), lambda i, pos: (i, 0, 0)),
        ),
        out_shape=jax.ShapeDtypeStruct((frames, tok, width), hidden.dtype),
        compiler_params=MEDIUM,
        name="add_branch",
    )(position, branch, hidden, shifted, entering)


def body(hidden, queries, keys, values, out_weight, gate_table, levels, entering):
    frames = queries.shape[0]
    position = lax.axis_index("queue")
    spatial = lax.axis_index("spatial")
    y_low, x = position // RING, position % RING
    core = spatial % CORES
    position_now = position.astype(jnp.int32)[None]
    place = jnp.stack((x, core)).astype(jnp.int32)

    up = [(p, p + 1) for p in range(QUEUE - 1)]
    down = [(p + 1, p) for p in range(QUEUE - 1)]
    ring = [[r * RING + i for i in range(RING)] for r in range(QUEUE // RING)]
    ring_up = [(g[i], g[(i + 1) % RING]) for g in ring for i in range(RING)]
    ring_down = [(g[(i + 1) % RING], g[i]) for g in ring for i in range(RING)]
    swap_low = [(p, (p + RING) % QUEUE) for p in range(QUEUE)]
    swap_core = [(s, s ^ 1) for s in range(SPATIAL)]
    along_y = [
        [(low * RING + i) * SPATIAL + side * (SPATIAL // 2) + r for side in range(2) for low in range(2)]
        for i in range(RING)
        for r in range(SPATIAL // 2)
    ]
    along_z = [
        [side * (SPATIAL // 2) + z * CORES + c for z in range(SPATIAL // 2 // CORES)]
        for side in range(2)
        for c in range(CORES)
    ]

    to_heads = functools.partial(
        lax.all_to_all, axis_name="spatial", split_axis=0, concat_axis=0, tiled=True
    )

    selector = (levels[:, None] == jnp.arange(gate_table.shape[0], dtype=jnp.int32)[None, :]).astype(
        jnp.float32
    )
    gates = jnp.dot(
        selector, gate_table, precision=lax.Precision.HIGHEST, preferred_element_type=jnp.float32
    )
    other_gates = lax.ppermute(gates, "queue", swap_low)
    gates = jnp.where(y_low == 0, jnp.stack((gates, other_gates)), jnp.stack((other_gates, gates)))
    count = RING * frames
    is_last = (jnp.arange(count, dtype=jnp.int32) == count - 1)[None, :, None] & (y_low == 1)
    gates = jnp.where(
        is_last,
        gates[:, count - 1 : count],
        lax.dynamic_slice_in_dim(gates, y_low * count, count, axis=1),
    )

    kv0, kv1, q0, q1 = pack(queries, keys, values)
    kv0 = to_heads(kv0)
    kv1 = to_heads(hold(kv1, kv0, gates))
    q0 = to_heads(hold(q0, kv1))
    kv0 = hold(kv0, q0)
    kv0_before, kv0_after = lax.ppermute(kv0, "queue", up), lax.ppermute(kv0, "queue", down)
    q1 = to_heads(hold(q1, kv0_before, kv0_after))
    kv1 = hold(kv1, kv0_before, kv0_after)
    kv1_before, kv1_after = lax.ppermute(kv1, "queue", up), lax.ppermute(kv1, "queue", down)

    weight = lax.all_gather(out_weight, ("queue", "spatial"), axis_index_groups=along_y, axis=0)
    weight = hold(weight, q0)
    weight = lax.all_gather(weight, "spatial", axis_index_groups=along_z, axis=0)
    weight = weight.reshape(-1, 2, 2, *out_weight.shape)

    cross = [(RING - 1, QUEUE - 1)]

    def with_crossing(even, odd, crossing):
        odd = jnp.where(position == QUEUE - 1, crossing, odd)
        return jnp.concatenate((even, odd), axis=1)

    def spread(mine):
        left = lax.ppermute(mine, "queue", ring_up)
        right = lax.ppermute(mine, "queue", ring_down)
        far_low = lax.ppermute(left[: SPATIAL // 2], "queue", ring_up)
        far_high = lax.ppermute(right[SPATIAL // 2 :], "queue", ring_down)
        return mine, left, right, far_low, far_high

    head0 = (position_now, q0, kv0, kv0_before, kv0_after)
    head1 = (position_now, q1, kv1, kv1_before, kv1_after)
    odd0, token = attend(1, *head0)
    odd0_crossing = lax.ppermute(odd0, "queue", cross)
    even0, token = attend(0, *head0, token)
    first = with_crossing(even0, odd0, odd0_crossing)
    odd1, token = attend(1, *head1, token, first)
    odd1_crossing = lax.ppermute(odd1, "queue", cross)
    first_sources = spread(hold(to_heads(first), token))
    shifted = lax.ppermute(hold(hidden[frames - 1 :], kv1_before, token), "queue", up)
    weight_own = hold(weight, token)
    weight_pair = lax.ppermute(weight_own, "spatial", swap_core)
    even1, token = attend(0, *head1, token)
    second = with_crossing(even1, odd1, odd1_crossing)
    second_sources = spread(to_heads(hold(second, shifted)))

    partial = project(0, place, first_sources, weight_own, weight_pair, None, None)
    branch = project(1, place, second_sources, weight_own, weight_pair, partial, gates)
    branch = lax.all_to_all(
        branch, "queue", split_axis=0, concat_axis=0, axis_index_groups=ring, tiled=True
    )
    branch = branch.reshape(RING, frames, *branch.shape[1:])
    return add_branch(position_now, branch, hidden, shifted, entering)


def solution(mesh):
    return jax.shard_map(
        body,
        mesh=mesh,
        in_specs=(
            P("queue", "spatial", None),
            P("queue", "spatial", None),
            P("queue", "spatial", None),
            P("queue", "spatial", None),
            P("spatial", "queue"),
            P(None, "queue"),
            P(),
            P("spatial", None),
        ),
        out_specs=P("queue", "spatial", None),
        check_vma=False,
    )
```

```python
import functools

import jax
import jax.numpy as jnp
from jax import lax
from jax.experimental import pallas as pl
from jax.experimental.pallas import tpu as pltpu
from jax.sharding import PartitionSpec as P

HEADS = 32
HD = 128
WMAX = 2
NEG_FILL = -1e30
SCALE_LOG2 = (HD ** -0.5) * 1.4426950408889634
BLOCK_Q = 512
VMEM = 28 * 1024 * 1024
LARGE = pltpu.CompilerParams(vmem_limit_bytes=58 * 1024 * 1024)
MEDIUM = pltpu.CompilerParams(vmem_limit_bytes=12 * 1024 * 1024)
QUEUE = 8
RING = 4
SPATIAL = 16
CORES = 2
PACK = 4
SPAN = 2 * WMAX + 1
ANY = pl.BlockSpec(memory_space=pl.ANY)
TOKEN = (8, 128)


def corner(array):
    rows = 8 if array.dtype == jnp.float32 else 16
    block = (1,) * (array.ndim - 2) + (rows, 128)
    return pl.BlockSpec(block, lambda *at: (0,) * array.ndim)


def pack(queries, keys, values):
    frames, tok, width = keys.shape
    group = width // SPATIAL
    piece = width // PACK
    count = SPATIAL // PACK

    def kernel(q_ref, k_ref, v_ref, kv0_ref, kv1_ref, out_ref):
        for i in range(count):
            for head, kv_ref in enumerate((kv0_ref, kv1_ref)):
                cols = slice(i * group + head * HD, i * group + (head + 1) * HD)
                kv_ref[i, 0] = k_ref[:, :, cols]
                kv_ref[i, 1] = v_ref[:, :, cols]
            out_ref[i] = q_ref[:, :, i * group : (i + 1) * group]

    spec = pl.BlockSpec((frames, tok, piece), lambda s: (0, 0, s))
    kv_spec = pl.BlockSpec((count, 2, frames, tok, HD), lambda s: (s, 0, 0, 0, 0))
    kv_shape = jax.ShapeDtypeStruct((SPATIAL, 2, frames, tok, HD), keys.dtype)
    return pl.pallas_call(
        kernel,
        grid=(PACK,),
        in_specs=[spec] * 3,
        out_specs=[kv_spec, kv_spec, pl.BlockSpec((count, frames, tok, group), lambda s: (s, 0, 0, 0))],
        out_shape=[
            kv_shape,
            kv_shape,
            jax.ShapeDtypeStruct((SPATIAL, frames, tok, group), queries.dtype),
        ],
        compiler_params=LARGE,
        name="pack",
    )(queries, keys, values)


def hold(array, *earlier, room=1):
    def kernel(*refs):
        pass

    return pl.pallas_call(
        kernel,
        grid=(1,),
        in_specs=[ANY] + [corner(e) for e in earlier],
        out_specs=ANY,
        out_shape=jax.ShapeDtypeStruct(array.shape, array.dtype),
        input_output_aliases={0: 0},
        compiler_params=pltpu.CompilerParams(vmem_limit_bytes=room * 1024 * 1024),
        name="hold",
    )(array, *earlier)


def attend(frame, position, query, head, own, before, after, *earlier):
    groups, frames, tok, both = query.shape
    width = own.shape[-1]
    row_count = groups * tok
    groups_block = BLOCK_Q // tok
    blocks = row_count // BLOCK_Q
    asked = range(frames) if frame is None else (frame,)
    before_from = min(asked)
    before_count = frames - before_from
    after_count = max(asked) + 1
    loaded = before_count + frames + after_count

    def kernel(pos_ref, q_ref, own_ref, before_ref, after_ref, *rest):
        out_ref, token_ref, kt_ref, vx_ref = rest[-4:]
        sources = (
            [(before_ref, f) for f in range(before_count)]
            + [(own_ref, f) for f in range(frames)]
            + [(after_ref, f) for f in range(after_count)]
        )
        turn_frame = pl.program_id(0)

        @pl.when((turn_frame == 0) & (pl.program_id(1) == 0))
        def _():
            for at, (ref, f) in enumerate(sources):
                rows = slice(at * row_count, (at + 1) * row_count)
                turned = ref[:, 0, f].reshape(row_count, width).T
                kt_ref[:width, rows] = turned
                kt_ref[width:, rows] = turned
                vx_ref[rows, :width] = ref[:, 1, f].reshape(row_count, width)
                vx_ref[rows, width:] = jnp.ones((row_count, width), vx_ref.dtype)

        q = q_ref[:, 0].reshape(BLOCK_Q, width).astype(jnp.float32) * SCALE_LOG2
        high = q.astype(jnp.bfloat16)
        low = (q - high.astype(jnp.float32)).astype(jnp.bfloat16)
        q = jnp.concatenate((high, low), axis=1)
        position_now = pos_ref[0]

        def rows_of(step):
            start = (turn_frame + step) * row_count
            return pl.ds(pl.multiple_of(start, row_count), row_count)

        def scores(step):
            return jnp.dot(q, kt_ref[:, rows_of(step)], preferred_element_type=jnp.float32)

        top = jnp.full((BLOCK_Q, 1), NEG_FILL, jnp.float32)
        total = jnp.zeros((BLOCK_Q, 2 * width), jnp.float32)
        order = (2, 1, 3, 0, 4)
        ahead = scores(order[0])
        for turn, step in enumerate(order):
            s = ahead
            if turn + 1 < SPAN:
                ahead = scores(order[turn + 1])
            at = turn_frame + step
            absent = ((position_now == 0) & (at < before_count)) | (
                (position_now == QUEUE - 1) & (at >= before_count + frames)
            )
            peak = jnp.max(s, axis=1, keepdims=True)
            peak = jnp.where(absent, NEG_FILL, peak)
            lifted_top = jnp.maximum(top, peak)
            less = jnp.where(absent, -NEG_FILL, lifted_top)
            weights = jnp.exp2(s - less).astype(jnp.bfloat16)
            part = jnp.dot(weights, vx_ref[rows_of(step)], preferred_element_type=jnp.float32)
            total = total * jnp.exp2(top - lifted_top) + part
            top = lifted_top
        result = total[:, :width] / total[:, width:]
        out_ref[:, 0] = result.astype(out_ref.dtype).reshape(groups_block, tok, width)
        token_ref[...] = jnp.zeros_like(token_ref)

    first = asked[0]
    in_specs = [
        pl.BlockSpec((groups_block, 1, tok, width), lambda f, b, pos: (b, first + f, 0, head)),
        pl.BlockSpec(own.shape, lambda f, b, pos: (0, 0, 0, 0, 0)),
        pl.BlockSpec(
            (groups, 2, before_count, tok, width),
            lambda f, b, pos: (0, 0, before_from // before_count, 0, 0),
        ),
        pl.BlockSpec((groups, 2, after_count, tok, width), lambda f, b, pos: (0, 0, 0, 0, 0)),
    ]
    return pl.pallas_call(
        kernel,
        grid_spec=pltpu.PrefetchScalarGridSpec(
            num_scalar_prefetch=1,
            grid=(len(asked), blocks),
            in_specs=in_specs + [corner(e) for e in earlier],
            out_specs=[
                pl.BlockSpec((groups_block, 1, tok, width), lambda f, b, pos: (b, f, 0, 0)),
                pl.BlockSpec(TOKEN, lambda f, b, pos: (0, 0)),
            ],
            scratch_shapes=[
                pltpu.VMEM((2 * width, loaded * row_count), jnp.bfloat16),
                pltpu.VMEM((loaded * row_count, 2 * width), jnp.bfloat16),
            ],
        ),
        out_shape=[
            jax.ShapeDtypeStruct((groups, len(asked), tok, width), query.dtype),
            jax.ShapeDtypeStruct(TOKEN, jnp.float32),
        ],
        compiler_params=pltpu.CompilerParams(vmem_limit_bytes=VMEM),
        cost_estimate=pl.CostEstimate(
            flops=len(asked) * row_count * SPAN * row_count * width * 8,
            bytes_accessed=4 * 1024 * 1024,
            transcendentals=len(asked) * row_count * SPAN * row_count,
        ),
        name="attend",
    )(position, query, own, before, after, *earlier)


def project(head, place, sources, weight_own, weight_pair, partial, gates, *earlier):
    mine = sources[0]
    groups, frames, tok, width = mine.shape
    steps, sides, halves, rows_dev, cols_dev = weight_own.shape
    half = steps * sides
    rows = frames * tok
    last = partial is not None

    def kernel(place_ref, mine_ref, left_ref, right_ref, low_ref, high_ref, wo_ref, wp_ref, *rest):
        out_ref, a_ref = rest[-2:]
        x, core = place_ref[0], place_ref[1]

        @pl.when(pl.program_id(0) == 0)
        def _():
            for i in range(half):
                z, side = i // sides, i % sides
                for part in range(CORES):
                    group = side * half + CORES * z + (core if part == 0 else 1 - core)
                    cols = slice((part * half + i) * width, (part * half + i + 1) * width)
                    far = high_ref[group - half] if side else low_ref[group]
                    a_ref[0:rows, cols] = mine_ref[group].reshape(rows, width)
                    a_ref[rows : 2 * rows, cols] = right_ref[group].reshape(rows, width)
                    a_ref[2 * rows : 3 * rows, cols] = far.reshape(rows, width)
                    a_ref[3 * rows :, cols] = left_ref[group].reshape(rows, width)

        total = jnp.dot(
            a_ref[:, : half * width],
            wo_ref[:, :, 0].reshape(half * width, cols_dev),
            preferred_element_type=jnp.float32,
        )
        total += jnp.dot(
            a_ref[:, half * width :],
            wp_ref[:, :, 0].reshape(half * width, cols_dev),
            preferred_element_type=jnp.float32,
        )
        if not last:
            out_ref[0] = total
            return
        total += rest[0][0]
        gates_ref = rest[1]
        for source in range(RING):
            at = lax.rem(x + source, RING)
            for f in range(frames):
                gate = gates_ref[0, pl.ds(at * frames + f, 1), :]
                start = source * rows + f * tok
                slot = at * frames + 1 if f == 0 else lax.rem(at + 1, RING) * frames
                out_ref[slot, 0] = (gate * total[start : start + tok]).astype(out_ref.dtype)

    def whole(array):
        return pl.BlockSpec(array.shape, lambda n, place: (0,) * array.ndim)

    weight = pl.BlockSpec(
        (steps, sides, 1, width, cols_dev), lambda n, place: (0, 0, n, head, 0)
    )
    partial_spec = pl.BlockSpec((1, RING * rows, cols_dev), lambda n, place: (n, 0, 0))
    in_specs = [*map(whole, sources), weight, weight]
    operands = [*sources, weight_own, weight_pair]
    if last:
        in_specs += [partial_spec, pl.BlockSpec((1,) + gates.shape[1:], lambda n, place: (n, 0, 0))]
        operands += [partial, gates]
        out_spec = pl.BlockSpec((RING * frames, 1, tok, cols_dev), lambda n, place: (0, n, 0, 0))
        out_shape = jax.ShapeDtypeStruct((RING * frames, halves, tok, cols_dev), jnp.bfloat16)
    else:
        out_spec = partial_spec
        out_shape = jax.ShapeDtypeStruct((halves, RING * rows, cols_dev), jnp.float32)
    return pl.pallas_call(
        kernel,
        grid_spec=pltpu.PrefetchScalarGridSpec(
            num_scalar_prefetch=1,
            grid=(halves,),
            in_specs=in_specs + [corner(e) for e in earlier],
            out_specs=out_spec,
            scratch_shapes=[pltpu.VMEM((RING * rows, groups * width), jnp.bfloat16)],
        ),
        out_shape=out_shape,
        compiler_params=pltpu.CompilerParams(vmem_limit_bytes=48 * 1024 * 1024),
        cost_estimate=pl.CostEstimate(
            flops=2 * RING * rows * groups * width * halves * cols_dev,
            bytes_accessed=8 * 1024 * 1024,
            transcendentals=0,
        ),
        name="project_last" if last else "project_first",
    )(place, *operands, *earlier)


def add_branch(position, branch, hidden, shifted, entering):
    sources, frames, halves, tok, cols = branch.shape
    width = hidden.shape[-1]

    def kernel(pos_ref, b_ref, hidden_ref, shifted_ref, entering_ref, out_ref):
        def add(base_ref, replaced):
            for half in range(halves):
                for source in range(sources):
                    start = (half * sources + source) * cols
                    at = slice(start, start + cols)
                    value = base_ref[0, :, at].astype(jnp.float32)
                    value += b_ref[source, 0, half].astype(jnp.float32)
                    if replaced:
                        value = jnp.where(
                            pos_ref[0] == 0, entering_ref[:, at].astype(jnp.float32), value
                        )
                    out_ref[0, :, at] = value.astype(out_ref.dtype)

        @pl.when(pl.program_id(0) == 0)
        def _():
            add(shifted_ref, True)

        @pl.when(pl.program_id(0) == 1)
        def _():
            add(hidden_ref, False)

    frame_spec = pl.BlockSpec((1, tok, width), lambda i, pos: (0, 0, 0))
    return pl.pallas_call(
        kernel,
        grid_spec=pltpu.PrefetchScalarGridSpec(
            num_scalar_prefetch=1,
            grid=(frames,),
            in_specs=[
                pl.BlockSpec((sources, 1, halves, tok, cols), lambda i, pos: (0, i, 0, 0, 0)),
                frame_spec,
                frame_spec,
                pl.BlockSpec((tok, width), lambda i, pos: (0, 0)),
            ],
            out_specs=pl.BlockSpec((1, tok, width), lambda i, pos: (i, 0, 0)),
        ),
        out_shape=jax.ShapeDtypeStruct((frames, tok, width), hidden.dtype),
        compiler_params=MEDIUM,
        name="add_branch",
    )(position, branch, hidden, shifted, entering)


def body(hidden, queries, keys, values, out_weight, gate_table, levels, entering):
    frames = queries.shape[0]
    position = lax.axis_index("queue")
    spatial = lax.axis_index("spatial")
    y_low, x = position // RING, position % RING
    core = spatial % CORES
    position_now = position.astype(jnp.int32)[None]
    place = jnp.stack((x, core)).astype(jnp.int32)

    up = [(p, p + 1) for p in range(QUEUE - 1)]
    down = [(p + 1, p) for p in range(QUEUE - 1)]
    ring = [[r * RING + i for i in range(RING)] for r in range(QUEUE // RING)]
    ring_up = [(g[i], g[(i + 1) % RING]) for g in ring for i in range(RING)]
    ring_down = [(g[(i + 1) % RING], g[i]) for g in ring for i in range(RING)]
    swap_low = [(p, (p + RING) % QUEUE) for p in range(QUEUE)]
    swap_core = [(s, s ^ 1) for s in range(SPATIAL)]
    along_y = [
        [(low * RING + i) * SPATIAL + side * (SPATIAL // 2) + r for side in range(2) for low in range(2)]
        for i in range(RING)
        for r in range(SPATIAL // 2)
    ]
    along_z = [
        [side * (SPATIAL // 2) + z * CORES + c for z in range(SPATIAL // 2 // CORES)]
        for side in range(2)
        for c in range(CORES)
    ]

    to_heads = functools.partial(
        lax.all_to_all, axis_name="spatial", split_axis=0, concat_axis=0, tiled=True
    )

    selector = (levels[:, None] == jnp.arange(gate_table.shape[0], dtype=jnp.int32)[None, :]).astype(
        jnp.float32
    )
    gates = jnp.dot(
        selector, gate_table, precision=lax.Precision.HIGHEST, preferred_element_type=jnp.float32
    )
    other_gates = lax.ppermute(gates, "queue", swap_low)
    gates = jnp.where(y_low == 0, jnp.stack((gates, other_gates)), jnp.stack((other_gates, gates)))
    count = RING * frames
    is_last = (jnp.arange(count, dtype=jnp.int32) == count - 1)[None, :, None] & (y_low == 1)
    gates = jnp.where(
        is_last,
        gates[:, count - 1 : count],
        lax.dynamic_slice_in_dim(gates, y_low * count, count, axis=1),
    )

    kv0, kv1, query = pack(queries, keys, values)
    kv0 = to_heads(kv0)
    kv1_heads = to_heads(hold(kv1, kv0, gates))
    query = to_heads(hold(query, kv1_heads))
    kv0 = hold(kv0, query)
    kv0_before, kv0_after = lax.ppermute(kv0, "queue", up), lax.ppermute(kv0, "queue", down)
    kv1 = hold(kv1_heads, query)
    kv1_before, kv1_after = lax.ppermute(kv1, "queue", up), lax.ppermute(kv1, "queue", down)

    weight = lax.all_gather(out_weight, ("queue", "spatial"), axis_index_groups=along_y, axis=0)
    weight = hold(weight, query, room=56)
    weight = lax.all_gather(weight, "spatial", axis_index_groups=along_z, axis=0)
    weight = weight.reshape(-1, 2, 2, *out_weight.shape)

    cross = [(RING - 1, QUEUE - 1)]

    def returned(even, odd, crossing):
        odd = jnp.where(position == QUEUE - 1, crossing, odd)
        return to_heads(jnp.concatenate((even, odd), axis=1))

    def spread(mine):
        left = lax.ppermute(mine, "queue", ring_up)
        right = lax.ppermute(mine, "queue", ring_down)
        far_low = lax.ppermute(left[: SPATIAL // 2], "queue", ring_up)
        far_high = lax.ppermute(right[SPATIAL // 2 :], "queue", ring_down)
        return mine, left, right, far_low, far_high

    head0 = (position_now, query, 0, kv0, kv0_before, kv0_after)
    head1 = (position_now, query, 1, kv1, kv1_before, kv1_after)
    odd0, token = attend(1, *head0)
    odd0_crossing = lax.ppermute(odd0, "queue", cross)
    even0, token = attend(0, *head0, token)
    first = returned(even0, odd0, odd0_crossing)
    odd1, token = attend(1, *head1, token, odd0_crossing)
    odd1_crossing = lax.ppermute(odd1, "queue", cross)
    shifted = lax.ppermute(hold(hidden[frames - 1 :], kv1_before), "queue", up)
    weight_own = hold(weight, token, room=56)
    weight_pair = lax.ppermute(weight_own, "spatial", swap_core)
    even1, token = attend(0, *head1, token)
    first_sources = spread(hold(first, token, shifted))
    second_sources = spread(returned(even1, odd1, odd1_crossing))

    partial = project(0, place, first_sources, weight_own, weight_pair, None, None)
    branch = project(1, place, second_sources, weight_own, weight_pair, partial, gates)
    branch = lax.all_to_all(
        branch, "queue", split_axis=0, concat_axis=0, axis_index_groups=ring, tiled=True
    )
    branch = branch.reshape(RING, frames, *branch.shape[1:])
    return add_branch(position_now, branch, hidden, shifted, entering)


def solution(mesh):
    return jax.shard_map(
        body,
        mesh=mesh,
        in_specs=(
            P("queue", "spatial", None),
            P("queue", "spatial", None),
            P("queue", "spatial", None),
            P("queue", "spatial", None),
            P("spatial", "queue"),
            P(None, "queue"),
            P(),
            P("spatial", None),
        ),
        out_specs=P("queue", "spatial", None),
        check_vma=False,
    )
```

```python
import functools

import jax
import jax.numpy as jnp
from jax import lax
from jax.experimental import pallas as pl
from jax.experimental.pallas import tpu as pltpu
from jax.sharding import PartitionSpec as P

HEADS = 32
HD = 128
WMAX = 2
NEG_FILL = -1e30
SCALE_LOG2 = (HD ** -0.5) * 1.4426950408889634
BLOCK_Q = 512
VMEM = 28 * 1024 * 1024
LARGE = pltpu.CompilerParams(vmem_limit_bytes=58 * 1024 * 1024)
MEDIUM = pltpu.CompilerParams(vmem_limit_bytes=12 * 1024 * 1024)
QUEUE = 8
RING = 4
SPATIAL = 16
CORES = 2
PACK = 4
SPAN = 2 * WMAX + 1
ANY = pl.BlockSpec(memory_space=pl.ANY)
TOKEN = (8, 128)


def corner(array):
    rows = 8 if array.dtype == jnp.float32 else 16
    block = (1,) * (array.ndim - 2) + (rows, 128)
    return pl.BlockSpec(block, lambda *at: (0,) * array.ndim)


def pack(queries, keys, values, hidden):
    frames, tok, width = keys.shape
    group = width // SPATIAL
    piece = width // PACK
    count = SPATIAL // PACK

    def kernel(q_ref, k_ref, v_ref, hidden_ref, kv0_ref, kv1_ref, out_ref, last_ref):
        last_ref[...] = hidden_ref[...]
        for i in range(count):
            for head, kv_ref in enumerate((kv0_ref, kv1_ref)):
                cols = slice(i * group + head * HD, i * group + (head + 1) * HD)
                kv_ref[i, 0] = k_ref[:, :, cols]
                kv_ref[i, 1] = v_ref[:, :, cols]
            out_ref[i] = q_ref[:, :, i * group : (i + 1) * group]

    spec = pl.BlockSpec((frames, tok, piece), lambda s: (0, 0, s))
    part = hidden.shape[-1] // PACK
    kv_spec = pl.BlockSpec((count, 2, frames, tok, HD), lambda s: (s, 0, 0, 0, 0))
    kv_shape = jax.ShapeDtypeStruct((SPATIAL, 2, frames, tok, HD), keys.dtype)
    return pl.pallas_call(
        kernel,
        grid=(PACK,),
        in_specs=[spec] * 3 + [pl.BlockSpec((1, tok, part), lambda s: (frames - 1, 0, s))],
        out_specs=[
            kv_spec,
            kv_spec,
            pl.BlockSpec((count, frames, tok, group), lambda s: (s, 0, 0, 0)),
            pl.BlockSpec((1, tok, part), lambda s: (0, 0, s)),
        ],
        out_shape=[
            kv_shape,
            kv_shape,
            jax.ShapeDtypeStruct((SPATIAL, frames, tok, group), queries.dtype),
            jax.ShapeDtypeStruct((1, *hidden.shape[1:]), hidden.dtype),
        ],
        compiler_params=LARGE,
        name="pack",
    )(queries, keys, values, hidden)


def hold(array, *earlier, room=1):
    def kernel(*refs):
        pass

    return pl.pallas_call(
        kernel,
        grid=(1,),
        in_specs=[ANY] + [corner(e) for e in earlier],
        out_specs=ANY,
        out_shape=jax.ShapeDtypeStruct(array.shape, array.dtype),
        input_output_aliases={0: 0},
        compiler_params=pltpu.CompilerParams(vmem_limit_bytes=room * 1024 * 1024),
        name="hold",
    )(array, *earlier)


def attend(frame, position, query, head, own, before, after, *earlier):
    groups, frames, tok, both = query.shape
    width = own.shape[-1]
    row_count = groups * tok
    groups_block = BLOCK_Q // tok
    blocks = row_count // BLOCK_Q
    asked = range(frames) if frame is None else (frame,)
    before_from = min(asked)
    before_count = frames - before_from
    after_count = max(asked) + 1
    loaded = before_count + frames + after_count

    def kernel(pos_ref, q_ref, own_ref, before_ref, after_ref, *rest):
        out_ref, token_ref, kt_ref, vx_ref = rest[-4:]
        sources = (
            [(before_ref, f) for f in range(before_count)]
            + [(own_ref, f) for f in range(frames)]
            + [(after_ref, f) for f in range(after_count)]
        )
        turn_frame = pl.program_id(0)

        @pl.when((turn_frame == 0) & (pl.program_id(1) == 0))
        def _():
            for at, (ref, f) in enumerate(sources):
                rows = slice(at * row_count, (at + 1) * row_count)
                turned = ref[:, 0, f].reshape(row_count, width).T
                kt_ref[:width, rows] = turned
                kt_ref[width:, rows] = turned
                vx_ref[rows, :width] = ref[:, 1, f].reshape(row_count, width)
                vx_ref[rows, width:] = jnp.ones((row_count, width), vx_ref.dtype)

        q = q_ref[:, 0].reshape(BLOCK_Q, width).astype(jnp.float32) * SCALE_LOG2
        high = q.astype(jnp.bfloat16)
        low = (q - high.astype(jnp.float32)).astype(jnp.bfloat16)
        q = jnp.concatenate((high, low), axis=1)
        position_now = pos_ref[0]

        def rows_of(step):
            start = (turn_frame + step) * row_count
            return pl.ds(pl.multiple_of(start, row_count), row_count)

        def scores(step):
            return jnp.dot(q, kt_ref[:, rows_of(step)], preferred_element_type=jnp.float32)

        top = jnp.full((BLOCK_Q, 1), NEG_FILL, jnp.float32)
        total = jnp.zeros((BLOCK_Q, 2 * width), jnp.float32)
        order = (2, 1, 3, 0, 4)
        ahead = scores(order[0])
        for turn, step in enumerate(order):
            s = ahead
            if turn + 1 < SPAN:
                ahead = scores(order[turn + 1])
            at = turn_frame + step
            absent = ((position_now == 0) & (at < before_count)) | (
                (position_now == QUEUE - 1) & (at >= before_count + frames)
            )
            peak = jnp.max(s, axis=1, keepdims=True)
            peak = jnp.where(absent, NEG_FILL, peak)
            lifted_top = jnp.maximum(top, peak)
            less = jnp.where(absent, -NEG_FILL, lifted_top)
            weights = jnp.exp2(s - less).astype(jnp.bfloat16)
            part = jnp.dot(weights, vx_ref[rows_of(step)], preferred_element_type=jnp.float32)
            total = total * jnp.exp2(top - lifted_top) + part
            top = lifted_top
        result = total[:, :width] / total[:, width:]
        out_ref[:, 0] = result.astype(out_ref.dtype).reshape(groups_block, tok, width)
        token_ref[...] = jnp.zeros_like(token_ref)

    first = asked[0]
    in_specs = [
        pl.BlockSpec((groups_block, 1, tok, width), lambda f, b, pos: (b, first + f, 0, head)),
        pl.BlockSpec(own.shape, lambda f, b, pos: (0, 0, 0, 0, 0)),
        pl.BlockSpec(
            (groups, 2, before_count, tok, width),
            lambda f, b, pos: (0, 0, before_from // before_count, 0, 0),
        ),
        pl.BlockSpec((groups, 2, after_count, tok, width), lambda f, b, pos: (0, 0, 0, 0, 0)),
    ]
    return pl.pallas_call(
        kernel,
        grid_spec=pltpu.PrefetchScalarGridSpec(
            num_scalar_prefetch=1,
            grid=(len(asked), blocks),
            in_specs=in_specs + [corner(e) for e in earlier],
            out_specs=[
                pl.BlockSpec((groups_block, 1, tok, width), lambda f, b, pos: (b, f, 0, 0)),
                pl.BlockSpec(TOKEN, lambda f, b, pos: (0, 0)),
            ],
            scratch_shapes=[
                pltpu.VMEM((2 * width, loaded * row_count), jnp.bfloat16),
                pltpu.VMEM((loaded * row_count, 2 * width), jnp.bfloat16),
            ],
        ),
        out_shape=[
            jax.ShapeDtypeStruct((groups, len(asked), tok, width), query.dtype),
            jax.ShapeDtypeStruct(TOKEN, jnp.float32),
        ],
        compiler_params=pltpu.CompilerParams(vmem_limit_bytes=VMEM),
        cost_estimate=pl.CostEstimate(
            flops=len(asked) * row_count * SPAN * row_count * width * 8,
            bytes_accessed=4 * 1024 * 1024,
            transcendentals=len(asked) * row_count * SPAN * row_count,
        ),
        name="attend",
    )(position, query, own, before, after, *earlier)


def project(head, place, sources, weight_own, weight_pair, partial, gates, *earlier):
    mine = sources[0]
    groups, frames, tok, width = mine.shape
    steps, sides, halves, rows_dev, cols_dev = weight_own.shape
    half = steps * sides
    rows = frames * tok
    last = partial is not None

    def kernel(place_ref, mine_ref, left_ref, right_ref, low_ref, high_ref, wo_ref, wp_ref, *rest):
        out_ref, a_ref = rest[-2:]
        x, core = place_ref[0], place_ref[1]

        @pl.when(pl.program_id(0) == 0)
        def _():
            for i in range(half):
                z, side = i // sides, i % sides
                for part in range(CORES):
                    group = side * half + CORES * z + (core if part == 0 else 1 - core)
                    cols = slice((part * half + i) * width, (part * half + i + 1) * width)
                    far = high_ref[group - half] if side else low_ref[group]
                    a_ref[0:rows, cols] = mine_ref[group].reshape(rows, width)
                    a_ref[rows : 2 * rows, cols] = right_ref[group].reshape(rows, width)
                    a_ref[2 * rows : 3 * rows, cols] = far.reshape(rows, width)
                    a_ref[3 * rows :, cols] = left_ref[group].reshape(rows, width)

        total = jnp.dot(
            a_ref[:, : half * width],
            wo_ref[:, :, 0].reshape(half * width, cols_dev),
            preferred_element_type=jnp.float32,
        )
        total += jnp.dot(
            a_ref[:, half * width :],
            wp_ref[:, :, 0].reshape(half * width, cols_dev),
            preferred_element_type=jnp.float32,
        )
        if not last:
            out_ref[0] = total
            return
        total += rest[0][0]
        gates_ref = rest[1]
        for source in range(RING):
            at = lax.rem(x + source, RING)
            for f in range(frames):
                gate = gates_ref[0, pl.ds(at * frames + f, 1), :]
                start = source * rows + f * tok
                slot = at * frames + 1 if f == 0 else lax.rem(at + 1, RING) * frames
                out_ref[slot, 0] = (gate * total[start : start + tok]).astype(out_ref.dtype)

    def whole(array):
        return pl.BlockSpec(array.shape, lambda n, place: (0,) * array.ndim)

    weight = pl.BlockSpec(
        (steps, sides, 1, width, cols_dev), lambda n, place: (0, 0, n, head, 0)
    )
    partial_spec = pl.BlockSpec((1, RING * rows, cols_dev), lambda n, place: (n, 0, 0))
    in_specs = [*map(whole, sources), weight, weight]
    operands = [*sources, weight_own, weight_pair]
    if last:
        in_specs += [partial_spec, pl.BlockSpec((1,) + gates.shape[1:], lambda n, place: (n, 0, 0))]
        operands += [partial, gates]
        out_spec = pl.BlockSpec((RING * frames, 1, tok, cols_dev), lambda n, place: (0, n, 0, 0))
        out_shape = jax.ShapeDtypeStruct((RING * frames, halves, tok, cols_dev), jnp.bfloat16)
    else:
        out_spec = partial_spec
        out_shape = jax.ShapeDtypeStruct((halves, RING * rows, cols_dev), jnp.float32)
    return pl.pallas_call(
        kernel,
        grid_spec=pltpu.PrefetchScalarGridSpec(
            num_scalar_prefetch=1,
            grid=(halves,),
            in_specs=in_specs + [corner(e) for e in earlier],
            out_specs=out_spec,
            scratch_shapes=[pltpu.VMEM((RING * rows, groups * width), jnp.bfloat16)],
        ),
        out_shape=out_shape,
        compiler_params=pltpu.CompilerParams(vmem_limit_bytes=48 * 1024 * 1024),
        cost_estimate=pl.CostEstimate(
            flops=2 * RING * rows * groups * width * halves * cols_dev,
            bytes_accessed=8 * 1024 * 1024,
            transcendentals=0,
        ),
        name="project_last" if last else "project_first",
    )(place, *operands, *earlier)


def add_branch(position, branch, hidden, shifted, entering):
    sources, frames, halves, tok, cols = branch.shape
    width = hidden.shape[-1]

    def kernel(pos_ref, b_ref, hidden_ref, shifted_ref, entering_ref, out_ref):
        def add(base_ref, replaced):
            for half in range(halves):
                for source in range(sources):
                    start = (half * sources + source) * cols
                    at = slice(start, start + cols)
                    value = base_ref[0, :, at].astype(jnp.float32)
                    value += b_ref[source, 0, half].astype(jnp.float32)
                    if replaced:
                        value = jnp.where(
                            pos_ref[0] == 0, entering_ref[:, at].astype(jnp.float32), value
                        )
                    out_ref[0, :, at] = value.astype(out_ref.dtype)

        @pl.when(pl.program_id(0) == 0)
        def _():
            add(shifted_ref, True)

        @pl.when(pl.program_id(0) == 1)
        def _():
            add(hidden_ref, False)

    frame_spec = pl.BlockSpec((1, tok, width), lambda i, pos: (0, 0, 0))
    return pl.pallas_call(
        kernel,
        grid_spec=pltpu.PrefetchScalarGridSpec(
            num_scalar_prefetch=1,
            grid=(frames,),
            in_specs=[
                pl.BlockSpec((sources, 1, halves, tok, cols), lambda i, pos: (0, i, 0, 0, 0)),
                frame_spec,
                frame_spec,
                pl.BlockSpec((tok, width), lambda i, pos: (0, 0)),
            ],
            out_specs=pl.BlockSpec((1, tok, width), lambda i, pos: (i, 0, 0)),
        ),
        out_shape=jax.ShapeDtypeStruct((frames, tok, width), hidden.dtype),
        compiler_params=MEDIUM,
        name="add_branch",
    )(position, branch, hidden, shifted, entering)


def body(hidden, queries, keys, values, out_weight, gate_table, levels, entering):
    frames = queries.shape[0]
    position = lax.axis_index("queue")
    spatial = lax.axis_index("spatial")
    y_low, x = position // RING, position % RING
    core = spatial % CORES
    position_now = position.astype(jnp.int32)[None]
    place = jnp.stack((x, core)).astype(jnp.int32)

    up = [(p, p + 1) for p in range(QUEUE - 1)]
    down = [(p + 1, p) for p in range(QUEUE - 1)]
    ring = [[r * RING + i for i in range(RING)] for r in range(QUEUE // RING)]
    ring_up = [(g[i], g[(i + 1) % RING]) for g in ring for i in range(RING)]
    ring_down = [(g[(i + 1) % RING], g[i]) for g in ring for i in range(RING)]
    swap_low = [(p, (p + RING) % QUEUE) for p in range(QUEUE)]
    swap_core = [(s, s ^ 1) for s in range(SPATIAL)]
    along_y = [
        [(low * RING + i) * SPATIAL + side * (SPATIAL // 2) + r for side in range(2) for low in range(2)]
        for i in range(RING)
        for r in range(SPATIAL // 2)
    ]
    along_z = [
        [side * (SPATIAL // 2) + z * CORES + c for z in range(SPATIAL // 2 // CORES)]
        for side in range(2)
        for c in range(CORES)
    ]

    to_heads = functools.partial(
        lax.all_to_all, axis_name="spatial", split_axis=0, concat_axis=0, tiled=True
    )

    selector = (levels[:, None] == jnp.arange(gate_table.shape[0], dtype=jnp.int32)[None, :]).astype(
        jnp.float32
    )
    gates = jnp.dot(
        selector, gate_table, precision=lax.Precision.HIGHEST, preferred_element_type=jnp.float32
    )
    other_gates = lax.ppermute(gates, "queue", swap_low)
    gates = jnp.where(y_low == 0, jnp.stack((gates, other_gates)), jnp.stack((other_gates, gates)))
    count = RING * frames
    is_last = (jnp.arange(count, dtype=jnp.int32) == count - 1)[None, :, None] & (y_low == 1)
    gates = jnp.where(
        is_last,
        gates[:, count - 1 : count],
        lax.dynamic_slice_in_dim(gates, y_low * count, count, axis=1),
    )

    kv0, kv1, query, last_frame = pack(queries, keys, values, hidden)
    kv0 = to_heads(kv0)
    kv1_heads = to_heads(hold(kv1, kv0, gates))
    query = to_heads(hold(query, kv1_heads))
    kv0 = hold(kv0, query)
    kv0_before, kv0_after = lax.ppermute(kv0, "queue", up), lax.ppermute(kv0, "queue", down)
    kv1 = hold(kv1_heads, query)
    kv1_before, kv1_after = lax.ppermute(kv1, "queue", up), lax.ppermute(kv1, "queue", down)

    weight = lax.all_gather(out_weight, ("queue", "spatial"), axis_index_groups=along_y, axis=0)
    weight = hold(weight, query, room=56)
    weight = lax.all_gather(weight, "spatial", axis_index_groups=along_z, axis=0)
    weight = weight.reshape(-1, 2, 2, *out_weight.shape)

    cross = [(RING - 1, QUEUE - 1)]

    def with_crossing(even, odd, crossing):
        odd = jnp.where(position == QUEUE - 1, crossing, odd)
        return jnp.concatenate((even, odd), axis=1)

    def spread(mine):
        left = lax.ppermute(mine, "queue", ring_up)
        right = lax.ppermute(mine, "queue", ring_down)
        far_low = lax.ppermute(left[: SPATIAL // 2], "queue", ring_up)
        far_high = lax.ppermute(right[SPATIAL // 2 :], "queue", ring_down)
        return mine, left, right, far_low, far_high

    head0 = (position_now, query, 0, kv0, kv0_before, kv0_after)
    head1 = (position_now, query, 1, kv1, kv1_before, kv1_after)
    odd0, token = attend(1, *head0)
    odd0_crossing = lax.ppermute(odd0, "queue", cross)
    even0, token = attend(0, *head0, token)
    first = with_crossing(even0, odd0, odd0_crossing)
    odd1, token = attend(1, *head1, token, first)
    odd1_crossing = lax.ppermute(odd1, "queue", cross)
    first = hold(to_heads(first), token)
    first_sources = spread(first)
    shifted = lax.ppermute(hold(last_frame, kv1_before, token), "queue", up)
    even1, token = attend(0, *head1, token, first)
    weight_own = hold(weight, token, room=56)
    weight_pair = lax.ppermute(weight_own, "spatial", swap_core)
    second = to_heads(with_crossing(even1, odd1, odd1_crossing))
    second_sources = spread(hold(second, shifted))

    partial = project(0, place, first_sources, weight_own, weight_pair, None, None)
    branch = project(1, place, second_sources, weight_own, weight_pair, partial, gates)
    branch = lax.all_to_all(
        branch, "queue", split_axis=0, concat_axis=0, axis_index_groups=ring, tiled=True
    )
    branch = branch.reshape(RING, frames, *branch.shape[1:])
    return add_branch(position_now, branch, hidden, shifted, entering)


def solution(mesh):
    return jax.shard_map(
        body,
        mesh=mesh,
        in_specs=(
            P("queue", "spatial", None),
            P("queue", "spatial", None),
            P("queue", "spatial", None),
            P("queue", "spatial", None),
            P("spatial", "queue"),
            P(None, "queue"),
            P(),
            P("spatial", None),
        ),
        out_specs=P("queue", "spatial", None),
        check_vma=False,
    )
```

```python
import functools

import jax
import jax.numpy as jnp
from jax import lax
from jax.experimental import pallas as pl
from jax.experimental.pallas import tpu as pltpu
from jax.sharding import PartitionSpec as P

HEADS = 32
HD = 128
WMAX = 2
NEG_FILL = -1e30
SCALE_LOG2 = (HD ** -0.5) * 1.4426950408889634
BLOCK_Q = 512
VMEM = 28 * 1024 * 1024
LARGE = pltpu.CompilerParams(vmem_limit_bytes=58 * 1024 * 1024)
MEDIUM = pltpu.CompilerParams(vmem_limit_bytes=12 * 1024 * 1024)
QUEUE = 8
RING = 4
SPATIAL = 16
CORES = 2
PACK = 4
SPAN = 2 * WMAX + 1
ANY = pl.BlockSpec(memory_space=pl.ANY)
TOKEN = (8, 128)


def corner(array):
    rows = 8 if array.dtype == jnp.float32 else 16
    block = (1,) * (array.ndim - 2) + (rows, 128)
    return pl.BlockSpec(block, lambda *at: (0,) * array.ndim)


def pack(queries, keys, values, hidden):
    frames, tok, width = keys.shape
    group = width // SPATIAL
    piece = width // PACK
    count = SPATIAL // PACK

    def kernel(q_ref, k_ref, v_ref, hidden_ref, kv0_ref, kv1_ref, out_ref, last_ref):
        last_ref[...] = hidden_ref[...]
        for i in range(count):
            for head, kv_ref in enumerate((kv0_ref, kv1_ref)):
                cols = slice(i * group + head * HD, i * group + (head + 1) * HD)
                kv_ref[i, 0] = k_ref[:, :, cols]
                kv_ref[i, 1] = v_ref[:, :, cols]
            out_ref[i] = q_ref[:, :, i * group : (i + 1) * group]

    spec = pl.BlockSpec((frames, tok, piece), lambda s: (0, 0, s))
    part = hidden.shape[-1] // PACK
    kv_spec = pl.BlockSpec((count, 2, frames, tok, HD), lambda s: (s, 0, 0, 0, 0))
    kv_shape = jax.ShapeDtypeStruct((SPATIAL, 2, frames, tok, HD), keys.dtype)
    return pl.pallas_call(
        kernel,
        grid=(PACK,),
        in_specs=[spec] * 3 + [pl.BlockSpec((1, tok, part), lambda s: (frames - 1, 0, s))],
        out_specs=[
            kv_spec,
            kv_spec,
            pl.BlockSpec((count, frames, tok, group), lambda s: (s, 0, 0, 0)),
            pl.BlockSpec((1, tok, part), lambda s: (0, 0, s)),
        ],
        out_shape=[
            kv_shape,
            kv_shape,
            jax.ShapeDtypeStruct((SPATIAL, frames, tok, group), queries.dtype),
            jax.ShapeDtypeStruct((1, *hidden.shape[1:]), hidden.dtype),
        ],
        compiler_params=LARGE,
        name="pack",
    )(queries, keys, values, hidden)


def hold(array, *earlier, room=1):
    def kernel(*refs):
        pass

    return pl.pallas_call(
        kernel,
        grid=(1,),
        in_specs=[ANY] + [corner(e) for e in earlier],
        out_specs=ANY,
        out_shape=jax.ShapeDtypeStruct(array.shape, array.dtype),
        input_output_aliases={0: 0},
        compiler_params=pltpu.CompilerParams(vmem_limit_bytes=room * 1024 * 1024),
        name="hold",
    )(array, *earlier)


def attend(frame, position, query, head, own, before, after, *earlier):
    groups, frames, tok, both = query.shape
    width = own.shape[-1]
    row_count = groups * tok
    groups_block = BLOCK_Q // tok
    blocks = row_count // BLOCK_Q
    asked = range(frames) if frame is None else (frame,)
    before_from = min(asked)
    before_count = frames - before_from
    after_count = max(asked) + 1
    loaded = before_count + frames + after_count

    def kernel(pos_ref, q_ref, own_ref, before_ref, after_ref, *rest):
        out_ref, token_ref, kt_ref, vx_ref = rest[-4:]
        sources = (
            [(before_ref, f) for f in range(before_count)]
            + [(own_ref, f) for f in range(frames)]
            + [(after_ref, f) for f in range(after_count)]
        )
        turn_frame = pl.program_id(0)

        @pl.when((turn_frame == 0) & (pl.program_id(1) == 0))
        def _():
            for at, (ref, f) in enumerate(sources):
                rows = slice(at * row_count, (at + 1) * row_count)
                turned = ref[:, 0, f].reshape(row_count, width).T
                kt_ref[:width, rows] = turned
                kt_ref[width:, rows] = turned
                vx_ref[rows, :width] = ref[:, 1, f].reshape(row_count, width)
                vx_ref[rows, width:] = jnp.ones((row_count, width), vx_ref.dtype)

        q = q_ref[:, 0].reshape(BLOCK_Q, width).astype(jnp.float32) * SCALE_LOG2
        high = q.astype(jnp.bfloat16)
        low = (q - high.astype(jnp.float32)).astype(jnp.bfloat16)
        q = jnp.concatenate((high, low), axis=1)
        position_now = pos_ref[0]

        def rows_of(step):
            start = (turn_frame + step) * row_count
            return pl.ds(pl.multiple_of(start, row_count), row_count)

        def scores(step):
            return jnp.dot(q, kt_ref[:, rows_of(step)], preferred_element_type=jnp.float32)

        top = jnp.full((BLOCK_Q, 1), NEG_FILL, jnp.float32)
        total = jnp.zeros((BLOCK_Q, 2 * width), jnp.float32)
        order = (2, 1, 3, 0, 4)
        ahead = scores(order[0])
        for turn, step in enumerate(order):
            s = ahead
            if turn + 1 < SPAN:
                ahead = scores(order[turn + 1])
            at = turn_frame + step
            absent = ((position_now == 0) & (at < before_count)) | (
                (position_now == QUEUE - 1) & (at >= before_count + frames)
            )
            peak = jnp.max(s, axis=1, keepdims=True)
            peak = jnp.where(absent, NEG_FILL, peak)
            lifted_top = jnp.maximum(top, peak)
            less = jnp.where(absent, -NEG_FILL, lifted_top)
            weights = jnp.exp2(s - less).astype(jnp.bfloat16)
            part = jnp.dot(weights, vx_ref[rows_of(step)], preferred_element_type=jnp.float32)
            total = total * jnp.exp2(top - lifted_top) + part
            top = lifted_top
        result = total[:, :width] / total[:, width:]
        out_ref[:, 0] = result.astype(out_ref.dtype).reshape(groups_block, tok, width)
        token_ref[...] = jnp.zeros_like(token_ref)

    first = asked[0]
    in_specs = [
        pl.BlockSpec((groups_block, 1, tok, width), lambda f, b, pos: (b, first + f, 0, head)),
        pl.BlockSpec(own.shape, lambda f, b, pos: (0, 0, 0, 0, 0)),
        pl.BlockSpec(
            (groups, 2, before_count, tok, width),
            lambda f, b, pos: (0, 0, before_from // before_count, 0, 0),
        ),
        pl.BlockSpec((groups, 2, after_count, tok, width), lambda f, b, pos: (0, 0, 0, 0, 0)),
    ]
    return pl.pallas_call(
        kernel,
        grid_spec=pltpu.PrefetchScalarGridSpec(
            num_scalar_prefetch=1,
            grid=(len(asked), blocks),
            in_specs=in_specs + [corner(e) for e in earlier],
            out_specs=[
                pl.BlockSpec((groups_block, 1, tok, width), lambda f, b, pos: (b, f, 0, 0)),
                pl.BlockSpec(TOKEN, lambda f, b, pos: (0, 0)),
            ],
            scratch_shapes=[
                pltpu.VMEM((2 * width, loaded * row_count), jnp.bfloat16),
                pltpu.VMEM((loaded * row_count, 2 * width), jnp.bfloat16),
            ],
        ),
        out_shape=[
            jax.ShapeDtypeStruct((groups, len(asked), tok, width), query.dtype),
            jax.ShapeDtypeStruct(TOKEN, jnp.float32),
        ],
        compiler_params=pltpu.CompilerParams(vmem_limit_bytes=VMEM),
        cost_estimate=pl.CostEstimate(
            flops=len(asked) * row_count * SPAN * row_count * width * 8,
            bytes_accessed=4 * 1024 * 1024,
            transcendentals=len(asked) * row_count * SPAN * row_count,
        ),
        name="attend",
    )(position, query, own, before, after, *earlier)


def project(head, place, sources, weight_own, weight_pair, partial, gates, *earlier):
    mine = sources[0]
    groups, frames, tok, width = mine.shape
    steps, sides, halves, rows_dev, cols_dev = weight_own.shape
    half = steps * sides
    rows = frames * tok
    last = partial is not None

    def kernel(place_ref, mine_ref, left_ref, right_ref, low_ref, high_ref, wo_ref, wp_ref, *rest):
        out_ref, a_ref = rest[-2:]
        x, core = place_ref[0], place_ref[1]

        @pl.when(pl.program_id(0) == 0)
        def _():
            for i in range(half):
                z, side = i // sides, i % sides
                for part in range(CORES):
                    group = side * half + CORES * z + (core if part == 0 else 1 - core)
                    cols = slice((part * half + i) * width, (part * half + i + 1) * width)
                    far = high_ref[group - half] if side else low_ref[group]
                    a_ref[0:rows, cols] = mine_ref[group].reshape(rows, width)
                    a_ref[rows : 2 * rows, cols] = right_ref[group].reshape(rows, width)
                    a_ref[2 * rows : 3 * rows, cols] = far.reshape(rows, width)
                    a_ref[3 * rows :, cols] = left_ref[group].reshape(rows, width)

        total = jnp.dot(
            a_ref[:, : half * width],
            wo_ref[:, :, 0].reshape(half * width, cols_dev),
            preferred_element_type=jnp.float32,
        )
        total += jnp.dot(
            a_ref[:, half * width :],
            wp_ref[:, :, 0].reshape(half * width, cols_dev),
            preferred_element_type=jnp.float32,
        )
        if not last:
            out_ref[0] = total
            return
        total += rest[0][0]
        gates_ref = rest[1]
        for source in range(RING):
            at = lax.rem(x + source, RING)
            for f in range(frames):
                gate = gates_ref[0, pl.ds(at * frames + f, 1), :]
                start = source * rows + f * tok
                slot = at * frames + 1 if f == 0 else lax.rem(at + 1, RING) * frames
                out_ref[slot, 0] = (gate * total[start : start + tok]).astype(out_ref.dtype)

    def whole(array):
        return pl.BlockSpec(array.shape, lambda n, place: (0,) * array.ndim)

    weight = pl.BlockSpec(
        (steps, sides, 1, width, cols_dev), lambda n, place: (0, 0, n, head, 0)
    )
    partial_spec = pl.BlockSpec((1, RING * rows, cols_dev), lambda n, place: (n, 0, 0))
    in_specs = [*map(whole, sources), weight, weight]
    operands = [*sources, weight_own, weight_pair]
    if last:
        in_specs += [partial_spec, pl.BlockSpec((1,) + gates.shape[1:], lambda n, place: (n, 0, 0))]
        operands += [partial, gates]
        out_spec = pl.BlockSpec((RING * frames, 1, tok, cols_dev), lambda n, place: (0, n, 0, 0))
        out_shape = jax.ShapeDtypeStruct((RING * frames, halves, tok, cols_dev), jnp.bfloat16)
    else:
        out_spec = partial_spec
        out_shape = jax.ShapeDtypeStruct((halves, RING * rows, cols_dev), jnp.float32)
    return pl.pallas_call(
        kernel,
        grid_spec=pltpu.PrefetchScalarGridSpec(
            num_scalar_prefetch=1,
            grid=(halves,),
            in_specs=in_specs + [corner(e) for e in earlier],
            out_specs=out_spec,
            scratch_shapes=[pltpu.VMEM((RING * rows, groups * width), jnp.bfloat16)],
        ),
        out_shape=out_shape,
        compiler_params=pltpu.CompilerParams(vmem_limit_bytes=48 * 1024 * 1024),
        cost_estimate=pl.CostEstimate(
            flops=2 * RING * rows * groups * width * halves * cols_dev,
            bytes_accessed=8 * 1024 * 1024,
            transcendentals=0,
        ),
        name="project_last" if last else "project_first",
    )(place, *operands, *earlier)


def add_branch(position, branch, hidden, shifted, entering):
    sources, frames, halves, tok, cols = branch.shape
    width = hidden.shape[-1]

    def kernel(pos_ref, b_ref, hidden_ref, shifted_ref, entering_ref, out_ref):
        def add(base_ref, replaced):
            for half in range(halves):
                for source in range(sources):
                    start = (half * sources + source) * cols
                    at = slice(start, start + cols)
                    value = base_ref[0, :, at].astype(jnp.float32)
                    value += b_ref[source, 0, half].astype(jnp.float32)
                    if replaced:
                        value = jnp.where(
                            pos_ref[0] == 0, entering_ref[:, at].astype(jnp.float32), value
                        )
                    out_ref[0, :, at] = value.astype(out_ref.dtype)

        @pl.when(pl.program_id(0) == 0)
        def _():
            add(shifted_ref, True)

        @pl.when(pl.program_id(0) == 1)
        def _():
            add(hidden_ref, False)

    frame_spec = pl.BlockSpec((1, tok, width), lambda i, pos: (0, 0, 0))
    return pl.pallas_call(
        kernel,
        grid_spec=pltpu.PrefetchScalarGridSpec(
            num_scalar_prefetch=1,
            grid=(frames,),
            in_specs=[
                pl.BlockSpec((sources, 1, halves, tok, cols), lambda i, pos: (0, i, 0, 0, 0)),
                frame_spec,
                frame_spec,
                pl.BlockSpec((tok, width), lambda i, pos: (0, 0)),
            ],
            out_specs=pl.BlockSpec((1, tok, width), lambda i, pos: (i, 0, 0)),
        ),
        out_shape=jax.ShapeDtypeStruct((frames, tok, width), hidden.dtype),
        compiler_params=MEDIUM,
        name="add_branch",
    )(position, branch, hidden, shifted, entering)


def body(hidden, queries, keys, values, out_weight, gate_table, levels, entering):
    frames = queries.shape[0]
    position = lax.axis_index("queue")
    spatial = lax.axis_index("spatial")
    y_low, x = position // RING, position % RING
    core = spatial % CORES
    position_now = position.astype(jnp.int32)[None]
    place = jnp.stack((x, core)).astype(jnp.int32)

    up = [(p, p + 1) for p in range(QUEUE - 1)]
    down = [(p + 1, p) for p in range(QUEUE - 1)]
    ring = [[r * RING + i for i in range(RING)] for r in range(QUEUE // RING)]
    ring_up = [(g[i], g[(i + 1) % RING]) for g in ring for i in range(RING)]
    ring_down = [(g[(i + 1) % RING], g[i]) for g in ring for i in range(RING)]
    swap_low = [(p, (p + RING) % QUEUE) for p in range(QUEUE)]
    swap_core = [(s, s ^ 1) for s in range(SPATIAL)]
    along_y = [
        [(low * RING + i) * SPATIAL + side * (SPATIAL // 2) + r for side in range(2) for low in range(2)]
        for i in range(RING)
        for r in range(SPATIAL // 2)
    ]
    along_z = [
        [side * (SPATIAL // 2) + z * CORES + c for z in range(SPATIAL // 2 // CORES)]
        for side in range(2)
        for c in range(CORES)
    ]

    to_heads = functools.partial(
        lax.all_to_all, axis_name="spatial", split_axis=0, concat_axis=0, tiled=True
    )

    selector = (levels[:, None] == jnp.arange(gate_table.shape[0], dtype=jnp.int32)[None, :]).astype(
        jnp.float32
    )
    gates = jnp.dot(
        selector, gate_table, precision=lax.Precision.HIGHEST, preferred_element_type=jnp.float32
    )
    other_gates = lax.ppermute(gates, "queue", swap_low)
    gates = jnp.where(y_low == 0, jnp.stack((gates, other_gates)), jnp.stack((other_gates, gates)))
    count = RING * frames
    is_last = (jnp.arange(count, dtype=jnp.int32) == count - 1)[None, :, None] & (y_low == 1)
    gates = jnp.where(
        is_last,
        gates[:, count - 1 : count],
        lax.dynamic_slice_in_dim(gates, y_low * count, count, axis=1),
    )

    kv0, kv1, query, last_frame = pack(queries, keys, values, hidden)
    kv0 = to_heads(kv0)
    kv1_heads = to_heads(hold(kv1, kv0, gates))
    query = to_heads(hold(query, kv1_heads))
    kv0 = hold(kv0, query)
    kv0_before, kv0_after = lax.ppermute(kv0, "queue", up), lax.ppermute(kv0, "queue", down)
    kv1 = hold(kv1_heads, query)
    kv1_before, kv1_after = lax.ppermute(kv1, "queue", up), lax.ppermute(kv1, "queue", down)

    weight = lax.all_gather(out_weight, ("queue", "spatial"), axis_index_groups=along_y, axis=0)
    weight = hold(weight, query, room=56)
    weight = lax.all_gather(weight, "spatial", axis_index_groups=along_z, axis=0)
    weight = weight.reshape(-1, 2, 2, *out_weight.shape)

    cross = [(RING - 1, QUEUE - 1)]

    def with_crossing(even, odd, crossing):
        odd = jnp.where(position == QUEUE - 1, crossing, odd)
        return jnp.concatenate((even, odd), axis=1)

    def spread(mine):
        left = lax.ppermute(mine, "queue", ring_up)
        right = lax.ppermute(mine, "queue", ring_down)
        far_low = lax.ppermute(left[: SPATIAL // 2], "queue", ring_up)
        far_high = lax.ppermute(right[SPATIAL // 2 :], "queue", ring_down)
        return mine, left, right, far_low, far_high

    head0 = (position_now, query, 0, kv0, kv0_before, kv0_after)
    head1 = (position_now, query, 1, kv1, kv1_before, kv1_after)
    odd0, token = attend(1, *head0)
    odd0_crossing = lax.ppermute(odd0, "queue", cross)
    even0, token = attend(0, *head0, token)
    first = with_crossing(even0, odd0, odd0_crossing)
    odd1, token = attend(1, *head1, token, first)
    odd1_crossing = lax.ppermute(odd1, "queue", cross)
    first = hold(to_heads(first), token)
    first_sources = spread(first)
    shifted = lax.ppermute(hold(last_frame, kv1_before, token), "queue", up)
    even1, token = attend(0, *head1, token, first)
    weight_own = hold(weight, token, room=56)
    weight_pair = lax.ppermute(weight_own, "spatial", swap_core)
    second = with_crossing(even1, odd1, odd1_crossing)
    second = to_heads(hold(second, *first_sources[1:3]))
    second_sources = spread(hold(second, shifted, *first_sources[3:]))

    partial = project(0, place, first_sources, weight_own, weight_pair, None, None)
    branch = project(1, place, second_sources, weight_own, weight_pair, partial, gates)
    branch = lax.all_to_all(
        branch, "queue", split_axis=0, concat_axis=0, axis_index_groups=ring, tiled=True
    )
    branch = branch.reshape(RING, frames, *branch.shape[1:])
    return add_branch(position_now, branch, hidden, shifted, entering)


def solution(mesh):
    return jax.shard_map(
        body,
        mesh=mesh,
        in_specs=(
            P("queue", "spatial", None),
            P("queue", "spatial", None),
            P("queue", "spatial", None),
            P("queue", "spatial", None),
            P("spatial", "queue"),
            P(None, "queue"),
            P(),
            P("spatial", None),
        ),
        out_specs=P("queue", "spatial", None),
        check_vma=False,
    )
```

```python
import functools

import jax
import jax.numpy as jnp
from jax import lax
from jax.experimental import pallas as pl
from jax.experimental.pallas import tpu as pltpu
from jax.sharding import PartitionSpec as P

HEADS = 32
HD = 128
WMAX = 2
NEG_FILL = -1e30
SCALE_LOG2 = (HD ** -0.5) * 1.4426950408889634
BLOCK_Q = 512
VMEM = 28 * 1024 * 1024
LARGE = pltpu.CompilerParams(vmem_limit_bytes=58 * 1024 * 1024)
MEDIUM = pltpu.CompilerParams(vmem_limit_bytes=12 * 1024 * 1024)
QUEUE = 8
RING = 4
SPATIAL = 16
CORES = 2
PACK = 4
SPAN = 2 * WMAX + 1
ANY = pl.BlockSpec(memory_space=pl.ANY)
TOKEN = (8, 128)


def corner(array):
    rows = 8 if array.dtype == jnp.float32 else 16
    block = (1,) * (array.ndim - 2) + (rows, 128)
    return pl.BlockSpec(block, lambda *at: (0,) * array.ndim)


def pack(queries, keys, values, hidden):
    frames, tok, width = keys.shape
    group = width // SPATIAL
    piece = width // PACK
    count = SPATIAL // PACK

    def kernel(q_ref, k_ref, v_ref, hidden_ref, kv0_ref, kv1_ref, out_ref, last_ref):
        last_ref[...] = hidden_ref[...]
        for i in range(count):
            for head, kv_ref in enumerate((kv0_ref, kv1_ref)):
                cols = slice(i * group + head * HD, i * group + (head + 1) * HD)
                kv_ref[i, 0] = k_ref[:, :, cols]
                kv_ref[i, 1] = v_ref[:, :, cols]
            out_ref[i] = q_ref[:, :, i * group : (i + 1) * group]

    spec = pl.BlockSpec((frames, tok, piece), lambda s: (0, 0, s))
    part = hidden.shape[-1] // PACK
    kv_spec = pl.BlockSpec((count, 2, frames, tok, HD), lambda s: (s, 0, 0, 0, 0))
    kv_shape = jax.ShapeDtypeStruct((SPATIAL, 2, frames, tok, HD), keys.dtype)
    return pl.pallas_call(
        kernel,
        grid=(PACK,),
        in_specs=[spec] * 3 + [pl.BlockSpec((1, tok, part), lambda s: (frames - 1, 0, s))],
        out_specs=[
            kv_spec,
            kv_spec,
            pl.BlockSpec((count, frames, tok, group), lambda s: (s, 0, 0, 0)),
            pl.BlockSpec((1, tok, part), lambda s: (0, 0, s)),
        ],
        out_shape=[
            kv_shape,
            kv_shape,
            jax.ShapeDtypeStruct((SPATIAL, frames, tok, group), queries.dtype),
            jax.ShapeDtypeStruct((1, *hidden.shape[1:]), hidden.dtype),
        ],
        compiler_params=LARGE,
        name="pack",
    )(queries, keys, values, hidden)


def hold(array, *earlier, room=1):
    def kernel(*refs):
        pass

    return pl.pallas_call(
        kernel,
        grid=(1,),
        in_specs=[ANY] + [corner(e) for e in earlier],
        out_specs=ANY,
        out_shape=jax.ShapeDtypeStruct(array.shape, array.dtype),
        input_output_aliases={0: 0},
        compiler_params=pltpu.CompilerParams(vmem_limit_bytes=room * 1024 * 1024),
        name="hold",
    )(array, *earlier)


def attend(frame, position, query, head, own, before, after, *earlier):
    groups, frames, tok, both = query.shape
    width = own.shape[-1]
    row_count = groups * tok
    groups_block = BLOCK_Q // tok
    blocks = row_count // BLOCK_Q
    asked = range(frames) if frame is None else (frame,)
    before_from = min(asked)
    before_count = frames - before_from
    after_count = max(asked) + 1
    loaded = before_count + frames + after_count

    def kernel(pos_ref, q_ref, own_ref, before_ref, after_ref, *rest):
        out_ref, token_ref, kt_ref, vx_ref = rest[-4:]
        sources = (
            [(before_ref, f) for f in range(before_count)]
            + [(own_ref, f) for f in range(frames)]
            + [(after_ref, f) for f in range(after_count)]
        )
        turn_frame = pl.program_id(0)

        @pl.when((turn_frame == 0) & (pl.program_id(1) == 0))
        def _():
            for at, (ref, f) in enumerate(sources):
                rows = slice(at * row_count, (at + 1) * row_count)
                turned = ref[:, 0, f].reshape(row_count, width).T
                kt_ref[:width, rows] = turned
                kt_ref[width:, rows] = turned
                vx_ref[rows, :width] = ref[:, 1, f].reshape(row_count, width)
                vx_ref[rows, width:] = jnp.ones((row_count, width), vx_ref.dtype)

        q = q_ref[:, 0].reshape(BLOCK_Q, width).astype(jnp.float32) * SCALE_LOG2
        high = q.astype(jnp.bfloat16)
        low = (q - high.astype(jnp.float32)).astype(jnp.bfloat16)
        q = jnp.concatenate((high, low), axis=1)
        position_now = pos_ref[0]

        def rows_of(step):
            start = (turn_frame + step) * row_count
            return pl.ds(pl.multiple_of(start, row_count), row_count)

        def scores(step):
            return jnp.dot(q, kt_ref[:, rows_of(step)], preferred_element_type=jnp.float32)

        top = jnp.full((BLOCK_Q, 1), NEG_FILL, jnp.float32)
        total = jnp.zeros((BLOCK_Q, 2 * width), jnp.float32)
        order = (2, 1, 3, 0, 4)
        ahead = scores(order[0])
        for turn, step in enumerate(order):
            s = ahead
            if turn + 1 < SPAN:
                ahead = scores(order[turn + 1])
            at = turn_frame + step
            absent = ((position_now == 0) & (at < before_count)) | (
                (position_now == QUEUE - 1) & (at >= before_count + frames)
            )
            peak = jnp.max(s, axis=1, keepdims=True)
            peak = jnp.where(absent, NEG_FILL, peak)
            lifted_top = jnp.maximum(top, peak)
            less = jnp.where(absent, -NEG_FILL, lifted_top)
            weights = jnp.exp2(s - less).astype(jnp.bfloat16)
            part = jnp.dot(weights, vx_ref[rows_of(step)], preferred_element_type=jnp.float32)
            total = total * jnp.exp2(top - lifted_top) + part
            top = lifted_top
        result = total[:, :width] / total[:, width:]
        out_ref[:, 0] = result.astype(out_ref.dtype).reshape(groups_block, tok, width)
        token_ref[...] = jnp.zeros_like(token_ref)

    first = asked[0]
    in_specs = [
        pl.BlockSpec((groups_block, 1, tok, width), lambda f, b, pos: (b, first + f, 0, head)),
        pl.BlockSpec(own.shape, lambda f, b, pos: (0, 0, 0, 0, 0)),
        pl.BlockSpec(
            (groups, 2, before_count, tok, width),
            lambda f, b, pos: (0, 0, before_from // before_count, 0, 0),
        ),
        pl.BlockSpec((groups, 2, after_count, tok, width), lambda f, b, pos: (0, 0, 0, 0, 0)),
    ]
    return pl.pallas_call(
        kernel,
        grid_spec=pltpu.PrefetchScalarGridSpec(
            num_scalar_prefetch=1,
            grid=(len(asked), blocks),
            in_specs=in_specs + [corner(e) for e in earlier],
            out_specs=[
                pl.BlockSpec((groups_block, 1, tok, width), lambda f, b, pos: (b, f, 0, 0)),
                pl.BlockSpec(TOKEN, lambda f, b, pos: (0, 0)),
            ],
            scratch_shapes=[
                pltpu.VMEM((2 * width, loaded * row_count), jnp.bfloat16),
                pltpu.VMEM((loaded * row_count, 2 * width), jnp.bfloat16),
            ],
        ),
        out_shape=[
            jax.ShapeDtypeStruct((groups, len(asked), tok, width), query.dtype),
            jax.ShapeDtypeStruct(TOKEN, jnp.float32),
        ],
        compiler_params=pltpu.CompilerParams(vmem_limit_bytes=VMEM),
        cost_estimate=pl.CostEstimate(
            flops=len(asked) * row_count * SPAN * row_count * width * 8,
            bytes_accessed=4 * 1024 * 1024,
            transcendentals=len(asked) * row_count * SPAN * row_count,
        ),
        name="attend",
    )(position, query, own, before, after, *earlier)


def project(head, place, sources, weight_own, weight_pair, partial, gates, *earlier):
    mine = sources[0]
    groups, frames, tok, width = mine.shape
    steps, sides, halves, rows_dev, cols_dev = weight_own.shape
    half = steps * sides
    rows = frames * tok
    last = partial is not None

    def kernel(place_ref, mine_ref, left_ref, right_ref, low_ref, high_ref, wo_ref, wp_ref, *rest):
        out_ref, a_ref = rest[-2:]
        x, core = place_ref[0], place_ref[1]

        @pl.when(pl.program_id(0) == 0)
        def _():
            for i in range(half):
                z, side = i // sides, i % sides
                for part in range(CORES):
                    group = side * half + CORES * z + (core if part == 0 else 1 - core)
                    cols = slice((part * half + i) * width, (part * half + i + 1) * width)
                    far = high_ref[group - half] if side else low_ref[group]
                    a_ref[0:rows, cols] = mine_ref[group].reshape(rows, width)
                    a_ref[rows : 2 * rows, cols] = right_ref[group].reshape(rows, width)
                    a_ref[2 * rows : 3 * rows, cols] = far.reshape(rows, width)
                    a_ref[3 * rows :, cols] = left_ref[group].reshape(rows, width)

        total = jnp.dot(
            a_ref[:, : half * width],
            wo_ref[:, :, 0].reshape(half * width, cols_dev),
            preferred_element_type=jnp.float32,
        )
        total += jnp.dot(
            a_ref[:, half * width :],
            wp_ref[:, :, 0].reshape(half * width, cols_dev),
            preferred_element_type=jnp.float32,
        )
        if not last:
            out_ref[0] = total
            return
        total += rest[0][0]
        gates_ref = rest[1]
        for source in range(RING):
            at = lax.rem(x + source, RING)
            for f in range(frames):
                gate = gates_ref[0, pl.ds(at * frames + f, 1), :]
                start = source * rows + f * tok
                slot = at * frames + 1 if f == 0 else lax.rem(at + 1, RING) * frames
                out_ref[slot, 0] = (gate * total[start : start + tok]).astype(out_ref.dtype)

    def whole(array):
        return pl.BlockSpec(array.shape, lambda n, place: (0,) * array.ndim)

    weight = pl.BlockSpec(
        (steps, sides, 1, width, cols_dev), lambda n, place: (0, 0, n, head, 0)
    )
    partial_spec = pl.BlockSpec((1, RING * rows, cols_dev), lambda n, place: (n, 0, 0))
    in_specs = [*map(whole, sources), weight, weight]
    operands = [*sources, weight_own, weight_pair]
    if last:
        in_specs += [partial_spec, pl.BlockSpec((1,) + gates.shape[1:], lambda n, place: (n, 0, 0))]
        operands += [partial, gates]
        out_spec = pl.BlockSpec((RING * frames, 1, tok, cols_dev), lambda n, place: (0, n, 0, 0))
        out_shape = jax.ShapeDtypeStruct((RING * frames, halves, tok, cols_dev), jnp.bfloat16)
    else:
        out_spec = partial_spec
        out_shape = jax.ShapeDtypeStruct((halves, RING * rows, cols_dev), jnp.float32)
    return pl.pallas_call(
        kernel,
        grid_spec=pltpu.PrefetchScalarGridSpec(
            num_scalar_prefetch=1,
            grid=(halves,),
            in_specs=in_specs + [corner(e) for e in earlier],
            out_specs=out_spec,
            scratch_shapes=[pltpu.VMEM((RING * rows, groups * width), jnp.bfloat16)],
        ),
        out_shape=out_shape,
        compiler_params=pltpu.CompilerParams(vmem_limit_bytes=48 * 1024 * 1024),
        cost_estimate=pl.CostEstimate(
            flops=2 * RING * rows * groups * width * halves * cols_dev,
            bytes_accessed=8 * 1024 * 1024,
            transcendentals=0,
        ),
        name="project_last" if last else "project_first",
    )(place, *operands, *earlier)


def add_branch(position, branch, hidden, shifted, entering):
    sources, frames, halves, tok, cols = branch.shape
    width = hidden.shape[-1]

    def kernel(pos_ref, b_ref, hidden_ref, shifted_ref, entering_ref, out_ref):
        def add(base_ref, replaced):
            for half in range(halves):
                for source in range(sources):
                    start = (half * sources + source) * cols
                    at = slice(start, start + cols)
                    value = base_ref[0, :, at].astype(jnp.float32)
                    value += b_ref[source, 0, half].astype(jnp.float32)
                    if replaced:
                        value = jnp.where(
                            pos_ref[0] == 0, entering_ref[:, at].astype(jnp.float32), value
                        )
                    out_ref[0, :, at] = value.astype(out_ref.dtype)

        @pl.when(pl.program_id(0) == 0)
        def _():
            add(shifted_ref, True)

        @pl.when(pl.program_id(0) == 1)
        def _():
            add(hidden_ref, False)

    frame_spec = pl.BlockSpec((1, tok, width), lambda i, pos: (0, 0, 0))
    return pl.pallas_call(
        kernel,
        grid_spec=pltpu.PrefetchScalarGridSpec(
            num_scalar_prefetch=1,
            grid=(frames,),
            in_specs=[
                pl.BlockSpec((sources, 1, halves, tok, cols), lambda i, pos: (0, i, 0, 0, 0)),
                frame_spec,
                frame_spec,
                pl.BlockSpec((tok, width), lambda i, pos: (0, 0)),
            ],
            out_specs=pl.BlockSpec((1, tok, width), lambda i, pos: (i, 0, 0)),
        ),
        out_shape=jax.ShapeDtypeStruct((frames, tok, width), hidden.dtype),
        compiler_params=MEDIUM,
        name="add_branch",
    )(position, branch, hidden, shifted, entering)


def body(hidden, queries, keys, values, out_weight, gate_table, levels, entering):
    frames = queries.shape[0]
    position = lax.axis_index("queue")
    spatial = lax.axis_index("spatial")
    y_low, x = position // RING, position % RING
    core = spatial % CORES
    position_now = position.astype(jnp.int32)[None]
    place = jnp.stack((x, core)).astype(jnp.int32)

    up = [(p, p + 1) for p in range(QUEUE - 1)]
    down = [(p + 1, p) for p in range(QUEUE - 1)]
    ring = [[r * RING + i for i in range(RING)] for r in range(QUEUE // RING)]
    ring_up = [(g[i], g[(i + 1) % RING]) for g in ring for i in range(RING)]
    ring_down = [(g[(i + 1) % RING], g[i]) for g in ring for i in range(RING)]
    swap_low = [(p, (p + RING) % QUEUE) for p in range(QUEUE)]
    swap_core = [(s, s ^ 1) for s in range(SPATIAL)]
    along_y = [
        [(low * RING + i) * SPATIAL + side * (SPATIAL // 2) + r for side in range(2) for low in range(2)]
        for i in range(RING)
        for r in range(SPATIAL // 2)
    ]
    along_z = [
        [side * (SPATIAL // 2) + z * CORES + c for z in range(SPATIAL // 2 // CORES)]
        for side in range(2)
        for c in range(CORES)
    ]

    to_heads = functools.partial(
        lax.all_to_all, axis_name="spatial", split_axis=0, concat_axis=0, tiled=True
    )

    selector = (levels[:, None] == jnp.arange(gate_table.shape[0], dtype=jnp.int32)[None, :]).astype(
        jnp.float32
    )
    gates = jnp.dot(
        selector, gate_table, precision=lax.Precision.HIGHEST, preferred_element_type=jnp.float32
    )
    other_gates = lax.ppermute(gates, "queue", swap_low)
    gates = jnp.where(y_low == 0, jnp.stack((gates, other_gates)), jnp.stack((other_gates, gates)))
    count = RING * frames
    is_last = (jnp.arange(count, dtype=jnp.int32) == count - 1)[None, :, None] & (y_low == 1)
    gates = jnp.where(
        is_last,
        gates[:, count - 1 : count],
        lax.dynamic_slice_in_dim(gates, y_low * count, count, axis=1),
    )

    kv0, kv1, query, last_frame = pack(queries, keys, values, hidden)
    kv0 = to_heads(kv0)
    kv1_heads = to_heads(hold(kv1, kv0, gates))
    query = to_heads(hold(query, kv1_heads))
    kv0 = hold(kv0, query)
    kv0_before, kv0_after = lax.ppermute(kv0, "queue", up), lax.ppermute(kv0, "queue", down)
    kv1 = hold(kv1_heads, query)
    kv1_before, kv1_after = lax.ppermute(kv1, "queue", up), lax.ppermute(kv1, "queue", down)

    weight = lax.all_gather(out_weight, ("queue", "spatial"), axis_index_groups=along_y, axis=0)
    weight = hold(weight, query, room=56)
    weight = lax.all_gather(weight, "spatial", axis_index_groups=along_z, axis=0)
    weight = weight.reshape(-1, 2, 2, *out_weight.shape)

    cross = [(RING - 1, QUEUE - 1)]

    def with_crossing(even, odd, crossing):
        odd = jnp.where(position == QUEUE - 1, crossing, odd)
        return jnp.concatenate((even, odd), axis=1)

    def spread(mine):
        left = lax.ppermute(mine, "queue", ring_up)
        right = lax.ppermute(mine, "queue", ring_down)
        far_low = lax.ppermute(left[: SPATIAL // 2], "queue", ring_up)
        far_high = lax.ppermute(right[SPATIAL // 2 :], "queue", ring_down)
        return mine, left, right, far_low, far_high

    head0 = (position_now, query, 0, kv0, kv0_before, kv0_after)
    head1 = (position_now, query, 1, kv1, kv1_before, kv1_after)
    odd0, token = attend(1, *head0)
    odd0_crossing = lax.ppermute(odd0, "queue", cross)
    even0, token = attend(0, *head0, token)
    first = with_crossing(even0, odd0, odd0_crossing)
    odd1, token = attend(1, *head1, token, first)
    odd1_crossing = lax.ppermute(odd1, "queue", cross)
    first = hold(to_heads(first), token)
    first_sources = spread(first)
    shifted = lax.ppermute(hold(last_frame, kv1_before, token), "queue", up)
    even1, token = attend(0, *head1, token, first)
    weight_own = hold(weight, token, room=56)
    weight_pair = lax.ppermute(weight_own, "spatial", swap_core)
    second = hold(with_crossing(even1, odd1, odd1_crossing), shifted)
    second_sources = spread(to_heads(second))

    partial = project(0, place, first_sources, weight_own, weight_pair, None, None)
    branch = project(1, place, second_sources, weight_own, weight_pair, partial, gates)
    branch = lax.all_to_all(
        branch, "queue", split_axis=0, concat_axis=0, axis_index_groups=ring, tiled=True
    )
    branch = branch.reshape(RING, frames, *branch.shape[1:])
    return add_branch(position_now, branch, hidden, shifted, entering)


def solution(mesh):
    return jax.shard_map(
        body,
        mesh=mesh,
        in_specs=(
            P("queue", "spatial", None),
            P("queue", "spatial", None),
            P("queue", "spatial", None),
            P("queue", "spatial", None),
            P("spatial", "queue"),
            P(None, "queue"),
            P(),
            P("spatial", None),
        ),
        out_specs=P("queue", "spatial", None),
        check_vma=False,
    )
```

```python
import functools

import jax
import jax.numpy as jnp
from jax import lax
from jax.experimental import pallas as pl
from jax.experimental.pallas import tpu as pltpu
from jax.sharding import PartitionSpec as P

HEADS = 32
HD = 128
WMAX = 2
NEG_FILL = -1e30
SCALE_LOG2 = (HD ** -0.5) * 1.4426950408889634
BLOCK_Q = 512
VMEM = 28 * 1024 * 1024
LARGE = pltpu.CompilerParams(vmem_limit_bytes=58 * 1024 * 1024)
MEDIUM = pltpu.CompilerParams(vmem_limit_bytes=12 * 1024 * 1024)
QUEUE = 8
RING = 4
SPATIAL = 16
CORES = 2
PACK = 4
SPAN = 2 * WMAX + 1
ANY = pl.BlockSpec(memory_space=pl.ANY)
TOKEN = (8, 128)


def corner(array):
    rows = 8 if array.dtype == jnp.float32 else 16
    block = (1,) * (array.ndim - 2) + (rows, 128)
    return pl.BlockSpec(block, lambda *at: (0,) * array.ndim)


def pack(queries, keys, values, hidden):
    frames, tok, width = keys.shape
    group = width // SPATIAL
    piece = width // PACK
    count = SPATIAL // PACK

    def kernel(q_ref, k_ref, v_ref, hidden_ref, kv0_ref, kv1_ref, out_ref, last_ref):
        last_ref[...] = hidden_ref[...]
        for i in range(count):
            for head, kv_ref in enumerate((kv0_ref, kv1_ref)):
                cols = slice(i * group + head * HD, i * group + (head + 1) * HD)
                kv_ref[i, 0] = k_ref[:, :, cols]
                kv_ref[i, 1] = v_ref[:, :, cols]
            out_ref[i] = q_ref[:, :, i * group : (i + 1) * group]

    spec = pl.BlockSpec((frames, tok, piece), lambda s: (0, 0, s))
    part = hidden.shape[-1] // PACK
    kv_spec = pl.BlockSpec((count, 2, frames, tok, HD), lambda s: (s, 0, 0, 0, 0))
    kv_shape = jax.ShapeDtypeStruct((SPATIAL, 2, frames, tok, HD), keys.dtype)
    return pl.pallas_call(
        kernel,
        grid=(PACK,),
        in_specs=[spec] * 3 + [pl.BlockSpec((1, tok, part), lambda s: (frames - 1, 0, s))],
        out_specs=[
            kv_spec,
            kv_spec,
            pl.BlockSpec((count, frames, tok, group), lambda s: (s, 0, 0, 0)),
            pl.BlockSpec((1, tok, part), lambda s: (0, 0, s)),
        ],
        out_shape=[
            kv_shape,
            kv_shape,
            jax.ShapeDtypeStruct((SPATIAL, frames, tok, group), queries.dtype),
            jax.ShapeDtypeStruct((1, *hidden.shape[1:]), hidden.dtype),
        ],
        compiler_params=LARGE,
        name="pack",
    )(queries, keys, values, hidden)


def hold(array, *earlier, room=1):
    def kernel(*refs):
        pass

    return pl.pallas_call(
        kernel,
        grid=(1,),
        in_specs=[ANY] + [corner(e) for e in earlier],
        out_specs=ANY,
        out_shape=jax.ShapeDtypeStruct(array.shape, array.dtype),
        input_output_aliases={0: 0},
        compiler_params=pltpu.CompilerParams(vmem_limit_bytes=room * 1024 * 1024),
        name="hold",
    )(array, *earlier)


def attend(frame, position, query, head, own, before, after, *earlier):
    groups, frames, tok, both = query.shape
    width = own.shape[-1]
    row_count = groups * tok
    groups_block = BLOCK_Q // tok
    blocks = row_count // BLOCK_Q
    asked = range(frames) if frame is None else (frame,)
    before_from = min(asked)
    before_count = frames - before_from
    after_count = max(asked) + 1
    loaded = before_count + frames + after_count

    def kernel(pos_ref, q_ref, own_ref, before_ref, after_ref, *rest):
        out_ref, token_ref, kt_ref, vx_ref = rest[-4:]
        sources = (
            [(before_ref, f) for f in range(before_count)]
            + [(own_ref, f) for f in range(frames)]
            + [(after_ref, f) for f in range(after_count)]
        )
        turn_frame = pl.program_id(0)

        @pl.when((turn_frame == 0) & (pl.program_id(1) == 0))
        def _():
            for at, (ref, f) in enumerate(sources):
                rows = slice(at * row_count, (at + 1) * row_count)
                turned = ref[:, 0, f].reshape(row_count, width).T
                kt_ref[:width, rows] = turned
                kt_ref[width:, rows] = turned
                vx_ref[rows, :width] = ref[:, 1, f].reshape(row_count, width)
                vx_ref[rows, width:] = jnp.ones((row_count, width), vx_ref.dtype)

        q = q_ref[:, 0].reshape(BLOCK_Q, width).astype(jnp.float32) * SCALE_LOG2
        high = q.astype(jnp.bfloat16)
        low = (q - high.astype(jnp.float32)).astype(jnp.bfloat16)
        q = jnp.concatenate((high, low), axis=1)
        position_now = pos_ref[0]

        def rows_of(step):
            start = (turn_frame + step) * row_count
            return pl.ds(pl.multiple_of(start, row_count), row_count)

        def scores(step):
            return jnp.dot(q, kt_ref[:, rows_of(step)], preferred_element_type=jnp.float32)

        top = jnp.full((BLOCK_Q, 1), NEG_FILL, jnp.float32)
        total = jnp.zeros((BLOCK_Q, 2 * width), jnp.float32)
        order = (2, 1, 3, 0, 4)
        ahead = scores(order[0])
        for turn, step in enumerate(order):
            s = ahead
            if turn + 1 < SPAN:
                ahead = scores(order[turn + 1])
            at = turn_frame + step
            absent = ((position_now == 0) & (at < before_count)) | (
                (position_now == QUEUE - 1) & (at >= before_count + frames)
            )
            peak = jnp.max(s, axis=1, keepdims=True)
            peak = jnp.where(absent, NEG_FILL, peak)
            lifted_top = jnp.maximum(top, peak)
            less = jnp.where(absent, -NEG_FILL, lifted_top)
            weights = jnp.exp2(s - less).astype(jnp.bfloat16)
            part = jnp.dot(weights, vx_ref[rows_of(step)], preferred_element_type=jnp.float32)
            total = total * jnp.exp2(top - lifted_top) + part
            top = lifted_top
        result = total[:, :width] / total[:, width:]
        out_ref[:, 0] = result.astype(out_ref.dtype).reshape(groups_block, tok, width)
        token_ref[...] = jnp.zeros_like(token_ref)

    first = asked[0]
    in_specs = [
        pl.BlockSpec((groups_block, 1, tok, width), lambda f, b, pos: (b, first + f, 0, head)),
        pl.BlockSpec(own.shape, lambda f, b, pos: (0, 0, 0, 0, 0)),
        pl.BlockSpec(
            (groups, 2, before_count, tok, width),
            lambda f, b, pos: (0, 0, before_from // before_count, 0, 0),
        ),
        pl.BlockSpec((groups, 2, after_count, tok, width), lambda f, b, pos: (0, 0, 0, 0, 0)),
    ]
    return pl.pallas_call(
        kernel,
        grid_spec=pltpu.PrefetchScalarGridSpec(
            num_scalar_prefetch=1,
            grid=(len(asked), blocks),
            in_specs=in_specs + [corner(e) for e in earlier],
            out_specs=[
                pl.BlockSpec((groups_block, 1, tok, width), lambda f, b, pos: (b, f, 0, 0)),
                pl.BlockSpec(TOKEN, lambda f, b, pos: (0, 0)),
            ],
            scratch_shapes=[
                pltpu.VMEM((2 * width, loaded * row_count), jnp.bfloat16),
                pltpu.VMEM((loaded * row_count, 2 * width), jnp.bfloat16),
            ],
        ),
        out_shape=[
            jax.ShapeDtypeStruct((groups, len(asked), tok, width), query.dtype),
            jax.ShapeDtypeStruct(TOKEN, jnp.float32),
        ],
        compiler_params=pltpu.CompilerParams(vmem_limit_bytes=VMEM),
        cost_estimate=pl.CostEstimate(
            flops=len(asked) * row_count * SPAN * row_count * width * 8,
            bytes_accessed=4 * 1024 * 1024,
            transcendentals=len(asked) * row_count * SPAN * row_count,
        ),
        name="attend",
    )(position, query, own, before, after, *earlier)


def project(head, place, sources, weight_own, weight_pair, partial, gates, *earlier):
    mine = sources[0]
    groups, frames, tok, width = mine.shape
    steps, sides, halves, rows_dev, cols_dev = weight_own.shape
    half = steps * sides
    rows = frames * tok
    last = partial is not None

    def kernel(place_ref, mine_ref, left_ref, right_ref, low_ref, high_ref, wo_ref, wp_ref, *rest):
        out_ref, a_ref = rest[-2:]
        x, core = place_ref[0], place_ref[1]

        @pl.when(pl.program_id(0) == 0)
        def _():
            for i in range(half):
                z, side = i // sides, i % sides
                for part in range(CORES):
                    group = side * half + CORES * z + (core if part == 0 else 1 - core)
                    cols = slice((part * half + i) * width, (part * half + i + 1) * width)
                    far = high_ref[group - half] if side else low_ref[group]
                    a_ref[0:rows, cols] = mine_ref[group].reshape(rows, width)
                    a_ref[rows : 2 * rows, cols] = right_ref[group].reshape(rows, width)
                    a_ref[2 * rows : 3 * rows, cols] = far.reshape(rows, width)
                    a_ref[3 * rows :, cols] = left_ref[group].reshape(rows, width)

        total = jnp.dot(
            a_ref[:, : half * width],
            wo_ref[:, :, 0].reshape(half * width, cols_dev),
            preferred_element_type=jnp.float32,
        )
        total += jnp.dot(
            a_ref[:, half * width :],
            wp_ref[:, :, 0].reshape(half * width, cols_dev),
            preferred_element_type=jnp.float32,
        )
        if not last:
            out_ref[0] = total
            return
        total += rest[0][0]
        gates_ref = rest[1]
        for source in range(RING):
            at = lax.rem(x + source, RING)
            for f in range(frames):
                gate = gates_ref[0, pl.ds(at * frames + f, 1), :]
                start = source * rows + f * tok
                slot = at * frames + 1 if f == 0 else lax.rem(at + 1, RING) * frames
                out_ref[slot, 0] = (gate * total[start : start + tok]).astype(out_ref.dtype)

    def whole(array):
        return pl.BlockSpec(array.shape, lambda n, place: (0,) * array.ndim)

    weight = pl.BlockSpec(
        (steps, sides, 1, width, cols_dev), lambda n, place: (0, 0, n, head, 0)
    )
    partial_spec = pl.BlockSpec((1, RING * rows, cols_dev), lambda n, place: (n, 0, 0))
    in_specs = [*map(whole, sources), weight, weight]
    operands = [*sources, weight_own, weight_pair]
    if last:
        in_specs += [partial_spec, pl.BlockSpec((1,) + gates.shape[1:], lambda n, place: (n, 0, 0))]
        operands += [partial, gates]
        out_spec = pl.BlockSpec((RING * frames, 1, tok, cols_dev), lambda n, place: (0, n, 0, 0))
        out_shape = jax.ShapeDtypeStruct((RING * frames, halves, tok, cols_dev), jnp.bfloat16)
    else:
        out_spec = partial_spec
        out_shape = jax.ShapeDtypeStruct((halves, RING * rows, cols_dev), jnp.float32)
    return pl.pallas_call(
        kernel,
        grid_spec=pltpu.PrefetchScalarGridSpec(
            num_scalar_prefetch=1,
            grid=(halves,),
            in_specs=in_specs + [corner(e) for e in earlier],
            out_specs=out_spec,
            scratch_shapes=[pltpu.VMEM((RING * rows, groups * width), jnp.bfloat16)],
        ),
        out_shape=out_shape,
        compiler_params=pltpu.CompilerParams(vmem_limit_bytes=48 * 1024 * 1024),
        cost_estimate=pl.CostEstimate(
            flops=2 * RING * rows * groups * width * halves * cols_dev,
            bytes_accessed=8 * 1024 * 1024,
            transcendentals=0,
        ),
        name="project_last" if last else "project_first",
    )(place, *operands, *earlier)


def add_branch(position, branch, hidden, shifted, entering):
    sources, frames, halves, tok, cols = branch.shape
    width = hidden.shape[-1]

    def kernel(pos_ref, b_ref, hidden_ref, shifted_ref, entering_ref, out_ref):
        def add(base_ref, replaced):
            for half in range(halves):
                for source in range(sources):
                    start = (half * sources + source) * cols
                    at = slice(start, start + cols)
                    value = base_ref[0, :, at].astype(jnp.float32)
                    value += b_ref[source, 0, half].astype(jnp.float32)
                    if replaced:
                        value = jnp.where(
                            pos_ref[0] == 0, entering_ref[:, at].astype(jnp.float32), value
                        )
                    out_ref[0, :, at] = value.astype(out_ref.dtype)

        @pl.when(pl.program_id(0) == 0)
        def _():
            add(shifted_ref, True)

        @pl.when(pl.program_id(0) == 1)
        def _():
            add(hidden_ref, False)

    frame_spec = pl.BlockSpec((1, tok, width), lambda i, pos: (0, 0, 0))
    return pl.pallas_call(
        kernel,
        grid_spec=pltpu.PrefetchScalarGridSpec(
            num_scalar_prefetch=1,
            grid=(frames,),
            in_specs=[
                pl.BlockSpec((sources, 1, halves, tok, cols), lambda i, pos: (0, i, 0, 0, 0)),
                frame_spec,
                frame_spec,
                pl.BlockSpec((tok, width), lambda i, pos: (0, 0)),
            ],
            out_specs=pl.BlockSpec((1, tok, width), lambda i, pos: (i, 0, 0)),
        ),
        out_shape=jax.ShapeDtypeStruct((frames, tok, width), hidden.dtype),
        compiler_params=MEDIUM,
        name="add_branch",
    )(position, branch, hidden, shifted, entering)


def body(hidden, queries, keys, values, out_weight, gate_table, levels, entering):
    frames = queries.shape[0]
    position = lax.axis_index("queue")
    spatial = lax.axis_index("spatial")
    y_low, x = position // RING, position % RING
    core = spatial % CORES
    position_now = position.astype(jnp.int32)[None]
    place = jnp.stack((x, core)).astype(jnp.int32)

    up = [(p, p + 1) for p in range(QUEUE - 1)]
    down = [(p + 1, p) for p in range(QUEUE - 1)]
    ring = [[r * RING + i for i in range(RING)] for r in range(QUEUE // RING)]
    ring_up = [(g[i], g[(i + 1) % RING]) for g in ring for i in range(RING)]
    ring_down = [(g[(i + 1) % RING], g[i]) for g in ring for i in range(RING)]
    swap_low = [(p, (p + RING) % QUEUE) for p in range(QUEUE)]
    swap_core = [(s, s ^ 1) for s in range(SPATIAL)]
    along_y = [
        [(low * RING + i) * SPATIAL + side * (SPATIAL // 2) + r for side in range(2) for low in range(2)]
        for i in range(RING)
        for r in range(SPATIAL // 2)
    ]
    along_z = [
        [side * (SPATIAL // 2) + z * CORES + c for z in range(SPATIAL // 2 // CORES)]
        for side in range(2)
        for c in range(CORES)
    ]

    to_heads = functools.partial(
        lax.all_to_all, axis_name="spatial", split_axis=0, concat_axis=0, tiled=True
    )

    selector = (levels[:, None] == jnp.arange(gate_table.shape[0], dtype=jnp.int32)[None, :]).astype(
        jnp.float32
    )
    gates = jnp.dot(
        selector, gate_table, precision=lax.Precision.HIGHEST, preferred_element_type=jnp.float32
    )
    other_gates = lax.ppermute(gates, "queue", swap_low)
    gates = jnp.where(y_low == 0, jnp.stack((gates, other_gates)), jnp.stack((other_gates, gates)))
    count = RING * frames
    is_last = (jnp.arange(count, dtype=jnp.int32) == count - 1)[None, :, None] & (y_low == 1)
    gates = jnp.where(
        is_last,
        gates[:, count - 1 : count],
        lax.dynamic_slice_in_dim(gates, y_low * count, count, axis=1),
    )

    kv0, kv1, query, last_frame = pack(queries, keys, values, hidden)
    kv0 = to_heads(kv0)
    kv1_heads = to_heads(hold(kv1, kv0, gates))
    query = to_heads(hold(query, kv1_heads))
    kv0 = hold(kv0, query)
    kv0_before, kv0_after = lax.ppermute(kv0, "queue", up), lax.ppermute(kv0, "queue", down)
    kv1 = hold(kv1_heads, query)
    kv1_before, kv1_after = lax.ppermute(kv1, "queue", up), lax.ppermute(kv1, "queue", down)

    weight = lax.all_gather(out_weight, ("queue", "spatial"), axis_index_groups=along_y, axis=0)
    weight = hold(weight, query, room=56)
    weight = lax.all_gather(weight, "spatial", axis_index_groups=along_z, axis=0)
    weight = weight.reshape(-1, 2, 2, *out_weight.shape)

    cross = [(RING - 1, QUEUE - 1)]

    def with_crossing(even, odd, crossing):
        odd = jnp.where(position == QUEUE - 1, crossing, odd)
        return jnp.concatenate((even, odd), axis=1)

    def spread(mine):
        left = lax.ppermute(mine, "queue", ring_up)
        right = lax.ppermute(mine, "queue", ring_down)
        far_low = lax.ppermute(left[: SPATIAL // 2], "queue", ring_up)
        far_high = lax.ppermute(right[SPATIAL // 2 :], "queue", ring_down)
        return mine, left, right, far_low, far_high

    head0 = (position_now, query, 0, kv0, kv0_before, kv0_after)
    head1 = (position_now, query, 1, kv1, kv1_before, kv1_after)
    odd0, token = attend(1, *head0)
    odd0_crossing = lax.ppermute(odd0, "queue", cross)
    even0, token = attend(0, *head0, token)
    first = with_crossing(even0, odd0, odd0_crossing)
    shifted = lax.ppermute(hold(last_frame, kv1_before, token), "queue", up)
    odd1, token = attend(1, *head1, token, first)
    odd1_crossing = lax.ppermute(odd1, "queue", cross)
    first = hold(to_heads(first), token)
    first_sources = spread(first)
    even1, token = attend(0, *head1, token, first, shifted)
    weight_own = hold(weight, token, room=56)
    weight_pair = lax.ppermute(weight_own, "spatial", swap_core)
    second = to_heads(with_crossing(even1, odd1, odd1_crossing))
    second_sources = spread(second)

    partial = project(0, place, first_sources, weight_own, weight_pair, None, None)
    branch = project(1, place, second_sources, weight_own, weight_pair, partial, gates)
    branch = lax.all_to_all(
        branch, "queue", split_axis=0, concat_axis=0, axis_index_groups=ring, tiled=True
    )
    branch = branch.reshape(RING, frames, *branch.shape[1:])
    return add_branch(position_now, branch, hidden, shifted, entering)


def solution(mesh):
    return jax.shard_map(
        body,
        mesh=mesh,
        in_specs=(
            P("queue", "spatial", None),
            P("queue", "spatial", None),
            P("queue", "spatial", None),
            P("queue", "spatial", None),
            P("spatial", "queue"),
            P(None, "queue"),
            P(),
            P("spatial", None),
        ),
        out_specs=P("queue", "spatial", None),
        check_vma=False,
    )
```
